32 devices in a mesh: groups: 2 (over y), row: 4 (over z), col: 2 (over x), sub: 2 (over core).
Axes of the slice: x: 2, y: 2, z: 4, core: 2. Of those that a mesh axis runs over, the one named last changes fastest.
Arguments:
- stream_in: bfloat16 [4096, 5376], P(('groups', 'row'), ('col', 'sub')), parts along dimension 0, may hold values from -6 to 6
- in_gain: float32 [5376], replicated, may hold values from 0.1 to 1.9
- query_weight: bfloat16 [5376, 4096], P('row', ('col', 'sub')), may hold values from -0.078125 to 0.078125
- key_matrix: bfloat16 [5376, 2048], P('row', ('col', 'sub')), may hold values from -0.078125 to 0.078125
- value_matrix: bfloat16 [5376, 2048], P('row', ('col', 'sub')), may hold values from -0.078125 to 0.078125
- query_gain: float32 [128], replicated, may hold values from 0.45 to 10, as said below
- key_norm_gain: float32 [128], replicated, may hold values from 0.45 to 10, as said below
- output_weight: bfloat16 [4096, 5376], P('row', ('col', 'sub')), may hold values from -3 to 3
- post_gain: float32 [5376], P(('col', 'sub')), may hold values from 0.1 to 1.9
Outputs:
- stream_out: bfloat16 [4096, 5376], P(('groups', 'row'), ('col', 'sub')), parts along dimension 0
The draws below stay inside these ranges and needn't reach their ends.
There are 2 independent parts, one for each index of `groups`. The reference program is written for one: setup_inputs(seed, part) draws one part's arguments, and reference() takes and returns one part's arrays. A program takes and returns all parts, laid end to end along the dimension named above; an argument that names none is the same for every part. Nothing has to cross between parts.
Inputs may be any that keep to these rules, and one draw needn't show every extreme that they name: `query_gain`: positive. `key_norm_gain`: positive.
All inputs are finite; a program needn't handle non-finite values.
Results may differ from the reference program's by a relative error of at most 0.014.
The reference program's roundings to bfloat16 on the way count: a program that leaves them out, or rounds other values in their place, can miss the bound.
Values may be sent and summed in bfloat16 or wider, within the bound.
No kernel may reach another device: no remote copies, remote signals or barrier semaphores. Data moves between devices by JAX's collectives and lax.ppermute only.
A program may use at most 128 MiB of HBM per device.

```python
import jax
import jax.numpy as jnp
from jax import lax

MODEL_WIDTH = 5376
QUERY_HEAD_COUNT = 32
KEY_VALUE_HEADS = 16
HEAD_DIM = 128
WINDOW_LENGTH = 1024
TOKENS_PER_ROW = 512
S = 2048
N_ROW = 4


def head_gain(key):
    return jnp.exp(jax.random.uniform(key, (HEAD_DIM,), jnp.float32, -0.69, 0.69))


def draw_query_gain(key, part):
    return head_gain(jax.random.fold_in(key, 101))


def draw_key_norm_gain(key, part):
    return head_gain(jax.random.fold_in(key, 202))


def draw_output_weight(key, part):
    fan_rows = QUERY_HEAD_COUNT * HEAD_DIM
    base_values = jnp.clip(jax.random.normal(jax.random.fold_in(key, 1), (fan_rows, MODEL_WIDTH), jnp.float32), -6.0, 6.0)
    column = jnp.arange(MODEL_WIDTH, dtype=jnp.float32) / MODEL_WIDTH
    row_jitter = jnp.exp(jax.random.uniform(jax.random.fold_in(key, 2), (fan_rows, 1), jnp.float32, -0.5, 0.5))
    column_scale = jnp.exp(2.3 * column + jax.random.uniform(jax.random.fold_in(key, 3), (MODEL_WIDTH,), jnp.float32, -0.5, 0.5))
    return (base_values * row_jitter * column_scale[None, :] / 64.0).astype(jnp.bfloat16)


def level_of(own_key, shape, cuts, low, top_value):
    level = 1.0
    for position, parts in cuts:
        draws = jax.random.uniform(jax.random.fold_in(jax.random.fold_in(own_key, 6), position), (parts,), jnp.float32, low / len(cuts), top_value / len(cuts))
        level = level * jnp.repeat(jnp.exp(draws), shape[position] // parts).reshape((-1,) + (1,) * (len(shape) - 1 - position))
    return level


def centred(stream_key, shape, deviation, limit, pieces=(), kind=jnp.bfloat16):
    values = deviation * jax.random.normal(stream_key, shape, jnp.float32)
    if pieces:
        values = values * level_of(stream_key, shape, pieces, -0.22, 0.18)
    return jnp.clip(values, -limit, limit).astype(kind)


def setup_inputs(seed: int = 0, part: int = 0) -> dict:
    keys = jax.random.split(jax.random.key(seed), 10)
    own_keys = jax.random.split(jax.random.fold_in(keys[9], part), 10)
    stream_in = centred(own_keys[0], (S, MODEL_WIDTH), 1.0, 6.0, ((0, 4), (1, 4)))
    in_gain = jnp.clip(1.0 + 0.18 * jax.random.normal(keys[1], (MODEL_WIDTH,), jnp.float32), 0.1, 1.9)
    query_weight = centred(keys[2], (MODEL_WIDTH, QUERY_HEAD_COUNT * HEAD_DIM), MODEL_WIDTH ** -0.5, 0.078125, ((0, 4), (1, 4)))
    key_matrix = centred(keys[3], (MODEL_WIDTH, KEY_VALUE_HEADS * HEAD_DIM), MODEL_WIDTH ** -0.5, 0.078125, ((0, 4), (1, 4)))
    value_matrix = centred(keys[4], (MODEL_WIDTH, KEY_VALUE_HEADS * HEAD_DIM), MODEL_WIDTH ** -0.5, 0.078125, ((0, 4), (1, 4)))
    query_gain = draw_query_gain(jax.random.fold_in(keys[9], 71), part)
    key_norm_gain = draw_key_norm_gain(jax.random.fold_in(keys[9], 71), part)
    output_weight = draw_output_weight(jax.random.fold_in(keys[9], 71), part)
    post_gain = jnp.clip(1.0 + 0.18 * jax.random.normal(keys[8], (MODEL_WIDTH,), jnp.float32), 0.1, 1.9)
    return dict(stream_in=stream_in, in_gain=in_gain, query_weight=query_weight, key_matrix=key_matrix, value_matrix=value_matrix, query_gain=query_gain, key_norm_gain=key_norm_gain, output_weight=output_weight, post_gain=post_gain)


EPSILON = 1e-06

def root_mean_scale(values, gain):
    return values * lax.rsqrt(lax.optimization_barrier(jnp.mean(values * values, axis=-1, keepdims=True)) + EPSILON) * gain

def apply_rotary(tensor, token_positions):
    half_dim = tensor.shape[-1] // 2
    inverse = 10000.0 ** (-(jnp.arange(half_dim, dtype=jnp.float32) * 2.0) / tensor.shape[-1])
    angles = token_positions[:, None] * inverse[None, :]
    cosine = jnp.cos(angles)[:, None, :]
    sine_part = jnp.sin(angles)[:, None, :]
    first_half = tensor[..., :half_dim]
    second_half = tensor[..., half_dim:]
    return jnp.concatenate([first_half * cosine - second_half * sine_part, second_half * cosine + first_half * sine_part], axis=-1)

def reference(stream_in, in_gain, query_weight, key_matrix, value_matrix, query_gain, key_norm_gain, output_weight, post_gain):
    sequence_length = TOKENS_PER_ROW * N_ROW
    group_count = QUERY_HEAD_COUNT // KEY_VALUE_HEADS
    scale_factor = float(MODEL_WIDTH // QUERY_HEAD_COUNT) ** (-0.5)
    residual = stream_in.astype(jnp.float32)
    normed = root_mean_scale(residual, in_gain).astype(jnp.bfloat16)
    query_proj = jnp.dot(normed, query_weight, preferred_element_type=jnp.float32)
    projected_keys = jnp.dot(normed, key_matrix, preferred_element_type=jnp.float32)
    projected_values = jnp.dot(normed, value_matrix, preferred_element_type=jnp.float32).astype(jnp.bfloat16)
    token_positions = jnp.arange(sequence_length, dtype=jnp.int32).astype(jnp.float32)
    query_rot = apply_rotary(root_mean_scale(query_proj.reshape(sequence_length, QUERY_HEAD_COUNT, HEAD_DIM), query_gain), token_positions).astype(jnp.bfloat16)
    rotary_keys = apply_rotary(root_mean_scale(projected_keys.reshape(sequence_length, KEY_VALUE_HEADS, HEAD_DIM), key_norm_gain), token_positions).astype(jnp.bfloat16)
    value_head_rows = projected_values.reshape(sequence_length, KEY_VALUE_HEADS, HEAD_DIM)
    key_rows_padded = jnp.concatenate([jnp.zeros((WINDOW_LENGTH, KEY_VALUE_HEADS, HEAD_DIM), jnp.bfloat16), rotary_keys], axis=0)
    value_rows_padded = jnp.concatenate([jnp.zeros((WINDOW_LENGTH, KEY_VALUE_HEADS, HEAD_DIM), jnp.bfloat16), value_head_rows], axis=0)
    band_extent = WINDOW_LENGTH + TOKENS_PER_ROW

    def one_block(block_index):
        leading_row = (block_index * TOKENS_PER_ROW).astype(jnp.int32)
        starting_index = jnp.zeros((), jnp.int32)
        query_block_tile = lax.dynamic_slice(query_rot, (leading_row, starting_index, starting_index), (TOKENS_PER_ROW, QUERY_HEAD_COUNT, HEAD_DIM))
        query_block_tile = query_block_tile.reshape(TOKENS_PER_ROW, KEY_VALUE_HEADS, group_count, HEAD_DIM).astype(jnp.float32)
        key_block_tile = lax.dynamic_slice(key_rows_padded, (leading_row, starting_index, starting_index), (band_extent, KEY_VALUE_HEADS, HEAD_DIM)).astype(jnp.float32)
        value_block_tile = lax.dynamic_slice(value_rows_padded, (leading_row, starting_index, starting_index), (band_extent, KEY_VALUE_HEADS, HEAD_DIM)).astype(jnp.float32)
        scores = jnp.einsum('qhgd,shd->hgqs', query_block_tile, key_block_tile) * scale_factor
        query_places = leading_row + jnp.arange(TOKENS_PER_ROW, dtype=jnp.int32)
        key_places = leading_row - WINDOW_LENGTH + jnp.arange(band_extent, dtype=jnp.int32)
        distance = query_places[:, None] - key_places[None, :]
        visible = (distance >= 0) & (distance < WINDOW_LENGTH) & (key_places[None, :] >= 0)
        scores = jnp.where(visible, scores, -1e+30)
        row_max = lax.optimization_barrier(jnp.max(scores, axis=-1, keepdims=True))
        exponent = jnp.exp(scores - row_max)
        weights = (exponent / lax.optimization_barrier(jnp.sum(exponent, axis=-1, keepdims=True))).astype(jnp.bfloat16)
        attended = jnp.einsum('hgqs,shd->qhgd', weights.astype(jnp.float32), value_block_tile)
        return attended.reshape(TOKENS_PER_ROW, QUERY_HEAD_COUNT * HEAD_DIM).astype(jnp.bfloat16)
    attended = lax.map(one_block, jnp.arange(N_ROW, dtype=jnp.int32)).reshape(sequence_length, QUERY_HEAD_COUNT * HEAD_DIM)
    branch = jnp.dot(attended, output_weight, preferred_element_type=jnp.float32)
    return (residual + root_mean_scale(branch, post_gain)).astype(jnp.bfloat16)
```

```python
import functools

import jax
import jax.numpy as jnp
from jax import lax
from jax.experimental import pallas as pl
from jax.experimental.pallas import tpu as pltpu
from jax.sharding import PartitionSpec as P

MODEL_WIDTH = 5376
QUERY_HEAD_COUNT = 32
WINDOW_LENGTH = 1024


EPSILON = 1e-06
MIDDLE = (1, 2)
ENDS = (0, 3)
VMEM_BYTES = 60 * 1024 * 1024


def shifted(x, axis, by):
    count = lax.axis_size(axis)
    pairs = [(i, i + by) for i in range(count) if 0 <= i + by < count]
    return lax.ppermute(x, axis, pairs)


def root_mean_scale(values, gain):
    return values * lax.rsqrt(jnp.mean(values * values, axis=-1, keepdims=True) + EPSILON) * gain


def rotary_tables(token_positions, size):
    half_dim = size // 2
    inverse = 10000.0 ** (-(jnp.arange(half_dim, dtype=jnp.float32) * 2.0) / size)
    angles = token_positions[:, None] * inverse[None, :]
    return jnp.cos(angles), jnp.sin(angles)


def apply_rotary(tensor, token_positions):
    half_dim = tensor.shape[-1] // 2
    cosine, sine_part = rotary_tables(token_positions, tensor.shape[-1])
    cosine, sine_part = cosine[:, None, :], sine_part[:, None, :]
    first_half = tensor[..., :half_dim]
    second_half = tensor[..., half_dim:]
    return jnp.concatenate(
        [
            first_half * cosine - second_half * sine_part,
            second_half * cosine + first_half * sine_part,
        ],
        axis=-1,
    )


def general_form(
    stream_in,
    in_gain,
    query_weight,
    key_matrix,
    value_matrix,
    query_gain,
    key_norm_gain,
    output_weight,
    post_gain,
):
    token_rows = lax.all_gather(stream_in, ("col", "sub"), axis=1, tiled=True)
    tokens = token_rows.shape[0]
    normed = root_mean_scale(token_rows.astype(jnp.float32), in_gain).astype(jnp.bfloat16)

    def add_panel(panel_piece):
        return jnp.dot(normed, panel_piece, preferred_element_type=jnp.float32)

    query_proj = add_panel(lax.all_gather(query_weight, "row", axis=0, tiled=True))
    projected_keys = add_panel(lax.all_gather(key_matrix, "row", axis=0, tiled=True))
    projected_values = add_panel(lax.all_gather(value_matrix, "row", axis=0, tiled=True))
    head_size = query_gain.shape[0]
    query_heads = query_weight.shape[1] // head_size
    pair_heads = key_matrix.shape[1] // head_size
    group_count = query_heads // pair_heads
    scale_factor = float(MODEL_WIDTH // QUERY_HEAD_COUNT) ** (-0.5)
    row_index = lax.axis_index("row")
    query_places = row_index * tokens + jnp.arange(tokens, dtype=jnp.int32)
    query_rot = apply_rotary(
        root_mean_scale(query_proj.reshape(tokens, query_heads, head_size), query_gain),
        query_places.astype(jnp.float32),
    ).astype(jnp.bfloat16)
    rotary_keys = apply_rotary(
        root_mean_scale(projected_keys.reshape(tokens, pair_heads, head_size), key_norm_gain),
        query_places.astype(jnp.float32),
    ).astype(jnp.bfloat16)
    keys_flat = rotary_keys.reshape(tokens, pair_heads * head_size)
    values_flat = projected_values.astype(jnp.bfloat16)
    shards_back = min(WINDOW_LENGTH // tokens, lax.axis_size("row") - 1)
    band_length = (shards_back + 1) * tokens
    key_parts = [keys_flat]
    value_parts = [values_flat]
    for offset in range(1, shards_back + 1):
        keys_prior, values_prior = shifted((keys_flat, values_flat), "row", offset)
        key_parts = [keys_prior] + key_parts
        value_parts = [values_prior] + value_parts
    keys_band = jnp.concatenate(key_parts, axis=0)
    values_band = jnp.concatenate(value_parts, axis=0)
    key_places = (row_index - shards_back) * tokens + jnp.arange(band_length, dtype=jnp.int32)
    distance = query_places[:, None] - key_places[None, :]
    visible = (distance >= 0) & (distance < WINDOW_LENGTH) & (key_places[None, :] >= 0)
    grouped = query_rot.reshape(tokens, pair_heads, group_count, head_size)
    scores = (
        jnp.einsum(
            "qhgd,shd->hgqs",
            grouped,
            keys_band.reshape(band_length, pair_heads, head_size),
            preferred_element_type=jnp.float32,
        )
        * scale_factor
    )
    scores = jnp.where(visible, scores, -1e30)
    row_max = jnp.max(scores, axis=-1, keepdims=True)
    exponent = jnp.exp(scores - row_max)
    weights = (exponent / jnp.sum(exponent, axis=-1, keepdims=True)).astype(jnp.bfloat16)
    attended = jnp.einsum(
        "hgqs,shd->qhgd",
        weights,
        values_band.reshape(band_length, pair_heads, head_size),
        preferred_element_type=jnp.float32,
    )
    heads_out = attended.reshape(tokens, query_heads * head_size).astype(jnp.bfloat16)
    head_rows = lax.all_gather(heads_out, ("col", "sub"), axis=1, tiled=True)
    branch = jnp.dot(
        head_rows,
        lax.all_gather(output_weight, "row", axis=0, tiled=True),
        preferred_element_type=jnp.float32,
    )
    squares = lax.psum(jnp.sum(branch * branch, axis=-1), ("col", "sub"))
    scaled = branch * lax.rsqrt(squares[:, None] / MODEL_WIDTH + EPSILON) * post_gain
    return (stream_in.astype(jnp.float32) + scaled).astype(jnp.bfloat16)


def swapped(x, axis, rows):
    if axis == "groups":
        count = lax.axis_size("row")
        pairs = [(count * i + r, count * (1 - i) + r) for r in rows for i in range(2)]
        return lax.ppermute(x, ("groups", "row"), pairs)
    pairs = [(2 * r + i, 2 * r + 1 - i) for r in rows for i in range(2)]
    return lax.ppermute(x, ("row", axis), pairs)


def project_kernel(
    x0, x1, x2, x3, gain, weight, q_gain, k_gain, cosine, sine, q_out, k_out, v_out, total, scale
):
    pieces = (x0, x1, x2, x3)
    step = pl.program_id(0)
    head = q_gain.shape[-1]

    @pl.when(step == 0)
    def _():
        squares = sum(
            jnp.sum(jnp.square(p[...].astype(jnp.float32)), axis=-1, keepdims=True) for p in pieces
        )
        scale[...] = lax.rsqrt(squares / MODEL_WIDTH + EPSILON)

    for index, piece in enumerate(pieces):

        @pl.when(step == index)
        def _(index=index, piece=piece):
            normed = (piece[...].astype(jnp.float32) * scale[...] * gain[index : index + 1, :]).astype(
                jnp.bfloat16
            )
            half = weight.shape[-1]
            for part in range(2):
                product = jnp.dot(normed, weight[0, part], preferred_element_type=jnp.float32)
                columns = slice(part * half, (part + 1) * half)
                if index == 0:
                    total[:, columns] = product
                else:
                    total[:, columns] += product

    @pl.when(step == len(pieces) - 1)
    def _():
        cos, sin = cosine[...], sine[...]

        def rotated(columns, head_gain):
            values = total[:, columns]
            values = (
                values
                * lax.rsqrt(jnp.mean(values * values, axis=-1, keepdims=True) + EPSILON)
                * head_gain[...]
            )
            return (values * cos + pltpu.roll(values, head // 2, 1) * sin).astype(jnp.bfloat16)

        q_width, k_width = q_out.shape[-1], k_out.shape[-1]
        for start in range(0, q_width, head):
            q_out[:, start : start + head] = rotated(slice(start, start + head), q_gain)
        for start in range(0, k_width, head):
            k_out[:, start : start + head] = rotated(
                slice(q_width + start, q_width + start + head), k_gain
            )
        v_out[...] = total[:, q_width + k_width :].astype(jnp.bfloat16)


def project(pieces, gain, weight, q_gain, k_gain, cosine, sine):
    tokens, depth = pieces[0].shape
    width = weight.shape[-1]
    head = q_gain.shape[-1]
    whole = lambda shape: pl.BlockSpec(shape, lambda k: (0,) * len(shape))
    return pl.pallas_call(
        project_kernel,
        grid=(4,),
        in_specs=[whole((tokens, depth))] * 4
        + [
            whole((4, depth)),
            pl.BlockSpec((1, 2, depth, width), lambda k: (k, 0, 0, 0)),
            whole((1, head)),
            whole((1, head)),
            whole((tokens, head)),
            whole((tokens, head)),
        ],
        out_specs=[
            whole((tokens, width)),
            whole((tokens, width // 2)),
            whole((tokens, width // 2)),
        ],
        out_shape=[
            jax.ShapeDtypeStruct((tokens, width), jnp.bfloat16),
            jax.ShapeDtypeStruct((tokens, width // 2), jnp.bfloat16),
            jax.ShapeDtypeStruct((tokens, width // 2), jnp.bfloat16),
        ],
        scratch_shapes=[
            pltpu.VMEM((tokens, 2 * width), jnp.float32),
            pltpu.VMEM((tokens, 1), jnp.float32),
        ],
        compiler_params=pltpu.CompilerParams(vmem_limit_bytes=VMEM_BYTES),
        cost_estimate=pl.CostEstimate(
            flops=2 * tokens * 4 * depth * 2 * width,
            bytes_accessed=2 * (4 * tokens * depth + 8 * depth * width + 2 * tokens * width),
            transcendentals=0,
        ),
    )(*pieces, gain, weight, q_gain, k_gain, cosine, sine)


def attend_kernel(band, scale, table, q_ref, k0, k1, k2, k3, v0, v1, v2, v3, out, keys, values):
    tokens, tile = k0.shape[0], q_ref.shape[0]
    head = 128
    step = pl.program_id(0)

    @pl.when(step == 0)
    def _():
        for index, (k, v) in enumerate(((k0, v0), (k1, v1), (k2, v2), (k3, v3))):
            rows = pl.ds(pl.multiple_of(table[index + 1] * tokens, tokens), tokens)
            keys[rows, :] = k[...]
            values[rows, :] = v[...]

    first = table[0] * tokens + step * tile
    start = pl.multiple_of(
        jnp.clip(first + tile - band, 0, keys.shape[0] - band), tile
    )
    rows = pl.ds(start, band)
    distance = (
        (first - start)
        + lax.broadcasted_iota(jnp.int32, (tile, band), 0)
        - lax.broadcasted_iota(jnp.int32, (tile, band), 1)
    )
    visible = (distance >= 0) & (distance < WINDOW_LENGTH)
    group = (q_ref.shape[1] // head) // (keys.shape[1] // head)
    for index in range(q_ref.shape[1] // head):
        q = q_ref[:, index * head : (index + 1) * head]
        kv_columns = slice((index // group) * head, (index // group + 1) * head)
        scores = lax.dot_general(
            q, keys[rows, kv_columns], (((1,), (1,)), ((), ())), preferred_element_type=jnp.float32
        )
        scores = jnp.where(visible, scores * scale, -1e30)
        exponent = jnp.exp(scores - jnp.max(scores, axis=-1, keepdims=True))
        weights = exponent * (1.0 / jnp.sum(exponent, axis=-1, keepdims=True))
        out[:, index * head : (index + 1) * head] = jnp.dot(
            weights.astype(jnp.bfloat16), values[rows, kv_columns], preferred_element_type=jnp.float32
        ).astype(jnp.bfloat16)


def attend(table, q, ks, vs):
    tokens, q_width = q.shape
    kv_width = ks[0].shape[1]
    tile = tokens // 2
    band = min(WINDOW_LENGTH + tile, 4 * tokens)
    whole = lambda shape: pl.BlockSpec(shape, lambda t, *_: (0,) * len(shape))
    return pl.pallas_call(
        functools.partial(attend_kernel, band, float(MODEL_WIDTH // QUERY_HEAD_COUNT) ** (-0.5)),
        grid_spec=pltpu.PrefetchScalarGridSpec(
            num_scalar_prefetch=1,
            grid=(2,),
            in_specs=[pl.BlockSpec((tile, q_width), lambda t, *_: (t, 0))]
            + [whole((tokens, kv_width))] * 8,
            out_specs=pl.BlockSpec((tile, q_width), lambda t, *_: (t, 0)),
            scratch_shapes=[
                pltpu.VMEM((4 * tokens, kv_width), jnp.bfloat16),
                pltpu.VMEM((4 * tokens, kv_width), jnp.bfloat16),
            ],
        ),
        out_shape=jax.ShapeDtypeStruct((tokens, q_width), jnp.bfloat16),
        compiler_params=pltpu.CompilerParams(vmem_limit_bytes=VMEM_BYTES),
        cost_estimate=pl.CostEstimate(
            flops=4 * tokens * band * q_width,
            bytes_accessed=2 * (2 * tokens * q_width + 8 * tokens * kv_width),
            transcendentals=tokens * band * (q_width // 128),
        ),
    )(table, q, *ks, *vs)


def output_kernel(*refs):
    *parts, weight, out = refs
    step = pl.program_id(0)
    for index, part in enumerate(parts):

        @pl.when(step == index)
        def _(index=index, part=part):
            product = jnp.dot(part[...], weight[0], preferred_element_type=jnp.float32)
            if index == 0:
                out[...] = product
            else:
                out[...] += product


def output_product(parts, weight):
    tokens, depth = parts[0].shape
    width = weight.shape[-1]
    whole = lambda shape: pl.BlockSpec(shape, lambda k: (0,) * len(shape))
    return pl.pallas_call(
        output_kernel,
        grid=(len(parts),),
        in_specs=[whole((tokens, depth))] * len(parts)
        + [pl.BlockSpec((1, depth, width), lambda k: (k, 0, 0))],
        out_specs=whole((tokens, width)),
        out_shape=jax.ShapeDtypeStruct((tokens, width), jnp.float32),
        compiler_params=pltpu.CompilerParams(vmem_limit_bytes=VMEM_BYTES),
        cost_estimate=pl.CostEstimate(
            flops=2 * tokens * depth * len(parts) * width,
            bytes_accessed=2 * len(parts) * (tokens + width) * depth + 4 * tokens * width,
            transcendentals=0,
        ),
    )(*parts, weight)


def middle_form(
    stream_in,
    in_gain,
    query_weight,
    key_matrix,
    value_matrix,
    query_gain,
    key_norm_gain,
    output_weight,
    post_gain,
):
    tokens, features = stream_in.shape
    head = query_gain.shape[0]
    row = lax.axis_index("row")
    group = lax.axis_index("groups")
    place = lax.axis_index("col") * 2 + lax.axis_index("sub")
    upper = (row >= 2).astype(jnp.int32)
    in_middle = (row == 1) | (row == 2)
    own_block, near_block, cross_block, far_block = row, 3 * upper, 3 - row, 3 - 3 * upper
    slot = lambda block: jnp.bitwise_xor(place, block)

    half = query_weight.shape[1] // 2
    quarter = key_matrix.shape[1] // 2

    def side(which):
        queries = lax.dynamic_slice_in_dim(query_weight, which * half, half, axis=1)
        keys = lax.dynamic_slice_in_dim(key_matrix, which * quarter, quarter, axis=1)
        values = lax.dynamic_slice_in_dim(value_matrix, which * quarter, quarter, axis=1)
        return queries, jnp.concatenate([keys, values], axis=1)

    own_queries, own_pairs = side(upper)
    other_queries, other_pairs = side(1 - upper)
    own_side = jnp.where(group == 0, own_queries, own_pairs)
    other_side = jnp.where(group == 0, other_queries, other_pairs)

    x_near = lax.ppermute(stream_in, "row", [(0, 1), (3, 2)])
    x_cross = lax.ppermute(stream_in, "row", [(1, 2), (2, 1)])
    w_near = lax.ppermute(own_side, "row", [(0, 1), (3, 2)])
    w_cross = lax.ppermute(other_side, "row", [(1, 2), (2, 1)])
    w_far = lax.ppermute(other_side, "row", [(0, 2), (3, 1)])
    x_far = lax.ppermute(x_near, "row", [(1, 2), (2, 1)])

    weight = jnp.zeros((4, 2) + own_side.shape, jnp.bfloat16)

    def put(buffer, piece, *index):
        return lax.dynamic_update_slice(buffer, piece[None, None], (*index, 0, 0))

    weight = put(weight, own_queries, slot(own_block), 0)
    weight = put(weight, own_pairs, slot(own_block), 1)
    for piece, block in ((w_near, near_block), (w_cross, cross_block), (w_far, far_block)):
        weight = put(weight, piece, slot(block), group)
        weight = put(weight, swapped(piece, "groups", MIDDLE), slot(block), 1 - group)

    depth = output_weight.shape[0] // 2
    mine = lax.dynamic_slice_in_dim(output_weight, group * depth, depth, axis=0)
    o_pair = lax.ppermute(mine, "row", [(0, 1), (1, 0), (2, 3), (3, 2)])
    o_cross = lax.ppermute(mine, "row", [(1, 2), (2, 1)])
    o_far = lax.ppermute(o_pair, "row", [(1, 2), (2, 1)])
    o_end_cross = lax.ppermute(o_cross, "row", [(1, 0), (2, 3)])
    o_end_far = lax.ppermute(o_far, "row", [(1, 0), (2, 3)])
    out_weight = jnp.zeros((5, 2) + mine.shape, jnp.bfloat16)
    for part in range(2):
        out_weight = put(
            out_weight,
            output_weight[part * depth : (part + 1) * depth],
            slot(row),
            jnp.bitwise_xor(part, upper),
        )
    opposite = 3 - row
    pair_block = jnp.bitwise_xor(row, 1)
    cross_held = jnp.where(in_middle, slot(3 - row), 4)
    far_held = jnp.where(in_middle, slot(3 - pair_block), 4)
    end_cross_held = jnp.where(in_middle, 4, slot(3 - pair_block))
    end_far_held = jnp.where(in_middle, 4, slot(3 - row))
    for piece, where, rows in (
        (o_pair, slot(pair_block), MIDDLE + ENDS),
        (o_cross, cross_held, MIDDLE),
        (o_far, far_held, MIDDLE),
        (o_end_cross, end_cross_held, ENDS),
        (o_end_far, end_far_held, ENDS),
    ):
        out_weight = put(out_weight, piece, where, jnp.bitwise_xor(group, upper))
        out_weight = put(
            out_weight, swapped(piece, "groups", rows), where, jnp.bitwise_xor(1 - group, upper)
        )

    positions = jnp.arange(4 * tokens, dtype=jnp.int32).astype(jnp.float32)
    cosine, sine = rotary_tables(positions, head)
    cosine = jnp.concatenate([cosine, cosine], axis=1)
    sine = jnp.concatenate([-sine, sine], axis=1)
    gain_rows = in_gain.reshape(4, features)
    gain = jnp.concatenate(
        [lax.dynamic_slice_in_dim(gain_rows, slot(j), 1, axis=0) for j in range(4)], axis=0
    )

    def projected(piece, block):
        across = swapped(piece, "col", MIDDLE)
        pieces = (piece, swapped(piece, "sub", MIDDLE), across, swapped(across, "sub", MIDDLE))
        return project(
            pieces,
            gain,
            weight,
            query_gain[None],
            key_norm_gain[None],
            lax.dynamic_slice_in_dim(cosine, block * tokens, tokens, axis=0),
            lax.dynamic_slice_in_dim(sine, block * tokens, tokens, axis=0),
        )

    blocks = (own_block, near_block, cross_block, far_block)
    triples = [projected(p, b) for p, b in zip((stream_in, x_near, x_cross, x_far), blocks)]
    ks = [t[1] for t in triples]
    vs = [t[2] for t in triples]

    def attended(index):
        table = jnp.stack([blocks[index], *blocks]).astype(jnp.int32)
        return attend(table, triples[index][0], ks, vs)

    to_far = lax.ppermute(attended(3), "row", [(1, 3), (2, 0)])
    to_near = lax.ppermute(attended(1), "row", [(1, 0), (2, 3)])
    to_cross = lax.ppermute(attended(2), "row", [(1, 2), (2, 1)])
    this_side = jnp.where(in_middle, attended(0), to_near)
    that_side = jnp.where(in_middle, to_cross, to_far)
    everywhere = MIDDLE + ENDS
    this_across = swapped(this_side, "col", everywhere)
    that_across = swapped(that_side, "col", everywhere)
    parts = (
        this_side,
        that_side,
        swapped(this_side, "sub", everywhere),
        swapped(that_side, "sub", everywhere),
        this_across,
        that_across,
        swapped(this_across, "sub", everywhere),
        swapped(that_across, "sub", everywhere),
    )
    branch = output_product(parts, out_weight.reshape((10,) + mine.shape))

    squares = jnp.sum(branch * branch, axis=-1)
    squares = squares + swapped(squares, "sub", everywhere)
    squares = squares + swapped(squares, "col", everywhere)
    scaled = branch * lax.rsqrt(squares[:, None] / MODEL_WIDTH + EPSILON) * post_gain
    return (stream_in.astype(jnp.float32) + scaled).astype(jnp.bfloat16)


def on_device(*args):
    stream_in, _, query_weight, key_matrix, value_matrix, query_gain, *_ = args
    sizes = tuple(lax.axis_size(name) for name in ("groups", "row", "col", "sub"))
    tokens, head = stream_in.shape[0], query_gain.shape[0]
    fits = (
        sizes == (2, 4, 2, 2)
        and head == 128
        and tokens % 256 == 0
        and key_matrix.shape[1] % (2 * head) == 0
        and query_weight.shape[1] == 2 * key_matrix.shape[1]
        and value_matrix.shape[1] == key_matrix.shape[1]
    )
    return middle_form(*args) if fits else general_form(*args)


def solution(mesh):
    placed = (
        P(("groups", "row"), ("col", "sub")),
        P(),
        P("row", ("col", "sub")),
        P("row", ("col", "sub")),
        P("row", ("col", "sub")),
        P(),
        P(),
        P("row", ("col", "sub")),
        P(("col", "sub")),
    )
    return jax.shard_map(
        on_device,
        mesh=mesh,
        in_specs=placed,
        out_specs=P(("groups", "row"), ("col", "sub")),
        check_vma=False,
    )
```

```python
import functools

import jax
import jax.numpy as jnp
from jax import lax
from jax.experimental import pallas as pl
from jax.experimental.pallas import tpu as pltpu
from jax.sharding import PartitionSpec as P

MODEL_WIDTH = 5376
QUERY_HEAD_COUNT = 32
WINDOW_LENGTH = 1024


EPSILON = 1e-06
MIDDLE = (1, 2)
ENDS = (0, 3)
VMEM_BYTES = 60 * 1024 * 1024


def shifted(x, axis, by):
    count = lax.axis_size(axis)
    pairs = [(i, i + by) for i in range(count) if 0 <= i + by < count]
    return lax.ppermute(x, axis, pairs)


def root_mean_scale(values, gain):
    return values * lax.rsqrt(jnp.mean(values * values, axis=-1, keepdims=True) + EPSILON) * gain


def rotary_tables(token_positions, size):
    half_dim = size // 2
    inverse = 10000.0 ** (-(jnp.arange(half_dim, dtype=jnp.float32) * 2.0) / size)
    angles = token_positions[:, None] * inverse[None, :]
    return jnp.cos(angles), jnp.sin(angles)


def apply_rotary(tensor, token_positions):
    half_dim = tensor.shape[-1] // 2
    cosine, sine_part = rotary_tables(token_positions, tensor.shape[-1])
    cosine, sine_part = cosine[:, None, :], sine_part[:, None, :]
    first_half = tensor[..., :half_dim]
    second_half = tensor[..., half_dim:]
    return jnp.concatenate(
        [
            first_half * cosine - second_half * sine_part,
            second_half * cosine + first_half * sine_part,
        ],
        axis=-1,
    )


def general_form(
    stream_in,
    in_gain,
    query_weight,
    key_matrix,
    value_matrix,
    query_gain,
    key_norm_gain,
    output_weight,
    post_gain,
):
    token_rows = lax.all_gather(stream_in, ("col", "sub"), axis=1, tiled=True)
    tokens = token_rows.shape[0]
    normed = root_mean_scale(token_rows.astype(jnp.float32), in_gain).astype(jnp.bfloat16)

    def add_panel(panel_piece):
        return jnp.dot(normed, panel_piece, preferred_element_type=jnp.float32)

    query_proj = add_panel(lax.all_gather(query_weight, "row", axis=0, tiled=True))
    projected_keys = add_panel(lax.all_gather(key_matrix, "row", axis=0, tiled=True))
    projected_values = add_panel(lax.all_gather(value_matrix, "row", axis=0, tiled=True))
    head_size = query_gain.shape[0]
    query_heads = query_weight.shape[1] // head_size
    pair_heads = key_matrix.shape[1] // head_size
    group_count = query_heads // pair_heads
    scale_factor = float(MODEL_WIDTH // QUERY_HEAD_COUNT) ** (-0.5)
    row_index = lax.axis_index("row")
    query_places = row_index * tokens + jnp.arange(tokens, dtype=jnp.int32)
    query_rot = apply_rotary(
        root_mean_scale(query_proj.reshape(tokens, query_heads, head_size), query_gain),
        query_places.astype(jnp.float32),
    ).astype(jnp.bfloat16)
    rotary_keys = apply_rotary(
        root_mean_scale(projected_keys.reshape(tokens, pair_heads, head_size), key_norm_gain),
        query_places.astype(jnp.float32),
    ).astype(jnp.bfloat16)
    keys_flat = rotary_keys.reshape(tokens, pair_heads * head_size)
    values_flat = projected_values.astype(jnp.bfloat16)
    shards_back = min(WINDOW_LENGTH // tokens, lax.axis_size("row") - 1)
    band_length = (shards_back + 1) * tokens
    key_parts = [keys_flat]
    value_parts = [values_flat]
    for offset in range(1, shards_back + 1):
        keys_prior, values_prior = shifted((keys_flat, values_flat), "row", offset)
        key_parts = [keys_prior] + key_parts
        value_parts = [values_prior] + value_parts
    keys_band = jnp.concatenate(key_parts, axis=0)
    values_band = jnp.concatenate(value_parts, axis=0)
    key_places = (row_index - shards_back) * tokens + jnp.arange(band_length, dtype=jnp.int32)
    distance = query_places[:, None] - key_places[None, :]
    visible = (distance >= 0) & (distance < WINDOW_LENGTH) & (key_places[None, :] >= 0)
    grouped = query_rot.reshape(tokens, pair_heads, group_count, head_size)
    scores = (
        jnp.einsum(
            "qhgd,shd->hgqs",
            grouped,
            keys_band.reshape(band_length, pair_heads, head_size),
            preferred_element_type=jnp.float32,
        )
        * scale_factor
    )
    scores = jnp.where(visible, scores, -1e30)
    row_max = jnp.max(scores, axis=-1, keepdims=True)
    exponent = jnp.exp(scores - row_max)
    weights = (exponent / jnp.sum(exponent, axis=-1, keepdims=True)).astype(jnp.bfloat16)
    attended = jnp.einsum(
        "hgqs,shd->qhgd",
        weights,
        values_band.reshape(band_length, pair_heads, head_size),
        preferred_element_type=jnp.float32,
    )
    heads_out = attended.reshape(tokens, query_heads * head_size).astype(jnp.bfloat16)
    head_rows = lax.all_gather(heads_out, ("col", "sub"), axis=1, tiled=True)
    branch = jnp.dot(
        head_rows,
        lax.all_gather(output_weight, "row", axis=0, tiled=True),
        preferred_element_type=jnp.float32,
    )
    squares = lax.psum(jnp.sum(branch * branch, axis=-1), ("col", "sub"))
    scaled = branch * lax.rsqrt(squares[:, None] / MODEL_WIDTH + EPSILON) * post_gain
    return (stream_in.astype(jnp.float32) + scaled).astype(jnp.bfloat16)


def swapped(x, axis, rows):
    if axis == "groups":
        count = lax.axis_size("row")
        pairs = [(count * i + r, count * (1 - i) + r) for r in rows for i in range(2)]
        return lax.ppermute(x, ("groups", "row"), pairs)
    pairs = [(2 * r + i, 2 * r + 1 - i) for r in rows for i in range(2)]
    return lax.ppermute(x, ("row", axis), pairs)


def after(x, *earlier):
    return lax.optimization_barrier((x, *earlier))[0]


def whole(shape):
    return pl.BlockSpec(shape, lambda *_: (0,) * len(shape))


def norm_kernel(table, *refs):
    *pieces, gain, out = refs[-6:]
    depth = pieces[0].shape[0]
    squares = sum(
        jnp.sum(jnp.square(p[...].astype(jnp.float32)), axis=0, keepdims=True) for p in pieces
    )
    scale = lax.rsqrt(squares / MODEL_WIDTH + EPSILON)
    for index, piece in enumerate(pieces):
        rows = pl.ds(pl.multiple_of(table[index] * depth, depth), depth)
        out[0, rows, :] = (piece[...].astype(jnp.float32) * scale * gain[rows, :]).astype(jnp.bfloat16)


def norm_block(table, pieces, gain, index, held):
    depth, tokens = pieces[0].shape
    lanes = 128
    shape = (4, 4 * depth, tokens)
    before = () if held is None else (held,)
    return pl.pallas_call(
        norm_kernel,
        grid_spec=pltpu.PrefetchScalarGridSpec(
            num_scalar_prefetch=1,
            grid=(tokens // lanes,),
            in_specs=[pl.BlockSpec(memory_space=pl.ANY)] * len(before)
            + [pl.BlockSpec((depth, lanes), lambda t, *_: (0, t))] * 4
            + [whole((4 * depth, 1))],
            out_specs=pl.BlockSpec((1, 4 * depth, lanes), lambda t, *_: (index, 0, t)),
        ),
        out_shape=jax.ShapeDtypeStruct(shape, jnp.bfloat16),
        input_output_aliases={1: 0} if before else {},
        compiler_params=pltpu.CompilerParams(vmem_limit_bytes=VMEM_BYTES),
        cost_estimate=pl.CostEstimate(
            flops=40 * depth * tokens, bytes_accessed=16 * depth * tokens, transcendentals=0
        ),
    )(table, *before, *pieces, gain)


def project_kernel(last, table, *refs):
    parts, pieces, refs = refs[:2], refs[2:6], refs[6:]
    turned = refs[-1]
    width, depth = pieces[0].shape[1], pieces[0].shape[0]

    @pl.when(pl.program_id(0) == 0)
    def _():
        for index, piece in enumerate(pieces):
            rows = pl.ds(pl.multiple_of(table[6 + index] * width, width), width)
            turned[index // 2, rows, :] = piece[...].T

    total = refs[-2] if last else refs[0].at[0]
    step = width // 2
    for start in range(0, 2 * width, step):
        rows = slice(start, start + step)
        product = sum(
            jnp.dot(turned[index, rows, :], part[0], preferred_element_type=jnp.float32)
            for index, part in enumerate(parts)
        )
        total[rows, :] = product + refs[0][0, rows, :] if last else product

    if last:
        _, q_gain, k_gain, cosine, sine, q_out, k_out, v_out = refs[:8]
        head = q_gain.shape[0]
        half = head // 2
        cos, sin = cosine[...], sine[...]

        def rotated(start, head_gain):
            values = total[start : start + head, :]
            values = (
                values
                * lax.rsqrt(jnp.mean(values * values, axis=0, keepdims=True) + EPSILON)
                * head_gain[...]
            )
            first, second = values[:half], values[half:]
            return jnp.concatenate(
                [first * cos - second * sin, second * cos + first * sin], axis=0
            ).astype(jnp.bfloat16)

        for start in range(0, width, head):
            q_out[0, start : start + head, :] = rotated(start, q_gain)
        for start in range(0, width // 2, head):
            k_out[:, start : start + head] = rotated(width + start, k_gain).T
        v_out[...] = total[width + width // 2 :, :].astype(jnp.bfloat16)


def project(table, normed, pieces, held=None, extras=()):
    blocks, features, tokens = normed.shape
    depth, width = pieces[0].shape
    last = held is not None
    part = lambda which: pl.BlockSpec((1, depth, tokens), lambda i, t: (i, t[which], 0))
    total = pl.BlockSpec((1, 2 * width, tokens), lambda i, t: (i, 0, 0))
    in_specs = [part(0), part(1)] + [whole((depth, width))] * 4
    scratch = [pltpu.VMEM((2, 2 * width, depth), jnp.bfloat16)]
    if last:
        head = extras[0].shape[0]
        half = head // 2
        turn = pl.BlockSpec((half, tokens), lambda i, t: (0, t[2 + i]))
        in_specs += [total, whole((head, 1)), whole((head, 1)), turn, turn]
        out_specs = [
            pl.BlockSpec((1, width, tokens), lambda i, t: (i, 0, 0)),
            pl.BlockSpec((tokens, width // 2), lambda i, t: (t[2 + i], 0)),
            pl.BlockSpec((width // 2, tokens), lambda i, t: (0, t[2 + i])),
        ]
        out_shape = [
            jax.ShapeDtypeStruct((blocks, width, tokens), jnp.bfloat16),
            jax.ShapeDtypeStruct((blocks * tokens, width // 2), jnp.bfloat16),
            jax.ShapeDtypeStruct((width // 2, blocks * tokens), jnp.bfloat16),
        ]
        scratch = [pltpu.VMEM((2 * width, tokens), jnp.float32)] + scratch
        operands = (held, *extras)
    else:
        out_specs = total
        out_shape = jax.ShapeDtypeStruct((blocks, 2 * width, tokens), jnp.float32)
        operands = ()
    return pl.pallas_call(
        functools.partial(project_kernel, last),
        grid_spec=pltpu.PrefetchScalarGridSpec(
            num_scalar_prefetch=1,
            grid=(blocks,),
            in_specs=in_specs,
            out_specs=out_specs,
            scratch_shapes=scratch,
        ),
        out_shape=out_shape,
        compiler_params=pltpu.CompilerParams(vmem_limit_bytes=VMEM_BYTES),
        cost_estimate=pl.CostEstimate(
            flops=2 * blocks * tokens * 2 * depth * 2 * width,
            bytes_accessed=4 * blocks * depth * tokens + 8 * depth * width + 8 * blocks * width * tokens,
            transcendentals=0,
        ),
    )(table, normed, normed, *pieces, *operands)


def attend_kernel(band, scale, table, q_ref, keys, values, out):
    head = 128
    tile = out.shape[1]
    first = table[0] * (2 * tile) + pl.program_id(0) * tile
    start = pl.multiple_of(jnp.clip(first + tile - band, 0, keys.shape[0] - band), tile)
    rows = pl.ds(start, band)
    distance = (
        (first - start)
        + lax.broadcasted_iota(jnp.int32, (band, tile), 1)
        - lax.broadcasted_iota(jnp.int32, (band, tile), 0)
    )
    visible = (distance >= 0) & (distance < WINDOW_LENGTH)
    heads = out.shape[0] // head
    group = heads // (keys.shape[1] // head)
    for index in range(heads):
        here = slice(index * head, (index + 1) * head)
        shared = slice((index // group) * head, (index // group + 1) * head)
        scores = jnp.dot(keys[rows, shared], q_ref[0, here, :], preferred_element_type=jnp.float32)
        scores = jnp.where(visible, scores * scale, -1e30)
        exponent = jnp.exp(scores - jnp.max(scores, axis=0, keepdims=True))
        weights = exponent * (1.0 / jnp.sum(exponent, axis=0, keepdims=True))
        out[here, :] = jnp.dot(
            values[shared, rows], weights.astype(jnp.bfloat16), preferred_element_type=jnp.float32
        ).astype(jnp.bfloat16)


def attend(block, index, queries, keys, values):
    _, width, tokens = queries.shape
    tile = tokens // 2
    band = min(WINDOW_LENGTH + tile, keys.shape[0])
    return pl.pallas_call(
        functools.partial(attend_kernel, band, float(MODEL_WIDTH // QUERY_HEAD_COUNT) ** (-0.5)),
        grid_spec=pltpu.PrefetchScalarGridSpec(
            num_scalar_prefetch=1,
            grid=(2,),
            in_specs=[
                pl.BlockSpec((1, width, tile), lambda t, *_: (index, 0, t)),
                whole(keys.shape),
                whole(values.shape),
            ],
            out_specs=pl.BlockSpec((width, tile), lambda t, *_: (0, t)),
        ),
        out_shape=jax.ShapeDtypeStruct((width, tokens), jnp.bfloat16),
        compiler_params=pltpu.CompilerParams(vmem_limit_bytes=VMEM_BYTES),
        cost_estimate=pl.CostEstimate(
            flops=4 * tokens * band * width,
            bytes_accessed=4 * tokens * width + 4 * keys.shape[0] * keys.shape[1],
            transcendentals=tokens * band * (width // 128),
        ),
    )(block[None], queries, keys, values)


def output_kernel(count, table, *refs):
    parts, pieces, (out, squares, held) = refs[:8], refs[8 : 8 + count], refs[8 + count :]
    step = pl.program_id(0)

    @pl.when(step == 0)
    def _():
        for index, part in enumerate(parts):
            held[index] = part[...]

    for index, piece in enumerate(pieces):

        @pl.when((step == index) & (table[index] < len(parts)))
        def _(index=index, piece=piece):
            product = jnp.dot(piece[...], held[table[index]], preferred_element_type=jnp.float32)
            if index == 0:
                out[...] = product
            else:
                out[...] += product

    @pl.when(step == count - 1)
    def _():
        squares[...] = jnp.sum(jnp.square(out[...]), axis=0, keepdims=True)


def output_product(table, parts, pieces):
    depth, tokens = parts[0].shape
    width = pieces[0].shape[0]
    count = len(pieces)
    return pl.pallas_call(
        functools.partial(output_kernel, count),
        grid_spec=pltpu.PrefetchScalarGridSpec(
            num_scalar_prefetch=1,
            grid=(count,),
            in_specs=[whole((depth, tokens))] * 8 + [whole((width, depth))] * count,
            out_specs=[whole((width, tokens)), whole((1, tokens))],
            scratch_shapes=[pltpu.VMEM((8, depth, tokens), jnp.bfloat16)],
        ),
        out_shape=[
            jax.ShapeDtypeStruct((width, tokens), jnp.float32),
            jax.ShapeDtypeStruct((1, tokens), jnp.float32),
        ],
        compiler_params=pltpu.CompilerParams(vmem_limit_bytes=VMEM_BYTES),
        cost_estimate=pl.CostEstimate(
            flops=2 * tokens * depth * 8 * width,
            bytes_accessed=2 * 8 * (tokens + width) * depth + 4 * tokens * width,
            transcendentals=0,
        ),
    )(table, *parts, *pieces)


def middle_form(
    stream_in,
    in_gain,
    query_weight,
    key_matrix,
    value_matrix,
    query_gain,
    key_norm_gain,
    output_weight,
    post_gain,
):
    stream = stream_in.T
    features, tokens = stream.shape
    head = query_gain.shape[0]
    row = lax.axis_index("row")
    group = lax.axis_index("groups")
    place = lax.axis_index("col") * 2 + lax.axis_index("sub")
    upper = (row >= 2).astype(jnp.int32)
    in_middle = (row == 1) | (row == 2)
    near_block, cross_block, far_block = 3 * upper, 3 - row, 3 - 3 * upper
    blocks = (row, near_block, cross_block, far_block)
    slot = lambda block: jnp.bitwise_xor(place, block)
    everywhere = MIDDLE + ENDS
    inward = [(0, 1), (3, 2)]
    across = [(1, 2), (2, 1)]
    outward = [(1, 0), (2, 3)]

    x_near = lax.ppermute(stream, "row", inward)
    x_cross = lax.ppermute(stream, "row", across)
    own_sub = swapped(stream, "sub", MIDDLE)
    own_col = swapped(stream, "col", MIDDLE)

    half = query_weight.shape[1] // 2
    quarter = key_matrix.shape[1] // 2

    def side(which):
        queries = lax.dynamic_slice_in_dim(query_weight, which * half, half, axis=1)
        keys = lax.dynamic_slice_in_dim(key_matrix, which * quarter, quarter, axis=1)
        values = lax.dynamic_slice_in_dim(value_matrix, which * quarter, quarter, axis=1)
        return queries, jnp.concatenate([keys, values], axis=1)

    own_queries, own_pairs = side(upper)
    other_queries, other_pairs = side(1 - upper)
    own_side = jnp.where(group == 0, own_queries, own_pairs)
    other_side = jnp.where(group == 0, other_queries, other_pairs)

    x_far = lax.ppermute(x_near, "row", across)
    w_near = lax.ppermute(own_side, "row", inward)
    w_far = lax.ppermute(other_side, "row", [(0, 2), (3, 1)])
    w_cross = lax.ppermute(after(other_side, x_far), "row", across)
    w_near_y = swapped(w_near, "groups", MIDDLE)
    w_far_y = swapped(w_far, "groups", MIDDLE)
    w_cross_y = swapped(w_cross, "groups", MIDDLE)

    depth = output_weight.shape[0] // 2
    turned = output_weight.T
    mine = lax.dynamic_slice_in_dim(turned, group * depth, depth, axis=1)
    mine = after(mine, x_far)
    o_pair = lax.ppermute(mine, "row", inward + outward)
    mine = after(mine, w_far)
    o_cross = lax.ppermute(mine, "row", across)
    o_far = lax.ppermute(o_pair, "row", across)
    o_end_cross = lax.ppermute(o_cross, "row", outward)
    o_end_far = lax.ppermute(o_far, "row", outward)
    pair_block = jnp.bitwise_xor(row, 1)
    mine_half = jnp.bitwise_xor(group, upper)
    out_pieces, out_table = [], []
    for part in range(2):
        out_pieces.append(turned[:, part * depth : (part + 1) * depth])
        out_table.append(2 * slot(row) + jnp.bitwise_xor(part, upper))
    for piece, block, rows in (
        (o_pair, pair_block, everywhere),
        (o_cross, 3 - row, MIDDLE),
        (o_far, 3 - pair_block, MIDDLE),
        (o_end_cross, 3 - pair_block, ENDS),
        (o_end_far, 3 - row, ENDS),
    ):
        here = True if rows == everywhere else in_middle if rows == MIDDLE else ~in_middle
        out_pieces += [piece, swapped(piece, "groups", rows)]
        out_table += [
            jnp.where(here, 2 * slot(block) + mine_half, 8),
            jnp.where(here, 2 * slot(block) + 1 - mine_half, 8),
        ]

    positions = jnp.arange(4 * tokens, dtype=jnp.int32).astype(jnp.float32)
    cosine, sine = rotary_tables(positions, head)
    gain = in_gain[:, None]
    order = jnp.stack([slot(j) for j in range(4)]).astype(jnp.int32)
    normed = None
    for index, piece in enumerate((stream, x_near, x_cross, x_far)):
        sub = own_sub if index == 0 else swapped(piece, "sub", MIDDLE)
        col = own_col if index == 0 else swapped(piece, "col", MIDDLE)
        pieces = (piece, sub, col, swapped(col, "sub", MIDDLE))
        normed = norm_block(order, pieces, gain, index, normed)

    zero, one = jnp.zeros_like(group), jnp.ones_like(group)
    total = project(
        jnp.stack([row, near_block, *blocks, zero, one, group, 1 - group]).astype(jnp.int32),
        normed,
        (own_queries, own_pairs, w_near, w_near_y),
    )
    queries, keys, values = project(
        jnp.stack([far_block, cross_block, *blocks, group, 1 - group, group, 1 - group]).astype(jnp.int32),
        normed,
        (w_far, w_far_y, w_cross, w_cross_y),
        total,
        (query_gain[:, None], key_norm_gain[:, None], cosine.T, sine.T),
    )

    def attended(index):
        return attend(blocks[index].astype(jnp.int32), index, queries, keys, values)

    to_far = lax.ppermute(attended(3), "row", [(1, 3), (2, 0)])
    to_near = lax.ppermute(attended(1), "row", outward)
    to_cross = lax.ppermute(attended(2), "row", across)
    this_side = jnp.where(in_middle, attended(0), to_near)
    that_side = jnp.where(in_middle, to_cross, to_far)
    this_across = swapped(this_side, "col", everywhere)
    that_across = swapped(that_side, "col", everywhere)
    parts = (
        this_side,
        that_side,
        swapped(this_side, "sub", everywhere),
        swapped(that_side, "sub", everywhere),
        this_across,
        that_across,
        swapped(this_across, "sub", everywhere),
        swapped(that_across, "sub", everywhere),
    )
    branch, squares = output_product(jnp.stack(out_table).astype(jnp.int32), parts, out_pieces)
    squares = squares + swapped(squares, "sub", everywhere)
    squares = squares + swapped(squares, "col", everywhere)
    scaled = branch * lax.rsqrt(squares / MODEL_WIDTH + EPSILON) * post_gain[:, None]
    return (stream.astype(jnp.float32) + scaled).astype(jnp.bfloat16).T


def on_device(*args):
    stream_in, _, query_weight, key_matrix, value_matrix, query_gain, *_ = args
    sizes = tuple(lax.axis_size(name) for name in ("groups", "row", "col", "sub"))
    tokens, head = stream_in.shape[0], query_gain.shape[0]
    fits = (
        sizes == (2, 4, 2, 2)
        and head == 128
        and tokens % 256 == 0
        and key_matrix.shape[1] % (2 * head) == 0
        and query_weight.shape[1] == 2 * key_matrix.shape[1]
        and value_matrix.shape[1] == key_matrix.shape[1]
    )
    return middle_form(*args) if fits else general_form(*args)


def solution(mesh):
    placed = (
        P(("groups", "row"), ("col", "sub")),
        P(),
        P("row", ("col", "sub")),
        P("row", ("col", "sub")),
        P("row", ("col", "sub")),
        P(),
        P(),
        P("row", ("col", "sub")),
        P(("col", "sub")),
    )
    return jax.shard_map(
        on_device,
        mesh=mesh,
        in_specs=placed,
        out_specs=P(("groups", "row"), ("col", "sub")),
        check_vma=False,
    )
```

```python
import functools

import jax
import jax.numpy as jnp
from jax import lax
from jax.experimental import pallas as pl
from jax.experimental.pallas import tpu as pltpu
from jax.sharding import PartitionSpec as P

MODEL_WIDTH = 5376
QUERY_HEAD_COUNT = 32
WINDOW_LENGTH = 1024


EPSILON = 1e-06
MIDDLE = (1, 2)
ENDS = (0, 3)
VMEM_BYTES = 60 * 1024 * 1024


def shifted(x, axis, by):
    count = lax.axis_size(axis)
    pairs = [(i, i + by) for i in range(count) if 0 <= i + by < count]
    return lax.ppermute(x, axis, pairs)


def root_mean_scale(values, gain):
    return values * lax.rsqrt(jnp.mean(values * values, axis=-1, keepdims=True) + EPSILON) * gain


def rotary_tables(token_positions, size):
    half_dim = size // 2
    inverse = 10000.0 ** (-(jnp.arange(half_dim, dtype=jnp.float32) * 2.0) / size)
    angles = token_positions[:, None] * inverse[None, :]
    return jnp.cos(angles), jnp.sin(angles)


def apply_rotary(tensor, token_positions):
    half_dim = tensor.shape[-1] // 2
    cosine, sine_part = rotary_tables(token_positions, tensor.shape[-1])
    cosine, sine_part = cosine[:, None, :], sine_part[:, None, :]
    first_half = tensor[..., :half_dim]
    second_half = tensor[..., half_dim:]
    return jnp.concatenate(
        [
            first_half * cosine - second_half * sine_part,
            second_half * cosine + first_half * sine_part,
        ],
        axis=-1,
    )


def general_form(
    stream_in,
    in_gain,
    query_weight,
    key_matrix,
    value_matrix,
    query_gain,
    key_norm_gain,
    output_weight,
    post_gain,
):
    token_rows = lax.all_gather(stream_in, ("col", "sub"), axis=1, tiled=True)
    tokens = token_rows.shape[0]
    normed = root_mean_scale(token_rows.astype(jnp.float32), in_gain).astype(jnp.bfloat16)

    def add_panel(panel_piece):
        return jnp.dot(normed, panel_piece, preferred_element_type=jnp.float32)

    query_proj = add_panel(lax.all_gather(query_weight, "row", axis=0, tiled=True))
    projected_keys = add_panel(lax.all_gather(key_matrix, "row", axis=0, tiled=True))
    projected_values = add_panel(lax.all_gather(value_matrix, "row", axis=0, tiled=True))
    head_size = query_gain.shape[0]
    query_heads = query_weight.shape[1] // head_size
    pair_heads = key_matrix.shape[1] // head_size
    group_count = query_heads // pair_heads
    scale_factor = float(MODEL_WIDTH // QUERY_HEAD_COUNT) ** (-0.5)
    row_index = lax.axis_index("row")
    query_places = row_index * tokens + jnp.arange(tokens, dtype=jnp.int32)
    query_rot = apply_rotary(
        root_mean_scale(query_proj.reshape(tokens, query_heads, head_size), query_gain),
        query_places.astype(jnp.float32),
    ).astype(jnp.bfloat16)
    rotary_keys = apply_rotary(
        root_mean_scale(projected_keys.reshape(tokens, pair_heads, head_size), key_norm_gain),
        query_places.astype(jnp.float32),
    ).astype(jnp.bfloat16)
    keys_flat = rotary_keys.reshape(tokens, pair_heads * head_size)
    values_flat = projected_values.astype(jnp.bfloat16)
    shards_back = min(WINDOW_LENGTH // tokens, lax.axis_size("row") - 1)
    band_length = (shards_back + 1) * tokens
    key_parts = [keys_flat]
    value_parts = [values_flat]
    for offset in range(1, shards_back + 1):
        keys_prior, values_prior = shifted((keys_flat, values_flat), "row", offset)
        key_parts = [keys_prior] + key_parts
        value_parts = [values_prior] + value_parts
    keys_band = jnp.concatenate(key_parts, axis=0)
    values_band = jnp.concatenate(value_parts, axis=0)
    key_places = (row_index - shards_back) * tokens + jnp.arange(band_length, dtype=jnp.int32)
    distance = query_places[:, None] - key_places[None, :]
    visible = (distance >= 0) & (distance < WINDOW_LENGTH) & (key_places[None, :] >= 0)
    grouped = query_rot.reshape(tokens, pair_heads, group_count, head_size)
    scores = (
        jnp.einsum(
            "qhgd,shd->hgqs",
            grouped,
            keys_band.reshape(band_length, pair_heads, head_size),
            preferred_element_type=jnp.float32,
        )
        * scale_factor
    )
    scores = jnp.where(visible, scores, -1e30)
    row_max = jnp.max(scores, axis=-1, keepdims=True)
    exponent = jnp.exp(scores - row_max)
    weights = (exponent / jnp.sum(exponent, axis=-1, keepdims=True)).astype(jnp.bfloat16)
    attended = jnp.einsum(
        "hgqs,shd->qhgd",
        weights,
        values_band.reshape(band_length, pair_heads, head_size),
        preferred_element_type=jnp.float32,
    )
    heads_out = attended.reshape(tokens, query_heads * head_size).astype(jnp.bfloat16)
    head_rows = lax.all_gather(heads_out, ("col", "sub"), axis=1, tiled=True)
    branch = jnp.dot(
        head_rows,
        lax.all_gather(output_weight, "row", axis=0, tiled=True),
        preferred_element_type=jnp.float32,
    )
    squares = lax.psum(jnp.sum(branch * branch, axis=-1), ("col", "sub"))
    scaled = branch * lax.rsqrt(squares[:, None] / MODEL_WIDTH + EPSILON) * post_gain
    return (stream_in.astype(jnp.float32) + scaled).astype(jnp.bfloat16)


def swapped(x, axis, rows):
    if axis == "groups":
        count = lax.axis_size("row")
        pairs = [(count * i + r, count * (1 - i) + r) for r in rows for i in range(2)]
        return lax.ppermute(x, ("groups", "row"), pairs)
    pairs = [(2 * r + i, 2 * r + 1 - i) for r in rows for i in range(2)]
    return lax.ppermute(x, ("row", axis), pairs)


def after(x, *earlier):
    return lax.optimization_barrier((x, *earlier))[0]


def settle(*values):
    return lax.optimization_barrier(values)


def whole(shape):
    return pl.BlockSpec(shape, lambda *_: (0,) * len(shape))


ANYWHERE = pl.BlockSpec(memory_space=pl.ANY)


def norm_kernel(table, *refs):
    *pieces, gain, out = refs[-6:]
    depth = pieces[0].shape[1]
    squares = sum(
        jnp.sum(jnp.square(p[0].astype(jnp.float32)), axis=0, keepdims=True) for p in pieces
    )
    scale = lax.rsqrt(squares / MODEL_WIDTH + EPSILON)
    for index, piece in enumerate(pieces):
        rows = pl.ds(pl.multiple_of(table[index] * depth, depth), depth)
        out[0, rows, :] = (piece[0].astype(jnp.float32) * scale * gain[index]).astype(jnp.bfloat16)


def norm_block(table, pieces, which, gain, index, held):
    _, depth, tokens = pieces[0].shape
    lanes = tokens // 2
    shape = (4, 4 * depth, tokens)
    before = () if held is None else (held,)
    return pl.pallas_call(
        norm_kernel,
        grid_spec=pltpu.PrefetchScalarGridSpec(
            num_scalar_prefetch=1,
            grid=(tokens // lanes,),
            in_specs=[ANYWHERE] * len(before)
            + [pl.BlockSpec((1, depth, lanes), lambda t, *_: (which, 0, t))] * 4
            + [whole((4, depth, 1))],
            out_specs=pl.BlockSpec((1, 4 * depth, lanes), lambda t, *_: (index, 0, t)),
        ),
        out_shape=jax.ShapeDtypeStruct(shape, jnp.bfloat16),
        input_output_aliases={1: 0} if before else {},
        compiler_params=pltpu.CompilerParams(vmem_limit_bytes=VMEM_BYTES),
        cost_estimate=pl.CostEstimate(
            flops=40 * depth * tokens, bytes_accessed=16 * depth * tokens, transcendentals=0
        ),
    )(table, *before, *pieces, gain)


def order_pieces(table, pieces, ordered):
    base = 0
    for index, piece in enumerate(pieces):
        depth, width = piece.shape
        rows = pl.ds(pl.multiple_of(table[2 * index], 16), depth)
        columns = pl.ds(pl.multiple_of(table[2 * index + 1], width), width)
        ordered[rows, columns] = piece[...]


def project_early_kernel(count, table, normed, *refs):
    pieces, out, ordered = refs[:count], refs[-2], refs[-1]

    @pl.when(pl.program_id(0) == 0)
    def _():
        order_pieces(table, pieces, ordered)

    out[0] = lax.dot_general(
        ordered[...], normed[0], (((0,), (0,)), ((), ())), preferred_element_type=jnp.float32
    )


def project_early(table, normed, pieces, first, blocks, held):
    _, features, tokens = normed.shape
    width = 2 * pieces[0].shape[1]
    before = () if held is None else (held,)
    return pl.pallas_call(
        functools.partial(project_early_kernel, len(pieces)),
        grid_spec=pltpu.PrefetchScalarGridSpec(
            num_scalar_prefetch=1,
            grid=(blocks,),
            in_specs=[pl.BlockSpec((1, features // 2, tokens), lambda i, t: (first + i, 0, 0))]
            + [whole(p.shape) for p in pieces]
            + [ANYWHERE] * len(before),
            out_specs=pl.BlockSpec((1, width, tokens), lambda i, t: (first + i, 0, 0)),
            scratch_shapes=[pltpu.VMEM((features // 2, width), jnp.bfloat16)],
        ),
        out_shape=jax.ShapeDtypeStruct((4, width, tokens), jnp.float32),
        input_output_aliases={2 + len(pieces): 0} if before else {},
        compiler_params=pltpu.CompilerParams(vmem_limit_bytes=VMEM_BYTES),
        cost_estimate=pl.CostEstimate(
            flops=2 * blocks * tokens * features // 2 * width,
            bytes_accessed=blocks * features * tokens + features * width + 4 * blocks * width * tokens,
            transcendentals=0,
        ),
    )(table, normed, *pieces, *before)


def project_late_kernel(count, table, normed, *refs):
    pieces, refs = refs[:count], refs[count:]
    early, q_gain, k_gain, cosine, sine, q_out, k_out, v_out, total, ordered = refs

    @pl.when(pl.program_id(0) == 0)
    def _():
        order_pieces(table, pieces, ordered)

    total[...] = early[0] + lax.dot_general(
        ordered[...], normed[0], (((0,), (0,)), ((), ())), preferred_element_type=jnp.float32
    )
    head = q_gain.shape[0]
    half = head // 2
    width = q_out.shape[1]
    cos, sin = cosine[...], sine[...]

    def rotated(start, head_gain):
        values = total[start : start + head, :]
        values = (
            values
            * lax.rsqrt(jnp.mean(values * values, axis=0, keepdims=True) + EPSILON)
            * head_gain[...]
        )
        first, second = values[:half], values[half:]
        return jnp.concatenate(
            [first * cos - second * sin, second * cos + first * sin], axis=0
        ).astype(jnp.bfloat16)

    for start in range(0, width, head):
        q_out[0, start : start + head, :] = rotated(start, q_gain)
    for start in range(0, width // 2, head):
        k_out[:, start : start + head] = rotated(width + start, k_gain).T
    v_out[...] = total[width + width // 2 :, :].astype(jnp.bfloat16)


def project_late(table, normed, pieces, early, extras):
    blocks, features, tokens = normed.shape
    width = early.shape[1] // 2
    head = extras[0].shape[0]
    half = head // 2
    count = len(pieces)
    turn = pl.BlockSpec((half, tokens), lambda i, t: (0, t[2 * count + i]))
    return pl.pallas_call(
        functools.partial(project_late_kernel, count),
        grid_spec=pltpu.PrefetchScalarGridSpec(
            num_scalar_prefetch=1,
            grid=(blocks,),
            in_specs=[pl.BlockSpec((1, features // 2, tokens), lambda i, t: (i, 1, 0))]
            + [whole(p.shape) for p in pieces]
            + [
                pl.BlockSpec((1, 2 * width, tokens), lambda i, t: (i, 0, 0)),
                whole((head, 1)),
                whole((head, 1)),
                turn,
                turn,
            ],
            out_specs=[
                pl.BlockSpec((1, width, tokens), lambda i, t: (i, 0, 0)),
                pl.BlockSpec((tokens, width // 2), lambda i, t: (t[2 * count + i], 0)),
                pl.BlockSpec((width // 2, tokens), lambda i, t: (0, t[2 * count + i])),
            ],
            scratch_shapes=[
                pltpu.VMEM((2 * width, tokens), jnp.float32),
                pltpu.VMEM((features // 2, 2 * width), jnp.bfloat16),
            ],
        ),
        out_shape=[
            jax.ShapeDtypeStruct((blocks, width, tokens), jnp.bfloat16),
            jax.ShapeDtypeStruct((blocks * tokens, width // 2), jnp.bfloat16),
            jax.ShapeDtypeStruct((width // 2, blocks * tokens), jnp.bfloat16),
        ],
        compiler_params=pltpu.CompilerParams(vmem_limit_bytes=VMEM_BYTES),
        cost_estimate=pl.CostEstimate(
            flops=2 * blocks * tokens * features * width,
            bytes_accessed=blocks * features * tokens + 2 * features * width + 8 * blocks * width * tokens,
            transcendentals=0,
        ),
    )(table, normed, *pieces, early, *extras)


def attend_kernel(band, scale, table, q_ref, keys, values, *refs):
    out, mask = refs[-2:]
    head = 128
    tile = out.shape[1]
    first = table[0] * (2 * tile) + pl.program_id(0) * tile
    start = pl.multiple_of(jnp.clip(first + tile - band, 0, keys.shape[0] - band), tile)
    places = lax.broadcasted_iota(jnp.int32, (band, tile), 1)
    distance = (first - start) + places - lax.broadcasted_iota(jnp.int32, (band, tile), 0)
    hidden = jnp.where((distance >= 0) & (distance < WINDOW_LENGTH), 0.0, -1e30)
    mask[:, :tile] = hidden
    mask[:, tile:] = hidden
    pairs = keys.shape[1] // head
    factor = scale * 1.4426950408889634
    chunks = [slice(a, min(a + tile, band)) for a in range(0, band, tile)]

    def pair_of(ref, index):
        return [slice((2 * index + i) * head, (2 * index + i + 1) * head) for i in range(2)]

    def query(index):
        return jnp.concatenate([q_ref[0, rows, :] for rows in pair_of(q_ref, index)], axis=1)

    def within(chunk):
        return pl.ds(pl.multiple_of(start + chunk.start, tile), chunk.stop - chunk.start)

    def score(index, chunk, queries):
        columns = slice(index * head, (index + 1) * head)
        return mask[chunk, :] + jnp.dot(
            keys[within(chunk), columns], queries, preferred_element_type=jnp.float32
        )

    queries = query(0)
    scores = [score(0, chunk, queries) for chunk in chunks]
    for index in range(pairs):
        top = functools.reduce(
            jnp.maximum, [jnp.max(part, axis=0, keepdims=True) for part in scores]
        )
        queries = query(index + 1) if index + 1 < pairs else None
        exponents, upcoming, total = [], [], 0.0
        for chunk, part in zip(chunks, scores):
            exponent = jnp.exp2((part - top) * factor)
            exponents.append(exponent)
            total = total + jnp.sum(exponent, axis=0, keepdims=True)
            if queries is not None:
                upcoming.append(score(index + 1, chunk, queries))
        inverse = 1.0 / total
        result = 0.0
        rows = slice(index * head, (index + 1) * head)
        for chunk, exponent in zip(chunks, exponents):
            result = result + jnp.dot(
                values[rows, within(chunk)],
                (exponent * inverse).astype(jnp.bfloat16),
                preferred_element_type=jnp.float32,
            )
        for i, here in enumerate(pair_of(out, index)):
            out[here, :] = result[:, i * tile : (i + 1) * tile].astype(jnp.bfloat16)
        scores = upcoming


def attend(block, index, queries, keys, values, earlier):
    _, width, tokens = queries.shape
    tile = tokens // 2
    band = min(WINDOW_LENGTH + tile, keys.shape[0])
    return pl.pallas_call(
        functools.partial(attend_kernel, band, float(MODEL_WIDTH // QUERY_HEAD_COUNT) ** (-0.5)),
        grid_spec=pltpu.PrefetchScalarGridSpec(
            num_scalar_prefetch=1,
            grid=(2,),
            in_specs=[
                pl.BlockSpec((1, width, tile), lambda t, *_: (index, 0, t)),
                whole(keys.shape),
                whole(values.shape),
            ]
            + [ANYWHERE] * len(earlier),
            out_specs=pl.BlockSpec((width, tile), lambda t, *_: (0, t)),
            scratch_shapes=[pltpu.VMEM((band, 2 * tile), jnp.float32)],
        ),
        out_shape=jax.ShapeDtypeStruct((width, tokens), jnp.bfloat16),
        compiler_params=pltpu.CompilerParams(vmem_limit_bytes=VMEM_BYTES),
        cost_estimate=pl.CostEstimate(
            flops=4 * tokens * band * width,
            bytes_accessed=4 * tokens * width + 4 * keys.shape[0] * keys.shape[1],
            transcendentals=tokens * band * (width // 128),
        ),
    )(block[None], queries, keys, values, *earlier)


def output_kernel(count, full, table, *refs):
    parts, pieces, (out, squares, held, row_held) = refs[:8], refs[8 : 8 + count], refs[8 + count :]
    depth = parts[0].shape[0]
    step = pl.program_id(0)

    @pl.when(step == 0)
    def _():
        for index, part in enumerate(parts):
            held[index * depth : (index + 1) * depth, :] = part[...]
        squares[...] = jnp.zeros_like(squares)

    for index, piece in enumerate(pieces):

        @pl.when(table[index] < full)
        def _(index=index, piece=piece):
            there = pl.ds(pl.multiple_of(table[index], 128), piece.shape[1])
            row_held[:, there] = piece[...]

    product = jnp.dot(row_held[...], held[...], preferred_element_type=jnp.float32)
    out[...] = product
    squares[...] += jnp.sum(jnp.square(product), axis=0, keepdims=True)


def output_product(table, parts, pieces):
    depth, tokens = parts[0].shape
    width = pieces[0][0].shape[0]
    full = 8 * depth
    tile = width // 4

    def rows(index, column, columns):
        return pl.BlockSpec(
            (tile, columns), lambda t, table: (jnp.where(table[index] < full, t, 0), column)
        )

    return pl.pallas_call(
        functools.partial(output_kernel, len(pieces), full),
        grid_spec=pltpu.PrefetchScalarGridSpec(
            num_scalar_prefetch=1,
            grid=(width // tile,),
            in_specs=[whole((depth, tokens))] * 8
            + [rows(index, column, columns) for index, (_, column, columns) in enumerate(pieces)],
            out_specs=[pl.BlockSpec((tile, tokens), lambda t, *_: (t, 0)), whole((1, tokens))],
            scratch_shapes=[
                pltpu.VMEM((full, tokens), jnp.bfloat16),
                pltpu.VMEM((tile, full), jnp.bfloat16),
            ],
        ),
        out_shape=[
            jax.ShapeDtypeStruct((width, tokens), jnp.float32),
            jax.ShapeDtypeStruct((1, tokens), jnp.float32),
        ],
        compiler_params=pltpu.CompilerParams(vmem_limit_bytes=VMEM_BYTES),
        cost_estimate=pl.CostEstimate(
            flops=2 * tokens * full * width,
            bytes_accessed=2 * full * (tokens + width) + 4 * tokens * width,
            transcendentals=0,
        ),
    )(table, *parts, *(piece for piece, _, _ in pieces))


def middle_form(
    stream_in,
    in_gain,
    query_weight,
    key_matrix,
    value_matrix,
    query_gain,
    key_norm_gain,
    output_weight,
    post_gain,
):
    stream = stream_in.T
    features, tokens = stream.shape
    head = query_gain.shape[0]
    row = lax.axis_index("row")
    group = lax.axis_index("groups")
    place = lax.axis_index("col") * 2 + lax.axis_index("sub")
    upper = (row >= 2).astype(jnp.int32)
    in_middle = (row == 1) | (row == 2)
    near_block, cross_block, far_block = 3 * upper, 3 - row, 3 - 3 * upper
    blocks = (row, near_block, cross_block, far_block)
    slot = lambda block: jnp.bitwise_xor(place, block)
    ints = lambda *values: jnp.stack([jnp.asarray(v, jnp.int32) for v in values])
    everywhere = MIDDLE + ENDS
    inward = [(0, 1), (3, 2)]
    across = [(1, 2), (2, 1)]
    outward = [(1, 0), (2, 3)]

    half = query_weight.shape[1] // 2
    quarter = key_matrix.shape[1] // 2

    def side(which):
        queries = lax.dynamic_slice_in_dim(query_weight, which * half, half, axis=1)
        keys = lax.dynamic_slice_in_dim(key_matrix, which * quarter, quarter, axis=1)
        values = lax.dynamic_slice_in_dim(value_matrix, which * quarter, quarter, axis=1)
        return queries, jnp.concatenate([keys, values], axis=1)

    own_queries, own_pairs = side(upper)
    own_side = jnp.where(group == 0, own_queries, own_pairs)
    other_side = jnp.where(group == 0, *side(1 - upper))
    turned = output_weight.T
    depth = turned.shape[1] // 2
    mine = lax.dynamic_slice_in_dim(turned, group * depth, depth, axis=1)
    theirs = lax.dynamic_slice_in_dim(turned, (1 - group) * depth, depth, axis=1)

    gain_rows = in_gain.reshape(4, features)
    gain = jnp.concatenate(
        [lax.dynamic_slice_in_dim(gain_rows, slot(j), 1, axis=0) for j in range(4)], axis=0
    )[:, :, None]
    arrival = lambda block: jnp.where(
        block == row, 0, jnp.where(block == near_block, 1, jnp.where(block == far_block, 2, 3))
    )
    order = ints(*(arrival(slot(j)) for j in range(4)))

    x_cross = lax.ppermute(stream, "row", across)
    x_near = lax.ppermute(stream, "row", inward)
    own_col = swapped(stream, "col", MIDDLE)
    own_sub = swapped(stream, "sub", MIDDLE)
    x_cross, x_near, own_col, own_sub, own_side, other_side, mine = settle(
        x_cross, x_near, own_col, own_sub, own_side, other_side, mine
    )

    x_far = lax.ppermute(x_near, "row", across)
    w_near = lax.ppermute(own_side, "row", inward)
    x_pair = jnp.stack([x_near, x_cross])
    pair_col = swapped(x_pair, "col", MIDDLE)
    own_both = swapped(own_col, "sub", MIDDLE)
    pair_sub = swapped(x_pair, "sub", MIDDLE)
    own_pieces = (stream[None], own_sub[None], own_col[None], own_both[None])
    normed = norm_block(order, own_pieces, 0, gain, 0, None)
    x_far, w_near, other_side, mine, normed = settle(x_far, w_near, other_side, mine, normed)
    w_cross = lax.ppermute(other_side, "row", across)
    o_in = lax.ppermute(mine, "row", inward)
    w_near_y = swapped(w_near, "groups", MIDDLE)
    far_sub = swapped(x_far, "sub", MIDDLE)
    w_cross, o_in, w_near_y, pair_col, x_far, pair_sub, normed, other_side, turned, mine, theirs = settle(
        w_cross, o_in, w_near_y, pair_col, x_far, pair_sub, normed, other_side, turned, mine, theirs
    )

    w_far = lax.ppermute(other_side, "row", [(0, 2), (3, 1)])
    far_col = swapped(x_far, "col", MIDDLE)
    w_cross_y = swapped(w_cross, "groups", MIDDLE)
    pair_both = swapped(pair_col, "sub", MIDDLE)
    o_out = lax.ppermute(turned, "row", outward)
    pair_pieces = (x_pair, pair_sub, pair_col, pair_both)
    normed = norm_block(order, pair_pieces, 0, gain, 1, normed)
    normed = norm_block(order, pair_pieces, 1, gain, 2, normed)
    early_table = ints(0, 0, 0, half, features, group * half, features, (1 - group) * half)
    early_pieces = (own_queries, own_pairs, w_near, w_near_y)
    total = project_early(early_table, normed, early_pieces, 0, 3, None)
    w_far, far_col, w_cross_y, total, mine, o_in, theirs = settle(
        w_far, far_col, w_cross_y, total, mine, o_in, theirs
    )

    cut = depth // 2
    w_far_y = swapped(w_far, "groups", MIDDLE)
    far_both = swapped(far_col, "sub", MIDDLE)
    o_cross = lax.ppermute(mine, "row", across)
    o_far_1 = lax.ppermute(o_in[:, :cut], "row", across)
    o_far_2 = lax.ppermute(o_in[:, cut:], "row", across)
    o_in_rest = lax.ppermute(theirs, "row", inward)
    far_pieces = (x_far[None], far_sub[None], far_col[None], far_both[None])
    normed = norm_block(order, far_pieces, 0, gain, 3, normed)
    total = project_early(early_table, normed, early_pieces, 3, 1, total)
    positions = jnp.arange(4 * tokens, dtype=jnp.int32).astype(jnp.float32)
    cosine, sine = rotary_tables(positions, head)
    here, there = group * half, (1 - group) * half
    queries, keys, values = project_late(
        ints(0, here, 0, there, features, here, features, there, *blocks),
        normed,
        (w_far, w_far_y, w_cross, w_cross_y),
        total,
        (query_gain[:, None], key_norm_gain[:, None], cosine.T, sine.T),
    )

    def attended(index, *earlier):
        return attend(blocks[index].astype(jnp.int32), index, queries, keys, values, earlier)

    queries, o_cross = settle(queries, o_cross)
    o_cross_y = swapped(o_cross, "groups", MIDDLE)
    o_end_cross = lax.ppermute(o_cross, "row", outward)
    cross_part = attended(2)
    to_cross = lax.ppermute(cross_part, "row", across)
    far_part = attended(3, cross_part)
    to_far = lax.ppermute(far_part, "row", [(1, 3), (2, 0)])
    near_part = attended(1, far_part, o_far_1)
    to_near = lax.ppermute(near_part, "row", outward)
    o_far_1_y = swapped(after(o_far_1, near_part), "groups", MIDDLE)
    o_end_far_1 = lax.ppermute(after(o_far_1, near_part), "row", outward)
    own_part = attended(0, near_part, o_far_2, o_cross_y, to_cross)
    o_far_2_y = swapped(after(o_far_2, own_part), "groups", MIDDLE)
    o_end_far_2 = lax.ppermute(after(o_far_2, own_part), "row", outward)
    this_side = jnp.where(in_middle, own_part, to_near)
    this_across = swapped(this_side, "col", everywhere)
    that_side = jnp.where(in_middle, to_cross, to_far)
    that_across = swapped(that_side, "col", everywhere)
    o_end_cross_y = swapped(after(o_end_cross, own_part), "groups", ENDS)
    o_end_far_1_y = swapped(after(o_end_far_1, this_side), "groups", ENDS)
    o_end_far_2_y = swapped(o_end_far_2, "groups", ENDS)
    o_far, o_far_y = (o_far_1, o_far_2), (o_far_1_y, o_far_2_y)
    o_end_far, o_end_far_y = (o_end_far_1, o_end_far_2), (o_end_far_1_y, o_end_far_2_y)

    pair_block = jnp.bitwise_xor(row, 1)
    out_pieces, out_table = [], []

    def put(piece, column, columns, block, which, offset, here):
        spot = (2 * slot(block) + jnp.bitwise_xor(which, upper)) * depth + offset
        out_pieces.append((piece, column, columns))
        out_table.append(spot if here is None else jnp.where(here, spot, 8 * depth))

    for part in range(2):
        put(turned, part, depth, row, part, 0, None)
        put(o_out, part, depth, pair_block, part, 0, ~in_middle)
    put(o_in, 0, depth, pair_block, group, 0, in_middle)
    put(o_in_rest, 0, depth, pair_block, 1 - group, 0, in_middle)
    put(o_cross, 0, depth, 3 - row, group, 0, in_middle)
    put(o_cross_y, 0, depth, 3 - row, 1 - group, 0, in_middle)
    put(o_end_cross, 0, depth, 3 - pair_block, group, 0, ~in_middle)
    put(o_end_cross_y, 0, depth, 3 - pair_block, 1 - group, 0, ~in_middle)
    for index, (piece, piece_y, end_piece, end_piece_y) in enumerate(
        zip(o_far, o_far_y, o_end_far, o_end_far_y)
    ):
        put(piece, 0, cut, 3 - pair_block, group, index * cut, in_middle)
        put(piece_y, 0, cut, 3 - pair_block, 1 - group, index * cut, in_middle)
        put(end_piece, 0, cut, 3 - row, group, index * cut, ~in_middle)
        put(end_piece_y, 0, cut, 3 - row, 1 - group, index * cut, ~in_middle)

    parts = (
        this_side,
        that_side,
        swapped(this_side, "sub", everywhere),
        swapped(that_side, "sub", everywhere),
        this_across,
        that_across,
        swapped(this_across, "sub", everywhere),
        swapped(that_across, "sub", everywhere),
    )
    branch, squares = output_product(ints(*out_table), parts, out_pieces)
    squares = squares + swapped(squares, "sub", everywhere)
    squares = squares + swapped(squares, "col", everywhere)
    scaled = branch * lax.rsqrt(squares / MODEL_WIDTH + EPSILON) * post_gain[:, None]
    return (stream.astype(jnp.float32) + scaled).astype(jnp.bfloat16).T


def on_device(*args):
    stream_in, _, query_weight, key_matrix, value_matrix, query_gain, *_ = args
    sizes = tuple(lax.axis_size(name) for name in ("groups", "row", "col", "sub"))
    tokens, head = stream_in.shape[0], query_gain.shape[0]
    fits = (
        sizes == (2, 4, 2, 2)
        and head == 128
        and tokens % 256 == 0
        and key_matrix.shape[1] % (2 * head) == 0
        and query_weight.shape[1] == 2 * key_matrix.shape[1]
        and value_matrix.shape[1] == key_matrix.shape[1]
    )
    return middle_form(*args) if fits else general_form(*args)


def solution(mesh):
    placed = (
        P(("groups", "row"), ("col", "sub")),
        P(),
        P("row", ("col", "sub")),
        P("row", ("col", "sub")),
        P("row", ("col", "sub")),
        P(),
        P(),
        P("row", ("col", "sub")),
        P(("col", "sub")),
    )
    return jax.shard_map(
        on_device,
        mesh=mesh,
        in_specs=placed,
        out_specs=P(("groups", "row"), ("col", "sub")),
        check_vma=False,
    )
```

```python
import functools

import jax
import jax.numpy as jnp
from jax import lax
from jax.experimental import pallas as pl
from jax.experimental.pallas import tpu as pltpu
from jax.sharding import PartitionSpec as P

MODEL_WIDTH = 5376
QUERY_HEAD_COUNT = 32
WINDOW_LENGTH = 1024


EPSILON = 1e-06
VMEM_BYTES = 60 * 1024 * 1024


def shifted(x, axis, by):
    count = lax.axis_size(axis)
    pairs = [(i, i + by) for i in range(count) if 0 <= i + by < count]
    return lax.ppermute(x, axis, pairs)


def root_mean_scale(values, gain):
    return values * lax.rsqrt(jnp.mean(values * values, axis=-1, keepdims=True) + EPSILON) * gain


def rotary_tables(token_positions, size):
    half_dim = size // 2
    inverse = 10000.0 ** (-(jnp.arange(half_dim, dtype=jnp.float32) * 2.0) / size)
    angles = token_positions[:, None] * inverse[None, :]
    return jnp.cos(angles), jnp.sin(angles)


def apply_rotary(tensor, token_positions):
    half_dim = tensor.shape[-1] // 2
    cosine, sine_part = rotary_tables(token_positions, tensor.shape[-1])
    cosine, sine_part = cosine[:, None, :], sine_part[:, None, :]
    first_half = tensor[..., :half_dim]
    second_half = tensor[..., half_dim:]
    return jnp.concatenate(
        [
            first_half * cosine - second_half * sine_part,
            second_half * cosine + first_half * sine_part,
        ],
        axis=-1,
    )


def general_form(
    stream_in,
    in_gain,
    query_weight,
    key_matrix,
    value_matrix,
    query_gain,
    key_norm_gain,
    output_weight,
    post_gain,
):
    token_rows = lax.all_gather(stream_in, ("col", "sub"), axis=1, tiled=True)
    tokens = token_rows.shape[0]
    normed = root_mean_scale(token_rows.astype(jnp.float32), in_gain).astype(jnp.bfloat16)

    def add_panel(panel_piece):
        return jnp.dot(normed, panel_piece, preferred_element_type=jnp.float32)

    query_proj = add_panel(lax.all_gather(query_weight, "row", axis=0, tiled=True))
    projected_keys = add_panel(lax.all_gather(key_matrix, "row", axis=0, tiled=True))
    projected_values = add_panel(lax.all_gather(value_matrix, "row", axis=0, tiled=True))
    head_size = query_gain.shape[0]
    query_heads = query_weight.shape[1] // head_size
    pair_heads = key_matrix.shape[1] // head_size
    group_count = query_heads // pair_heads
    scale_factor = float(MODEL_WIDTH // QUERY_HEAD_COUNT) ** (-0.5)
    row_index = lax.axis_index("row")
    query_places = row_index * tokens + jnp.arange(tokens, dtype=jnp.int32)
    query_rot = apply_rotary(
        root_mean_scale(query_proj.reshape(tokens, query_heads, head_size), query_gain),
        query_places.astype(jnp.float32),
    ).astype(jnp.bfloat16)
    rotary_keys = apply_rotary(
        root_mean_scale(projected_keys.reshape(tokens, pair_heads, head_size), key_norm_gain),
        query_places.astype(jnp.float32),
    ).astype(jnp.bfloat16)
    keys_flat = rotary_keys.reshape(tokens, pair_heads * head_size)
    values_flat = projected_values.astype(jnp.bfloat16)
    shards_back = min(WINDOW_LENGTH // tokens, lax.axis_size("row") - 1)
    band_length = (shards_back + 1) * tokens
    key_parts = [keys_flat]
    value_parts = [values_flat]
    for offset in range(1, shards_back + 1):
        keys_prior, values_prior = shifted((keys_flat, values_flat), "row", offset)
        key_parts = [keys_prior] + key_parts
        value_parts = [values_prior] + value_parts
    keys_band = jnp.concatenate(key_parts, axis=0)
    values_band = jnp.concatenate(value_parts, axis=0)
    key_places = (row_index - shards_back) * tokens + jnp.arange(band_length, dtype=jnp.int32)
    distance = query_places[:, None] - key_places[None, :]
    visible = (distance >= 0) & (distance < WINDOW_LENGTH) & (key_places[None, :] >= 0)
    grouped = query_rot.reshape(tokens, pair_heads, group_count, head_size)
    scores = (
        jnp.einsum(
            "qhgd,shd->hgqs",
            grouped,
            keys_band.reshape(band_length, pair_heads, head_size),
            preferred_element_type=jnp.float32,
        )
        * scale_factor
    )
    scores = jnp.where(visible, scores, -1e30)
    row_max = jnp.max(scores, axis=-1, keepdims=True)
    exponent = jnp.exp(scores - row_max)
    weights = (exponent / jnp.sum(exponent, axis=-1, keepdims=True)).astype(jnp.bfloat16)
    attended = jnp.einsum(
        "hgqs,shd->qhgd",
        weights,
        values_band.reshape(band_length, pair_heads, head_size),
        preferred_element_type=jnp.float32,
    )
    heads_out = attended.reshape(tokens, query_heads * head_size).astype(jnp.bfloat16)
    head_rows = lax.all_gather(heads_out, ("col", "sub"), axis=1, tiled=True)
    branch = jnp.dot(
        head_rows,
        lax.all_gather(output_weight, "row", axis=0, tiled=True),
        preferred_element_type=jnp.float32,
    )
    squares = lax.psum(jnp.sum(branch * branch, axis=-1), ("col", "sub"))
    scaled = branch * lax.rsqrt(squares[:, None] / MODEL_WIDTH + EPSILON) * post_gain
    return (stream_in.astype(jnp.float32) + scaled).astype(jnp.bfloat16)


def swapped(x, axis, rows=None):
    if rows is None:
        return lax.ppermute(x, axis, [(0, 1), (1, 0)])
    count = lax.axis_size("row")
    pairs = [(count * i + r, count * (1 - i) + r) for r in rows for i in range(2)]
    return lax.ppermute(x, ("groups", "row"), pairs)


def after(x, *earlier):
    return lax.optimization_barrier((x, *earlier))[0]


def settle(*values):
    return lax.optimization_barrier(values)


def whole(shape):
    return pl.BlockSpec(shape, lambda *_: (0,) * len(shape))


ANYWHERE = pl.BlockSpec(memory_space=pl.ANY)
LITTLE = pl.CostEstimate(flops=0, bytes_accessed=0, transcendentals=0)


def norm_kernel(table, *refs):
    *pieces, gain, out = refs[-6:]
    depth = pieces[0].shape[1]
    squares = sum(
        jnp.sum(jnp.square(p[0].astype(jnp.float32)), axis=0, keepdims=True) for p in pieces
    )
    scale = lax.rsqrt(squares / MODEL_WIDTH + EPSILON)
    for index, piece in enumerate(pieces):
        rows = pl.ds(pl.multiple_of(table[index] * depth, depth), depth)
        out[0, rows, :] = (piece[0].astype(jnp.float32) * scale * gain[index]).astype(jnp.bfloat16)


def norm_block(table, pieces, which, gain, index, held):
    _, depth, tokens = pieces[0].shape
    lanes = tokens // 2
    shape = (4, 4 * depth, tokens)
    before = () if held is None else (held,)
    return pl.pallas_call(
        norm_kernel,
        grid_spec=pltpu.PrefetchScalarGridSpec(
            num_scalar_prefetch=1,
            grid=(tokens // lanes,),
            in_specs=[ANYWHERE] * len(before)
            + [pl.BlockSpec((1, depth, lanes), lambda t, *_: (which, 0, t))] * 4
            + [whole((4, depth, 1))],
            out_specs=pl.BlockSpec((1, 4 * depth, lanes), lambda t, *_: (index, 0, t)),
        ),
        out_shape=jax.ShapeDtypeStruct(shape, jnp.bfloat16),
        input_output_aliases={1: 0} if before else {},
        compiler_params=pltpu.CompilerParams(vmem_limit_bytes=VMEM_BYTES),
        cost_estimate=pl.CostEstimate(
            flops=40 * depth * tokens, bytes_accessed=16 * depth * tokens, transcendentals=0
        ),
    )(table, *before, *pieces, gain)


def order_pieces(table, pieces, ordered):
    base = 0
    for index, piece in enumerate(pieces):
        depth, width = piece.shape
        rows = pl.ds(pl.multiple_of(table[2 * index], 16), depth)
        columns = pl.ds(pl.multiple_of(table[2 * index + 1], width), width)
        ordered[rows, columns] = piece[...]


def project_early_kernel(count, table, normed, *refs):
    pieces, out, ordered = refs[:count], refs[-2], refs[-1]

    @pl.when(pl.program_id(0) == 0)
    def _():
        order_pieces(table, pieces, ordered)

    out[0] = lax.dot_general(
        ordered[...], normed[0], (((0,), (0,)), ((), ())), preferred_element_type=jnp.float32
    )


def project_early(table, normed, pieces, first, blocks, held):
    _, features, tokens = normed.shape
    width = 2 * pieces[0].shape[1]
    before = () if held is None else (held,)
    return pl.pallas_call(
        functools.partial(project_early_kernel, len(pieces)),
        grid_spec=pltpu.PrefetchScalarGridSpec(
            num_scalar_prefetch=1,
            grid=(blocks,),
            in_specs=[pl.BlockSpec((1, features // 2, tokens), lambda i, t: (first + i, 0, 0))]
            + [whole(p.shape) for p in pieces]
            + [ANYWHERE] * len(before),
            out_specs=pl.BlockSpec((1, width, tokens), lambda i, t: (first + i, 0, 0)),
            scratch_shapes=[pltpu.VMEM((features // 2, width), jnp.bfloat16)],
        ),
        out_shape=jax.ShapeDtypeStruct((4, width, tokens), jnp.float32),
        input_output_aliases={2 + len(pieces): 0} if before else {},
        compiler_params=pltpu.CompilerParams(vmem_limit_bytes=VMEM_BYTES),
        cost_estimate=pl.CostEstimate(
            flops=2 * blocks * tokens * features // 2 * width,
            bytes_accessed=blocks * features * tokens + features * width + 4 * blocks * width * tokens,
            transcendentals=0,
        ),
    )(table, normed, *pieces, *before)


def project_late_kernel(count, table, normed, *refs):
    pieces, refs = refs[:count], refs[count:]
    early, q_gain, k_gain, cosine, sine, q_out, k_out, v_out, total, ordered = refs

    @pl.when(pl.program_id(0) == 0)
    def _():
        order_pieces(table, pieces, ordered)

    total[...] = early[0] + lax.dot_general(
        ordered[...], normed[0], (((0,), (0,)), ((), ())), preferred_element_type=jnp.float32
    )
    head = q_gain.shape[0]
    half = head // 2
    width = q_out.shape[1]
    cos, sin = cosine[...], sine[...]

    def rotated(start, head_gain):
        values = total[start : start + head, :]
        values = (
            values
            * lax.rsqrt(jnp.mean(values * values, axis=0, keepdims=True) + EPSILON)
            * head_gain[:, :1]
        )
        first, second = values[:half], values[half:]
        return jnp.concatenate(
            [first * cos - second * sin, second * cos + first * sin], axis=0
        ).astype(jnp.bfloat16)

    for start in range(0, width, head):
        q_out[0, start : start + head, :] = rotated(start, q_gain)
    for start in range(0, width // 2, head):
        k_out[:, start : start + head] = rotated(width + start, k_gain).T
    v_out[...] = total[width + width // 2 :, :].astype(jnp.bfloat16)


def project_late(table, normed, pieces, early, extras):
    blocks, features, tokens = normed.shape
    width = early.shape[1] // 2
    head = extras[0].shape[0]
    half = head // 2
    count = len(pieces)
    turn = pl.BlockSpec((half, tokens), lambda i, t: (0, t[2 * count + i]))
    return pl.pallas_call(
        functools.partial(project_late_kernel, count),
        grid_spec=pltpu.PrefetchScalarGridSpec(
            num_scalar_prefetch=1,
            grid=(blocks,),
            in_specs=[pl.BlockSpec((1, features // 2, tokens), lambda i, t: (i, 1, 0))]
            + [whole(p.shape) for p in pieces]
            + [
                pl.BlockSpec((1, 2 * width, tokens), lambda i, t: (i, 0, 0)),
                whole((head, head)),
                whole((head, head)),
                turn,
                turn,
            ],
            out_specs=[
                pl.BlockSpec((1, width, tokens), lambda i, t: (i, 0, 0)),
                pl.BlockSpec((tokens, width // 2), lambda i, t: (t[2 * count + i], 0)),
                pl.BlockSpec((width // 2, tokens), lambda i, t: (0, t[2 * count + i])),
            ],
            scratch_shapes=[
                pltpu.VMEM((2 * width, tokens), jnp.float32),
                pltpu.VMEM((features // 2, 2 * width), jnp.bfloat16),
            ],
        ),
        out_shape=[
            jax.ShapeDtypeStruct((blocks, width, tokens), jnp.bfloat16),
            jax.ShapeDtypeStruct((blocks * tokens, width // 2), jnp.bfloat16),
            jax.ShapeDtypeStruct((width // 2, blocks * tokens), jnp.bfloat16),
        ],
        compiler_params=pltpu.CompilerParams(vmem_limit_bytes=VMEM_BYTES),
        cost_estimate=LITTLE,
    )(table, normed, *pieces, early, *extras)


def attend_kernel(band, scale, table, q_ref, keys, values, *refs):
    out, mask = refs[-2:]
    head = 128
    tile = out.shape[1]
    first = table[0] * (2 * tile) + pl.program_id(0) * tile
    start = pl.multiple_of(jnp.clip(first + tile - band, 0, keys.shape[0] - band), tile)
    places = lax.broadcasted_iota(jnp.int32, (band, tile), 1)
    distance = (first - start) + places - lax.broadcasted_iota(jnp.int32, (band, tile), 0)
    hidden = jnp.where((distance >= 0) & (distance < WINDOW_LENGTH), 0.0, -1e30)
    mask[:, :tile] = hidden
    mask[:, tile:] = hidden
    pairs = keys.shape[1] // head
    factor = scale * 1.4426950408889634
    chunks = [slice(a, min(a + tile, band)) for a in range(0, band, tile)]

    def pair_of(ref, index):
        return [slice((2 * index + i) * head, (2 * index + i + 1) * head) for i in range(2)]

    def query(index):
        return jnp.concatenate([q_ref[0, rows, :] for rows in pair_of(q_ref, index)], axis=1)

    def within(chunk):
        return pl.ds(pl.multiple_of(start + chunk.start, tile), chunk.stop - chunk.start)

    def score(index, chunk, queries):
        columns = slice(index * head, (index + 1) * head)
        return mask[chunk, :] + jnp.dot(
            keys[within(chunk), columns], queries, preferred_element_type=jnp.float32
        )

    queries = query(0)
    scores = [score(0, chunk, queries) for chunk in chunks]
    for index in range(pairs):
        top = functools.reduce(
            jnp.maximum, [jnp.max(part, axis=0, keepdims=True) for part in scores]
        )
        queries = query(index + 1) if index + 1 < pairs else None
        exponents, upcoming, total = [], [], 0.0
        for chunk, part in zip(chunks, scores):
            exponent = jnp.exp2((part - top) * factor)
            exponents.append(exponent)
            total = total + jnp.sum(exponent, axis=0, keepdims=True)
            if queries is not None:
                upcoming.append(score(index + 1, chunk, queries))
        inverse = 1.0 / total
        result = 0.0
        rows = slice(index * head, (index + 1) * head)
        for chunk, exponent in zip(chunks, exponents):
            result = result + jnp.dot(
                values[rows, within(chunk)],
                (exponent * inverse).astype(jnp.bfloat16),
                preferred_element_type=jnp.float32,
            )
        for i, here in enumerate(pair_of(out, index)):
            out[here, :] = result[:, i * tile : (i + 1) * tile].astype(jnp.bfloat16)
        scores = upcoming


def attend(block, index, queries, keys, values, earlier):
    _, width, tokens = queries.shape
    tile = tokens // 2
    band = min(WINDOW_LENGTH + tile, keys.shape[0])
    return pl.pallas_call(
        functools.partial(attend_kernel, band, float(MODEL_WIDTH // QUERY_HEAD_COUNT) ** (-0.5)),
        grid_spec=pltpu.PrefetchScalarGridSpec(
            num_scalar_prefetch=1,
            grid=(2,),
            in_specs=[
                pl.BlockSpec((1, width, tile), lambda t, *_: (index, 0, t)),
                whole(keys.shape),
                whole(values.shape),
            ]
            + [ANYWHERE] * len(earlier),
            out_specs=pl.BlockSpec((width, tile), lambda t, *_: (0, t)),
            scratch_shapes=[pltpu.VMEM((band, 2 * tile), jnp.float32)],
        ),
        out_shape=jax.ShapeDtypeStruct((width, tokens), jnp.bfloat16),
        compiler_params=pltpu.CompilerParams(vmem_limit_bytes=VMEM_BYTES),
        cost_estimate=LITTLE,
    )(block[None], queries, keys, values, *earlier)


def output_kernel(count, full, table, *refs):
    parts, pieces, (out, squares, held, row_held) = refs[:8], refs[8 : 8 + count], refs[8 + count :]
    depth = parts[0].shape[0]
    step = pl.program_id(0)

    @pl.when(step == 0)
    def _():
        for index, part in enumerate(parts):
            held[index * depth : (index + 1) * depth, :] = part[...]
        squares[...] = jnp.zeros_like(squares)

    for index, piece in enumerate(pieces):

        @pl.when(table[index] < full)
        def _(index=index, piece=piece):
            there = pl.ds(pl.multiple_of(table[index], 128), piece.shape[1])
            row_held[:, there] = piece[...]

    product = jnp.dot(row_held[...], held[...], preferred_element_type=jnp.float32)
    out[...] = product
    squares[...] += jnp.sum(jnp.square(product), axis=0, keepdims=True)


def output_product(table, parts, pieces):
    depth, tokens = parts[0].shape
    width = pieces[0][0].shape[0]
    full = 8 * depth
    tile = width // 4

    def rows(index, column, columns):
        return pl.BlockSpec(
            (tile, columns), lambda t, table: (jnp.where(table[index] < full, t, 0), column)
        )

    return pl.pallas_call(
        functools.partial(output_kernel, len(pieces), full),
        grid_spec=pltpu.PrefetchScalarGridSpec(
            num_scalar_prefetch=1,
            grid=(width // tile,),
            in_specs=[whole((depth, tokens))] * 8
            + [rows(index, column, columns) for index, (_, column, columns) in enumerate(pieces)],
            out_specs=[pl.BlockSpec((tile, tokens), lambda t, *_: (t, 0)), whole((1, tokens))],
            scratch_shapes=[
                pltpu.VMEM((full, tokens), jnp.bfloat16),
                pltpu.VMEM((tile, full), jnp.bfloat16),
            ],
        ),
        out_shape=[
            jax.ShapeDtypeStruct((width, tokens), jnp.float32),
            jax.ShapeDtypeStruct((1, tokens), jnp.float32),
        ],
        compiler_params=pltpu.CompilerParams(vmem_limit_bytes=VMEM_BYTES),
        cost_estimate=pl.CostEstimate(
            flops=2 * tokens * full * width,
            bytes_accessed=2 * full * (tokens + width) + 4 * tokens * width,
            transcendentals=0,
        ),
    )(table, *parts, *(piece for piece, _, _ in pieces))


def middle_form(
    stream_in,
    in_gain,
    query_weight,
    key_matrix,
    value_matrix,
    query_gain,
    key_norm_gain,
    output_weight,
    post_gain,
):
    stream = stream_in.T
    features, tokens = stream.shape
    head = query_gain.shape[0]
    row = lax.axis_index("row")
    group = lax.axis_index("groups")
    place = lax.axis_index("col") * 2 + lax.axis_index("sub")
    upper = (row >= 2).astype(jnp.int32)
    in_middle = (row == 1) | (row == 2)
    near_block, cross_block, far_block = 3 * upper, 3 - row, 3 - 3 * upper
    blocks = (row, near_block, cross_block, far_block)
    slot = lambda block: jnp.bitwise_xor(place, block)
    ints = lambda *values: jnp.stack([jnp.asarray(v, jnp.int32) for v in values])
    beside = [(0, 1), (1, 0), (2, 3), (3, 2)]
    across = [(1, 2), (2, 1)]
    beyond = [(0, 2), (1, 0), (2, 3), (3, 1)]
    outside = [(1, 3), (2, 0)]
    outward = [(1, 0), (2, 3)]
    middles, ends = (1, 2), (0, 3)

    half = query_weight.shape[1] // 2
    quarter = key_matrix.shape[1] // 2

    def side(which):
        queries = lax.dynamic_slice_in_dim(query_weight, which * half, half, axis=1)
        keys = lax.dynamic_slice_in_dim(key_matrix, which * quarter, quarter, axis=1)
        values = lax.dynamic_slice_in_dim(value_matrix, which * quarter, quarter, axis=1)
        return queries, jnp.concatenate([keys, values], axis=1)

    own_queries, own_pairs = side(upper)
    own_side = jnp.where(group == 0, own_queries, own_pairs)
    other_side = jnp.where(group == 0, *side(1 - upper))
    turned = output_weight.T
    depth = turned.shape[1] // 2
    mine = lax.dynamic_slice_in_dim(turned, group * depth, depth, axis=1)
    theirs = lax.dynamic_slice_in_dim(turned, (1 - group) * depth, depth, axis=1)

    gain_rows = in_gain.reshape(4, features)
    gain = jnp.concatenate(
        [lax.dynamic_slice_in_dim(gain_rows, slot(j), 1, axis=0) for j in range(4)], axis=0
    )[:, :, None]
    arrival = lambda block: jnp.where(
        block == row, 0, jnp.where(block == near_block, 1, jnp.where(block == far_block, 2, 3))
    )
    order = ints(*(arrival(slot(j)) for j in range(4)))

    positions = jnp.arange(4 * tokens, dtype=jnp.int32).astype(jnp.float32)
    cosine, sine = rotary_tables(positions, head)
    spread = lambda gains: jnp.broadcast_to(gains[:, None], (head, head))
    tables = (spread(query_gain), spread(key_norm_gain), cosine.T, sine.T)

    x_cross = lax.ppermute(stream, "row", across)
    x_near = lax.ppermute(stream, "row", beside)
    own_col = swapped(stream, "col")
    own_sub = swapped(stream, "sub")
    x_cross, x_near, own_col, own_side, other_side, mine, *tables = settle(
        x_cross, x_near, own_col, own_side, other_side, mine, *tables
    )

    x_far = lax.ppermute(x_near, "row", across)
    w_near = lax.ppermute(own_side, "row", beside)
    near_col = swapped(x_near, "col")
    own_both = swapped(own_col, "sub")
    near_sub = swapped(x_near, "sub")
    own_pieces = (stream[None], own_sub[None], own_col[None], own_both[None])
    normed = norm_block(order, own_pieces, 0, gain, 0, None)
    x_far, w_near, near_col, other_side, mine, normed, x_cross = settle(
        x_far, w_near, near_col, other_side, mine, normed, x_cross
    )
    w_cross = lax.ppermute(other_side, "row", across)
    cross_col = swapped(x_cross, "col")
    o_in = lax.ppermute(mine, "row", beside)
    w_near_y = swapped(w_near, "groups")
    near_both = swapped(near_col, "sub")
    cross_sub = swapped(x_cross, "sub")
    far_sub = swapped(x_far, "sub")
    near_pieces = (x_near[None], near_sub[None], near_col[None], near_both[None])
    normed = norm_block(order, near_pieces, 0, gain, 1, normed)
    w_cross, o_in, w_near_y, cross_col, x_far, normed, other_side, theirs, cross_sub = settle(
        w_cross, o_in, w_near_y, cross_col, x_far, normed, other_side, theirs, cross_sub
    )

    w_far = lax.ppermute(other_side, "row", beyond)
    far_col = swapped(x_far, "col")
    cross_both = swapped(cross_col, "sub")
    w_cross_y = swapped(w_cross, "groups")
    cross_pieces = (x_cross[None], cross_sub[None], cross_col[None], cross_both[None])
    normed = norm_block(order, cross_pieces, 0, gain, 2, normed)
    early_table = ints(0, 0, 0, half, features, group * half, features, (1 - group) * half)
    early_pieces = (own_queries, own_pairs, w_near, w_near_y)
    total = project_early(early_table, normed, early_pieces, 0, 3, None)
    w_far, far_col, w_cross_y, total, o_in, theirs = settle(
        w_far, far_col, w_cross_y, total, o_in, theirs
    )

    w_far_y = swapped(w_far, "groups")
    far_both = swapped(far_col, "sub")
    o_far = lax.ppermute(o_in, "row", across)
    o_in_rest = lax.ppermute(theirs, "row", beside)
    far_pieces = (x_far[None], far_sub[None], far_col[None], far_both[None])
    normed = norm_block(order, far_pieces, 0, gain, 3, normed)
    total = project_early(early_table, normed, early_pieces, 3, 1, total)
    w_far_y, o_far, total, o_in_rest = settle(w_far_y, o_far, total, o_in_rest)
    o_end_far = lax.ppermute(o_far, "row", outward)
    o_cross = lax.ppermute(mine, "row", across)
    o_far_y = swapped(o_far, "groups", middles)
    here, there = group * half, (1 - group) * half
    queries, keys, values = project_late(
        ints(0, here, 0, there, features, here, features, there, *blocks),
        normed,
        (w_far, w_far_y, w_cross, w_cross_y),
        total,
        tables,
    )

    def attended(index, *earlier):
        return attend(blocks[index].astype(jnp.int32), index, queries, keys, values, earlier)

    cross_part = attended(2)
    to_cross = lax.ppermute(cross_part, "row", across)
    shown, o_end_far, o_cross = settle(cross_part, o_end_far, o_cross)
    o_end_cross = lax.ppermute(o_cross, "row", outward)
    o_end_far_y = swapped(o_end_far, "groups", ends)
    o_cross_y = swapped(o_cross, "groups", middles)
    near_part = attended(1, shown)
    to_near = lax.ppermute(near_part, "row", outward)
    far_part = attended(3, near_part, o_far_y)
    to_far = lax.ppermute(far_part, "row", outside)
    own_part = attended(0, far_part, to_cross, o_end_far_y)
    this_side = jnp.where(in_middle, own_part, to_near)
    this_across = swapped(this_side, "col")
    that_side = jnp.where(in_middle, to_cross, after(to_far, own_part))
    that_across = swapped(that_side, "col")
    o_end_cross_y = swapped(after(o_end_cross, own_part), "groups", ends)

    pair_block = jnp.bitwise_xor(row, 1)
    out_pieces, out_table = [], []

    def put(piece, column, columns, block, which, offset, here):
        spot = (2 * slot(block) + jnp.bitwise_xor(which, upper)) * depth + offset
        out_pieces.append((piece, column, columns))
        out_table.append(spot if here is None else jnp.where(here, spot, 8 * depth))

    for part in range(2):
        put(turned, part, depth, row, part, 0, None)
    put(o_in, 0, depth, pair_block, group, 0, None)
    put(o_in_rest, 0, depth, pair_block, 1 - group, 0, None)
    put(o_far, 0, depth, 3 - pair_block, group, 0, in_middle)
    put(o_far_y, 0, depth, 3 - pair_block, 1 - group, 0, in_middle)
    put(o_end_far, 0, depth, 3 - row, group, 0, ~in_middle)
    put(o_end_far_y, 0, depth, 3 - row, 1 - group, 0, ~in_middle)
    put(o_cross, 0, depth, 3 - row, group, 0, in_middle)
    put(o_cross_y, 0, depth, 3 - row, 1 - group, 0, in_middle)
    put(o_end_cross, 0, depth, 3 - pair_block, group, 0, ~in_middle)
    put(o_end_cross_y, 0, depth, 3 - pair_block, 1 - group, 0, ~in_middle)

    parts = (
        this_side,
        that_side,
        swapped(this_side, "sub"),
        swapped(that_side, "sub"),
        this_across,
        that_across,
        swapped(this_across, "sub"),
        swapped(that_across, "sub"),
    )
    branch, squares = output_product(ints(*out_table), parts, out_pieces)
    squares = squares + swapped(squares, "sub")
    squares = squares + swapped(squares, "col")
    scaled = branch * lax.rsqrt(squares / MODEL_WIDTH + EPSILON) * post_gain[:, None]
    return (stream.astype(jnp.float32) + scaled).astype(jnp.bfloat16).T


def on_device(*args):
    stream_in, _, query_weight, key_matrix, value_matrix, query_gain, *_ = args
    sizes = tuple(lax.axis_size(name) for name in ("groups", "row", "col", "sub"))
    tokens, head = stream_in.shape[0], query_gain.shape[0]
    fits = (
        sizes == (2, 4, 2, 2)
        and head == 128
        and tokens % 256 == 0
        and key_matrix.shape[1] % (2 * head) == 0
        and query_weight.shape[1] == 2 * key_matrix.shape[1]
        and value_matrix.shape[1] == key_matrix.shape[1]
    )
    return middle_form(*args) if fits else general_form(*args)


def solution(mesh):
    placed = (
        P(("groups", "row"), ("col", "sub")),
        P(),
        P("row", ("col", "sub")),
        P("row", ("col", "sub")),
        P("row", ("col", "sub")),
        P(),
        P(),
        P("row", ("col", "sub")),
        P(("col", "sub")),
    )
    return jax.shard_map(
        on_device,
        mesh=mesh,
        in_specs=placed,
        out_specs=P(("groups", "row"), ("col", "sub")),
        check_vma=False,
    )
```

```python
import functools

import jax
import jax.numpy as jnp
from jax import lax
from jax.experimental import pallas as pl
from jax.experimental.pallas import tpu as pltpu
from jax.sharding import PartitionSpec as P

MODEL_WIDTH = 5376
QUERY_HEAD_COUNT = 32
WINDOW_LENGTH = 1024


EPSILON = 1e-06
VMEM_BYTES = 60 * 1024 * 1024


def shifted(x, axis, by):
    count = lax.axis_size(axis)
    pairs = [(i, i + by) for i in range(count) if 0 <= i + by < count]
    return lax.ppermute(x, axis, pairs)


def root_mean_scale(values, gain):
    return values * lax.rsqrt(jnp.mean(values * values, axis=-1, keepdims=True) + EPSILON) * gain


def rotary_tables(token_positions, size):
    half_dim = size // 2
    inverse = 10000.0 ** (-(jnp.arange(half_dim, dtype=jnp.float32) * 2.0) / size)
    angles = token_positions[:, None] * inverse[None, :]
    return jnp.cos(angles), jnp.sin(angles)


def apply_rotary(tensor, token_positions):
    half_dim = tensor.shape[-1] // 2
    cosine, sine_part = rotary_tables(token_positions, tensor.shape[-1])
    cosine, sine_part = cosine[:, None, :], sine_part[:, None, :]
    first_half = tensor[..., :half_dim]
    second_half = tensor[..., half_dim:]
    return jnp.concatenate(
        [
            first_half * cosine - second_half * sine_part,
            second_half * cosine + first_half * sine_part,
        ],
        axis=-1,
    )


def general_form(
    stream_in,
    in_gain,
    query_weight,
    key_matrix,
    value_matrix,
    query_gain,
    key_norm_gain,
    output_weight,
    post_gain,
):
    token_rows = lax.all_gather(stream_in, ("col", "sub"), axis=1, tiled=True)
    tokens = token_rows.shape[0]
    normed = root_mean_scale(token_rows.astype(jnp.float32), in_gain).astype(jnp.bfloat16)

    def add_panel(panel_piece):
        return jnp.dot(normed, panel_piece, preferred_element_type=jnp.float32)

    query_proj = add_panel(lax.all_gather(query_weight, "row", axis=0, tiled=True))
    projected_keys = add_panel(lax.all_gather(key_matrix, "row", axis=0, tiled=True))
    projected_values = add_panel(lax.all_gather(value_matrix, "row", axis=0, tiled=True))
    head_size = query_gain.shape[0]
    query_heads = query_weight.shape[1] // head_size
    pair_heads = key_matrix.shape[1] // head_size
    group_count = query_heads // pair_heads
    scale_factor = float(MODEL_WIDTH // QUERY_HEAD_COUNT) ** (-0.5)
    row_index = lax.axis_index("row")
    query_places = row_index * tokens + jnp.arange(tokens, dtype=jnp.int32)
    query_rot = apply_rotary(
        root_mean_scale(query_proj.reshape(tokens, query_heads, head_size), query_gain),
        query_places.astype(jnp.float32),
    ).astype(jnp.bfloat16)
    rotary_keys = apply_rotary(
        root_mean_scale(projected_keys.reshape(tokens, pair_heads, head_size), key_norm_gain),
        query_places.astype(jnp.float32),
    ).astype(jnp.bfloat16)
    keys_flat = rotary_keys.reshape(tokens, pair_heads * head_size)
    values_flat = projected_values.astype(jnp.bfloat16)
    shards_back = min(WINDOW_LENGTH // tokens, lax.axis_size("row") - 1)
    band_length = (shards_back + 1) * tokens
    key_parts = [keys_flat]
    value_parts = [values_flat]
    for offset in range(1, shards_back + 1):
        keys_prior, values_prior = shifted((keys_flat, values_flat), "row", offset)
        key_parts = [keys_prior] + key_parts
        value_parts = [values_prior] + value_parts
    keys_band = jnp.concatenate(key_parts, axis=0)
    values_band = jnp.concatenate(value_parts, axis=0)
    key_places = (row_index - shards_back) * tokens + jnp.arange(band_length, dtype=jnp.int32)
    distance = query_places[:, None] - key_places[None, :]
    visible = (distance >= 0) & (distance < WINDOW_LENGTH) & (key_places[None, :] >= 0)
    grouped = query_rot.reshape(tokens, pair_heads, group_count, head_size)
    scores = (
        jnp.einsum(
            "qhgd,shd->hgqs",
            grouped,
            keys_band.reshape(band_length, pair_heads, head_size),
            preferred_element_type=jnp.float32,
        )
        * scale_factor
    )
    scores = jnp.where(visible, scores, -1e30)
    row_max = jnp.max(scores, axis=-1, keepdims=True)
    exponent = jnp.exp(scores - row_max)
    weights = (exponent / jnp.sum(exponent, axis=-1, keepdims=True)).astype(jnp.bfloat16)
    attended = jnp.einsum(
        "hgqs,shd->qhgd",
        weights,
        values_band.reshape(band_length, pair_heads, head_size),
        preferred_element_type=jnp.float32,
    )
    heads_out = attended.reshape(tokens, query_heads * head_size).astype(jnp.bfloat16)
    head_rows = lax.all_gather(heads_out, ("col", "sub"), axis=1, tiled=True)
    branch = jnp.dot(
        head_rows,
        lax.all_gather(output_weight, "row", axis=0, tiled=True),
        preferred_element_type=jnp.float32,
    )
    squares = lax.psum(jnp.sum(branch * branch, axis=-1), ("col", "sub"))
    scaled = branch * lax.rsqrt(squares[:, None] / MODEL_WIDTH + EPSILON) * post_gain
    return (stream_in.astype(jnp.float32) + scaled).astype(jnp.bfloat16)


def swapped(x, axis, rows=None):
    if rows is None or axis == "sub":
        return lax.ppermute(x, axis, [(0, 1), (1, 0)])
    count = lax.axis_size("row")
    names = ("groups", "row", "sub") if axis == "groups" else ("row", "col", "sub")
    row_stride = 2 if axis == "groups" else 4
    stride = 2 * count if axis == "groups" else 2
    pairs = []
    for device in range(4 * count):
        step = stride if (device // row_stride) % count in rows else 1
        pairs.append((device, device + step if (device // step) % 2 == 0 else device - step))
    return lax.ppermute(x, names, pairs)


def exchanged(x, planes):
    other = dict(zip(planes, planes[::-1]))
    pairs = [
        (2 * r + s, 2 * other[r] + s if r in other else 2 * r + 1 - s)
        for r in range(lax.axis_size("row"))
        for s in range(2)
    ]
    return lax.ppermute(x, ("row", "sub"), pairs)


def after(x, *earlier):
    return lax.optimization_barrier((x, *earlier))[0]


def settle(*values):
    return lax.optimization_barrier(values)


def whole(shape):
    return pl.BlockSpec(shape, lambda *_: (0,) * len(shape))


ANYWHERE = pl.BlockSpec(memory_space=pl.ANY)
LITTLE = pl.CostEstimate(flops=0, bytes_accessed=0, transcendentals=0)


def norm_kernel(table, *refs):
    *pieces, gain, out = refs[-6:]
    depth = pieces[0].shape[1]
    squares = sum(
        jnp.sum(jnp.square(p[0].astype(jnp.float32)), axis=0, keepdims=True) for p in pieces
    )
    scale = lax.rsqrt(squares / MODEL_WIDTH + EPSILON)
    for index, piece in enumerate(pieces):
        rows = pl.ds(pl.multiple_of(table[index] * depth, depth), depth)
        out[0, rows, :] = (piece[0].astype(jnp.float32) * scale * gain[index]).astype(jnp.bfloat16)


def norm_block(table, pieces, which, gain, index, held):
    _, depth, tokens = pieces[0].shape
    lanes = tokens // 2
    shape = (4, 4 * depth, tokens)
    before = () if held is None else (held,)
    return pl.pallas_call(
        norm_kernel,
        grid_spec=pltpu.PrefetchScalarGridSpec(
            num_scalar_prefetch=1,
            grid=(tokens // lanes,),
            in_specs=[ANYWHERE] * len(before)
            + [pl.BlockSpec((1, depth, lanes), lambda t, *_: (which, 0, t))] * 4
            + [whole((4, depth, 1))],
            out_specs=pl.BlockSpec((1, 4 * depth, lanes), lambda t, *_: (index, 0, t)),
        ),
        out_shape=jax.ShapeDtypeStruct(shape, jnp.bfloat16),
        input_output_aliases={1: 0} if before else {},
        compiler_params=pltpu.CompilerParams(vmem_limit_bytes=VMEM_BYTES),
        cost_estimate=pl.CostEstimate(
            flops=40 * depth * tokens, bytes_accessed=16 * depth * tokens, transcendentals=0
        ),
    )(table, *before, *pieces, gain)


def order_pieces(table, pieces, ordered):
    base = 0
    for index, piece in enumerate(pieces):
        depth, width = piece.shape
        rows = pl.ds(pl.multiple_of(table[2 * index], 16), depth)
        columns = pl.ds(pl.multiple_of(table[2 * index + 1], width), width)
        ordered[rows, columns] = piece[...]


def project_early_kernel(count, table, normed, *refs):
    pieces, out, ordered = refs[:count], refs[-2], refs[-1]

    @pl.when(pl.program_id(0) == 0)
    def _():
        order_pieces(table, pieces, ordered)

    out[0] = lax.dot_general(
        ordered[...], normed[0], (((0,), (0,)), ((), ())), preferred_element_type=jnp.float32
    )


def project_early(table, normed, pieces, first, blocks, held):
    _, features, tokens = normed.shape
    width = 2 * pieces[0].shape[1]
    before = () if held is None else (held,)
    return pl.pallas_call(
        functools.partial(project_early_kernel, len(pieces)),
        grid_spec=pltpu.PrefetchScalarGridSpec(
            num_scalar_prefetch=1,
            grid=(blocks,),
            in_specs=[pl.BlockSpec((1, features // 2, tokens), lambda i, t: (first + i, 0, 0))]
            + [whole(p.shape) for p in pieces]
            + [ANYWHERE] * len(before),
            out_specs=pl.BlockSpec((1, width, tokens), lambda i, t: (first + i, 0, 0)),
            scratch_shapes=[pltpu.VMEM((features // 2, width), jnp.bfloat16)],
        ),
        out_shape=jax.ShapeDtypeStruct((4, width, tokens), jnp.float32),
        input_output_aliases={2 + len(pieces): 0} if before else {},
        compiler_params=pltpu.CompilerParams(vmem_limit_bytes=VMEM_BYTES),
        cost_estimate=pl.CostEstimate(
            flops=2 * blocks * tokens * features // 2 * width,
            bytes_accessed=blocks * features * tokens + features * width + 4 * blocks * width * tokens,
            transcendentals=0,
        ),
    )(table, normed, *pieces, *before)


def project_late_kernel(count, table, normed, *refs):
    pieces, refs = refs[:count], refs[count:]
    early, q_gain, k_gain, cosine, sine, q_out, k_out, v_out, total, ordered = refs

    @pl.when(pl.program_id(0) == 0)
    def _():
        order_pieces(table, pieces, ordered)

    total[...] = early[0] + lax.dot_general(
        ordered[...], normed[0], (((0,), (0,)), ((), ())), preferred_element_type=jnp.float32
    )
    head = q_gain.shape[0]
    half = head // 2
    width = q_out.shape[1]
    cos, sin = cosine[...], sine[...]

    def rotated(start, head_gain):
        values = total[start : start + head, :]
        values = (
            values
            * lax.rsqrt(jnp.mean(values * values, axis=0, keepdims=True) + EPSILON)
            * head_gain[:, :1]
        )
        first, second = values[:half], values[half:]
        return jnp.concatenate(
            [first * cos - second * sin, second * cos + first * sin], axis=0
        ).astype(jnp.bfloat16)

    for start in range(0, width, head):
        q_out[0, start : start + head, :] = rotated(start, q_gain)
    for start in range(0, width // 2, head):
        k_out[:, start : start + head] = rotated(width + start, k_gain).T
    v_out[...] = total[width + width // 2 :, :].astype(jnp.bfloat16)


def project_late(table, normed, pieces, early, extras):
    blocks, features, tokens = normed.shape
    width = early.shape[1] // 2
    head = extras[0].shape[0]
    half = head // 2
    count = len(pieces)
    turn = pl.BlockSpec((half, tokens), lambda i, t: (0, t[2 * count + i]))
    return pl.pallas_call(
        functools.partial(project_late_kernel, count),
        grid_spec=pltpu.PrefetchScalarGridSpec(
            num_scalar_prefetch=1,
            grid=(blocks,),
            in_specs=[pl.BlockSpec((1, features // 2, tokens), lambda i, t: (i, 1, 0))]
            + [whole(p.shape) for p in pieces]
            + [
                pl.BlockSpec((1, 2 * width, tokens), lambda i, t: (i, 0, 0)),
                whole((head, head)),
                whole((head, head)),
                turn,
                turn,
            ],
            out_specs=[
                pl.BlockSpec((1, width, tokens), lambda i, t: (i, 0, 0)),
                pl.BlockSpec((tokens, width // 2), lambda i, t: (t[2 * count + i], 0)),
                pl.BlockSpec((width // 2, tokens), lambda i, t: (0, t[2 * count + i])),
            ],
            scratch_shapes=[
                pltpu.VMEM((2 * width, tokens), jnp.float32),
                pltpu.VMEM((features // 2, 2 * width), jnp.bfloat16),
            ],
        ),
        out_shape=[
            jax.ShapeDtypeStruct((blocks, width, tokens), jnp.bfloat16),
            jax.ShapeDtypeStruct((blocks * tokens, width // 2), jnp.bfloat16),
            jax.ShapeDtypeStruct((width // 2, blocks * tokens), jnp.bfloat16),
        ],
        compiler_params=pltpu.CompilerParams(vmem_limit_bytes=VMEM_BYTES),
        cost_estimate=LITTLE,
    )(table, normed, *pieces, early, *extras)


def attend_kernel(band, scale, table, q_ref, keys, values, *refs):
    out, mask = refs[-2:]
    head = 128
    tile = out.shape[1]
    first = table[0] * (2 * tile) + pl.program_id(0) * tile
    start = pl.multiple_of(jnp.clip(first + tile - band, 0, keys.shape[0] - band), tile)
    places = lax.broadcasted_iota(jnp.int32, (band, tile), 1)
    distance = (first - start) + places - lax.broadcasted_iota(jnp.int32, (band, tile), 0)
    hidden = jnp.where((distance >= 0) & (distance < WINDOW_LENGTH), 0.0, -1e30)
    mask[:, :tile] = hidden
    mask[:, tile:] = hidden
    pairs = keys.shape[1] // head
    factor = scale * 1.4426950408889634
    chunks = [slice(a, min(a + tile, band)) for a in range(0, band, tile)]

    def pair_of(ref, index):
        return [slice((2 * index + i) * head, (2 * index + i + 1) * head) for i in range(2)]

    def query(index):
        return jnp.concatenate([q_ref[0, rows, :] for rows in pair_of(q_ref, index)], axis=1)

    def within(chunk):
        return pl.ds(pl.multiple_of(start + chunk.start, tile), chunk.stop - chunk.start)

    def score(index, chunk, queries):
        columns = slice(index * head, (index + 1) * head)
        return mask[chunk, :] + jnp.dot(
            keys[within(chunk), columns], queries, preferred_element_type=jnp.float32
        )

    queries = query(0)
    scores = [score(0, chunk, queries) for chunk in chunks]
    for index in range(pairs):
        top = functools.reduce(
            jnp.maximum, [jnp.max(part, axis=0, keepdims=True) for part in scores]
        )
        queries = query(index + 1) if index + 1 < pairs else None
        exponents, upcoming, total = [], [], 0.0
        for chunk, part in zip(chunks, scores):
            exponent = jnp.exp2((part - top) * factor)
            exponents.append(exponent)
            total = total + jnp.sum(exponent, axis=0, keepdims=True)
            if queries is not None:
                upcoming.append(score(index + 1, chunk, queries))
        inverse = 1.0 / total
        result = 0.0
        rows = slice(index * head, (index + 1) * head)
        for chunk, exponent in zip(chunks, exponents):
            result = result + jnp.dot(
                values[rows, within(chunk)],
                (exponent * inverse).astype(jnp.bfloat16),
                preferred_element_type=jnp.float32,
            )
        for i, here in enumerate(pair_of(out, index)):
            out[here, :] = result[:, i * tile : (i + 1) * tile].astype(jnp.bfloat16)
        scores = upcoming


def attend(block, index, queries, keys, values, earlier):
    _, width, tokens = queries.shape
    tile = tokens // 2
    band = min(WINDOW_LENGTH + tile, keys.shape[0])
    return pl.pallas_call(
        functools.partial(attend_kernel, band, float(MODEL_WIDTH // QUERY_HEAD_COUNT) ** (-0.5)),
        grid_spec=pltpu.PrefetchScalarGridSpec(
            num_scalar_prefetch=1,
            grid=(2,),
            in_specs=[
                pl.BlockSpec((1, width, tile), lambda t, *_: (index, 0, t)),
                whole(keys.shape),
                whole(values.shape),
            ]
            + [ANYWHERE] * len(earlier),
            out_specs=pl.BlockSpec((width, tile), lambda t, *_: (0, t)),
            scratch_shapes=[pltpu.VMEM((band, 2 * tile), jnp.float32)],
        ),
        out_shape=jax.ShapeDtypeStruct((width, tokens), jnp.bfloat16),
        compiler_params=pltpu.CompilerParams(vmem_limit_bytes=VMEM_BYTES),
        cost_estimate=LITTLE,
    )(block[None], queries, keys, values, *earlier)


def output_kernel(count, full, table, *refs):
    parts, pieces, (out, squares, held, row_held) = refs[:8], refs[8 : 8 + count], refs[8 + count :]
    depth = parts[0].shape[0]
    step = pl.program_id(0)

    @pl.when(step == 0)
    def _():
        for index, part in enumerate(parts):
            held[index * depth : (index + 1) * depth, :] = part[...]
        squares[...] = jnp.zeros_like(squares)

    for index, piece in enumerate(pieces):

        @pl.when(table[index] < full)
        def _(index=index, piece=piece):
            there = pl.ds(pl.multiple_of(table[index], 128), piece.shape[1])
            row_held[:, there] = piece[...]

    product = jnp.dot(row_held[...], held[...], preferred_element_type=jnp.float32)
    out[...] = product
    squares[...] += jnp.sum(jnp.square(product), axis=0, keepdims=True)


def output_product(table, parts, pieces):
    depth, tokens = parts[0].shape
    width = pieces[0][0].shape[0]
    full = 8 * depth
    tile = width // 4

    def rows(index, column, columns):
        return pl.BlockSpec(
            (tile, columns), lambda t, table: (jnp.where(table[index] < full, t, 0), column)
        )

    return pl.pallas_call(
        functools.partial(output_kernel, len(pieces), full),
        grid_spec=pltpu.PrefetchScalarGridSpec(
            num_scalar_prefetch=1,
            grid=(width // tile,),
            in_specs=[whole((depth, tokens))] * 8
            + [rows(index, column, columns) for index, (_, column, columns) in enumerate(pieces)],
            out_specs=[pl.BlockSpec((tile, tokens), lambda t, *_: (t, 0)), whole((1, tokens))],
            scratch_shapes=[
                pltpu.VMEM((full, tokens), jnp.bfloat16),
                pltpu.VMEM((tile, full), jnp.bfloat16),
            ],
        ),
        out_shape=[
            jax.ShapeDtypeStruct((width, tokens), jnp.float32),
            jax.ShapeDtypeStruct((1, tokens), jnp.float32),
        ],
        compiler_params=pltpu.CompilerParams(vmem_limit_bytes=VMEM_BYTES),
        cost_estimate=pl.CostEstimate(
            flops=2 * tokens * full * width,
            bytes_accessed=2 * full * (tokens + width) + 4 * tokens * width,
            transcendentals=0,
        ),
    )(table, *parts, *(piece for piece, _, _ in pieces))


def middle_form(
    stream_in,
    in_gain,
    query_weight,
    key_matrix,
    value_matrix,
    query_gain,
    key_norm_gain,
    output_weight,
    post_gain,
):
    stream = stream_in.T
    features, tokens = stream.shape
    head = query_gain.shape[0]
    row = lax.axis_index("row")
    group = lax.axis_index("groups")
    place = lax.axis_index("col") * 2 + lax.axis_index("sub")
    upper = (row >= 2).astype(jnp.int32)
    in_middle = (row == 1) | (row == 2)
    near_block, cross_block, far_block = 3 * upper, 3 - row, 3 - 3 * upper
    blocks = (row, near_block, cross_block, far_block)
    slot = lambda block: jnp.bitwise_xor(place, block)
    ints = lambda *values: jnp.stack([jnp.asarray(v, jnp.int32) for v in values])
    beside = [(0, 1), (1, 0), (2, 3), (3, 2)]
    beyond = [(0, 2), (1, 0), (2, 3), (3, 1)]
    outside = [(0, 1), (1, 3), (2, 0), (3, 2)]
    middles, ends = (1, 2), (0, 3)

    half = query_weight.shape[1] // 2
    quarter = key_matrix.shape[1] // 2

    def side(which):
        queries = lax.dynamic_slice_in_dim(query_weight, which * half, half, axis=1)
        keys = lax.dynamic_slice_in_dim(key_matrix, which * quarter, quarter, axis=1)
        values = lax.dynamic_slice_in_dim(value_matrix, which * quarter, quarter, axis=1)
        return queries, jnp.concatenate([keys, values], axis=1)

    own_queries, own_pairs = side(upper)
    own_side = jnp.where(group == 0, own_queries, own_pairs)
    other_side = jnp.where(group == 0, *side(1 - upper))
    turned = output_weight.T
    depth = turned.shape[1] // 2
    mine = lax.dynamic_slice_in_dim(turned, group * depth, depth, axis=1)
    theirs = lax.dynamic_slice_in_dim(turned, (1 - group) * depth, depth, axis=1)

    gain_rows = in_gain.reshape(4, features)
    gain = jnp.concatenate(
        [lax.dynamic_slice_in_dim(gain_rows, slot(j), 1, axis=0) for j in range(4)], axis=0
    )[:, :, None]
    arrival = lambda block: jnp.where(
        block == row, 0, jnp.where(block == near_block, 1, jnp.where(block == far_block, 2, 3))
    )
    order = ints(*(arrival(slot(j)) for j in range(4)))

    positions = jnp.arange(4 * tokens, dtype=jnp.int32).astype(jnp.float32)
    cosine, sine = rotary_tables(positions, head)
    spread = lambda gains: jnp.broadcast_to(gains[:, None], (head, head))
    tables = (spread(query_gain), spread(key_norm_gain), cosine.T, sine.T)

    x_cross = exchanged(stream, middles)
    x_near = lax.ppermute(stream, "row", beside)
    own_col = swapped(stream, "col")
    own_sub = swapped(stream, "sub")
    x_cross, x_near, own_col, own_side, other_side, mine = settle(
        x_cross, x_near, own_col, own_side, other_side, mine
    )

    x_far = exchanged(x_near, middles)
    w_near = lax.ppermute(own_side, "row", beside)
    near_col = swapped(x_near, "col")
    own_both = swapped(own_col, "sub")
    near_sub = swapped(x_near, "sub")
    own_pieces = (stream[None], own_sub[None], own_col[None], own_both[None])
    order, *tables = settle(order, *tables)
    normed = norm_block(order, own_pieces, 0, gain, 0, None)
    x_far, w_near, near_col, other_side, mine, normed, x_cross = settle(
        x_far, w_near, near_col, other_side, mine, normed, x_cross
    )
    w_cross = exchanged(other_side, middles)
    cross_col = swapped(x_cross, "col")
    o_in = lax.ppermute(mine, "row", beside)
    w_near_y = swapped(w_near, "groups")
    near_both = swapped(near_col, "sub")
    cross_sub = swapped(x_cross, "sub")
    far_sub = swapped(x_far, "sub")
    near_pieces = (x_near[None], near_sub[None], near_col[None], near_both[None])
    normed = norm_block(order, near_pieces, 0, gain, 1, normed)
    w_cross, o_in, w_near_y, cross_col, x_far, normed, other_side, theirs, cross_sub = settle(
        w_cross, o_in, w_near_y, cross_col, x_far, normed, other_side, theirs, cross_sub
    )

    w_far = lax.ppermute(other_side, "row", beyond)
    far_col = swapped(x_far, "col")
    cross_both = swapped(cross_col, "sub")
    w_cross_y = swapped(w_cross, "groups")
    cross_pieces = (x_cross[None], cross_sub[None], cross_col[None], cross_both[None])
    normed = norm_block(order, cross_pieces, 0, gain, 2, normed)
    early_table = ints(0, 0, 0, half, features, group * half, features, (1 - group) * half)
    early_pieces = (own_queries, own_pairs, w_near, w_near_y)
    total = project_early(early_table, normed, early_pieces, 0, 3, None)
    w_far, far_col, w_cross_y, total, o_in, theirs = settle(
        w_far, far_col, w_cross_y, total, o_in, theirs
    )

    w_far_y = swapped(w_far, "groups")
    far_both = swapped(far_col, "sub")
    o_far = exchanged(o_in, middles)
    o_in_rest = lax.ppermute(theirs, "row", beside)
    far_pieces = (x_far[None], far_sub[None], far_col[None], far_both[None])
    normed = norm_block(order, far_pieces, 0, gain, 3, normed)
    total = project_early(early_table, normed, early_pieces, 3, 1, total)
    w_far_y, o_far, total, o_in_rest = settle(w_far_y, o_far, total, o_in_rest)
    o_end_far = lax.ppermute(o_far, "row", beside)
    o_cross = exchanged(mine, middles)
    o_far_y = swapped(o_far, "groups", middles)
    here, there = group * half, (1 - group) * half
    queries, keys, values = project_late(
        ints(0, here, 0, there, features, here, features, there, *blocks),
        normed,
        (w_far, w_far_y, w_cross, w_cross_y),
        total,
        tables,
    )

    def attended(index, *earlier):
        return attend(blocks[index].astype(jnp.int32), index, queries, keys, values, earlier)

    cross_part = attended(2)
    to_cross = exchanged(cross_part, middles)
    shown, o_end_far, o_cross = settle(cross_part, o_end_far, o_cross)
    o_end_cross = lax.ppermute(o_cross, "row", beside)
    o_end_far_y = swapped(o_end_far, "groups", ends)
    o_cross_y = swapped(o_cross, "groups", middles)
    near_part = attended(1, shown)
    to_near = lax.ppermute(near_part, "row", beside)
    far_part = attended(3, near_part, o_far_y)
    to_far = lax.ppermute(far_part, "row", outside)
    own_part = attended(0, far_part, to_cross, o_end_far_y)
    this_side = jnp.where(in_middle, own_part, to_near)
    this_across = swapped(this_side, "col")
    that_side = jnp.where(in_middle, to_cross, after(to_far, own_part))
    that_across = swapped(that_side, "col")
    o_end_cross_y = swapped(after(o_end_cross, own_part), "groups", ends)

    pair_block = jnp.bitwise_xor(row, 1)
    out_pieces, out_table = [], []

    def put(piece, column, columns, block, which, offset, here):
        spot = (2 * slot(block) + jnp.bitwise_xor(which, upper)) * depth + offset
        out_pieces.append((piece, column, columns))
        out_table.append(spot if here is None else jnp.where(here, spot, 8 * depth))

    for part in range(2):
        put(turned, part, depth, row, part, 0, None)
    put(o_in, 0, depth, pair_block, group, 0, None)
    put(o_in_rest, 0, depth, pair_block, 1 - group, 0, None)
    put(o_far, 0, depth, 3 - pair_block, group, 0, in_middle)
    put(o_far_y, 0, depth, 3 - pair_block, 1 - group, 0, in_middle)
    put(o_end_far, 0, depth, 3 - row, group, 0, ~in_middle)
    put(o_end_far_y, 0, depth, 3 - row, 1 - group, 0, ~in_middle)
    put(o_cross, 0, depth, 3 - row, group, 0, in_middle)
    put(o_cross_y, 0, depth, 3 - row, 1 - group, 0, in_middle)
    put(o_end_cross, 0, depth, 3 - pair_block, group, 0, ~in_middle)
    put(o_end_cross_y, 0, depth, 3 - pair_block, 1 - group, 0, ~in_middle)

    parts = (
        this_side,
        that_side,
        swapped(this_side, "sub"),
        swapped(that_side, "sub"),
        this_across,
        that_across,
        swapped(this_across, "sub"),
        swapped(that_across, "sub"),
    )
    branch, squares = output_product(ints(*out_table), parts, out_pieces)
    diagonal = lax.ppermute(squares, ("col", "sub"), [(0, 3), (1, 2), (2, 1), (3, 0)])
    squares = squares + swapped(squares, "sub") + swapped(squares, "col") + diagonal
    scaled = branch * lax.rsqrt(squares / MODEL_WIDTH + EPSILON) * post_gain[:, None]
    return (stream.astype(jnp.float32) + scaled).astype(jnp.bfloat16).T


def on_device(*args):
    stream_in, _, query_weight, key_matrix, value_matrix, query_gain, *_ = args
    sizes = tuple(lax.axis_size(name) for name in ("groups", "row", "col", "sub"))
    tokens, head = stream_in.shape[0], query_gain.shape[0]
    fits = (
        sizes == (2, 4, 2, 2)
        and head == 128
        and tokens % 256 == 0
        and key_matrix.shape[1] % (2 * head) == 0
        and query_weight.shape[1] == 2 * key_matrix.shape[1]
        and value_matrix.shape[1] == key_matrix.shape[1]
    )
    return middle_form(*args) if fits else general_form(*args)


def solution(mesh):
    placed = (
        P(("groups", "row"), ("col", "sub")),
        P(),
        P("row", ("col", "sub")),
        P("row", ("col", "sub")),
        P("row", ("col", "sub")),
        P(),
        P(),
        P("row", ("col", "sub")),
        P(("col", "sub")),
    )
    return jax.shard_map(
        on_device,
        mesh=mesh,
        in_specs=placed,
        out_specs=P(("groups", "row"), ("col", "sub")),
        check_vma=False,
    )
```

```python
import functools

import jax
import jax.numpy as jnp
from jax import lax
from jax.experimental import pallas as pl
from jax.experimental.pallas import tpu as pltpu
from jax.sharding import PartitionSpec as P

MODEL_WIDTH = 5376
QUERY_HEAD_COUNT = 32
WINDOW_LENGTH = 1024


EPSILON = 1e-06
VMEM_BYTES = 64 * 1024 * 1024 - 128 * 1024


def shifted(x, axis, by):
    count = lax.axis_size(axis)
    pairs = [(i, i + by) for i in range(count) if 0 <= i + by < count]
    return lax.ppermute(x, axis, pairs)


def root_mean_scale(values, gain):
    return values * lax.rsqrt(jnp.mean(values * values, axis=-1, keepdims=True) + EPSILON) * gain


def rotary_tables(token_positions, size):
    half_dim = size // 2
    inverse = 10000.0 ** (-(jnp.arange(half_dim, dtype=jnp.float32) * 2.0) / size)
    angles = token_positions[:, None] * inverse[None, :]
    return jnp.cos(angles), jnp.sin(angles)


def apply_rotary(tensor, token_positions):
    half_dim = tensor.shape[-1] // 2
    cosine, sine_part = rotary_tables(token_positions, tensor.shape[-1])
    cosine, sine_part = cosine[:, None, :], sine_part[:, None, :]
    first_half = tensor[..., :half_dim]
    second_half = tensor[..., half_dim:]
    return jnp.concatenate(
        [
            first_half * cosine - second_half * sine_part,
            second_half * cosine + first_half * sine_part,
        ],
        axis=-1,
    )


def general_form(
    stream_in,
    in_gain,
    query_weight,
    key_matrix,
    value_matrix,
    query_gain,
    key_norm_gain,
    output_weight,
    post_gain,
):
    token_rows = lax.all_gather(stream_in, ("col", "sub"), axis=1, tiled=True)
    tokens = token_rows.shape[0]
    normed = root_mean_scale(token_rows.astype(jnp.float32), in_gain).astype(jnp.bfloat16)

    def add_panel(panel_piece):
        return jnp.dot(normed, panel_piece, preferred_element_type=jnp.float32)

    query_proj = add_panel(lax.all_gather(query_weight, "row", axis=0, tiled=True))
    projected_keys = add_panel(lax.all_gather(key_matrix, "row", axis=0, tiled=True))
    projected_values = add_panel(lax.all_gather(value_matrix, "row", axis=0, tiled=True))
    head_size = query_gain.shape[0]
    query_heads = query_weight.shape[1] // head_size
    pair_heads = key_matrix.shape[1] // head_size
    group_count = query_heads // pair_heads
    scale_factor = float(MODEL_WIDTH // QUERY_HEAD_COUNT) ** (-0.5)
    row_index = lax.axis_index("row")
    query_places = row_index * tokens + jnp.arange(tokens, dtype=jnp.int32)
    query_rot = apply_rotary(
        root_mean_scale(query_proj.reshape(tokens, query_heads, head_size), query_gain),
        query_places.astype(jnp.float32),
    ).astype(jnp.bfloat16)
    rotary_keys = apply_rotary(
        root_mean_scale(projected_keys.reshape(tokens, pair_heads, head_size), key_norm_gain),
        query_places.astype(jnp.float32),
    ).astype(jnp.bfloat16)
    keys_flat = rotary_keys.reshape(tokens, pair_heads * head_size)
    values_flat = projected_values.astype(jnp.bfloat16)
    shards_back = min(WINDOW_LENGTH // tokens, lax.axis_size("row") - 1)
    band_length = (shards_back + 1) * tokens
    key_parts = [keys_flat]
    value_parts = [values_flat]
    for offset in range(1, shards_back + 1):
        keys_prior, values_prior = shifted((keys_flat, values_flat), "row", offset)
        key_parts = [keys_prior] + key_parts
        value_parts = [values_prior] + value_parts
    keys_band = jnp.concatenate(key_parts, axis=0)
    values_band = jnp.concatenate(value_parts, axis=0)
    key_places = (row_index - shards_back) * tokens + jnp.arange(band_length, dtype=jnp.int32)
    distance = query_places[:, None] - key_places[None, :]
    visible = (distance >= 0) & (distance < WINDOW_LENGTH) & (key_places[None, :] >= 0)
    grouped = query_rot.reshape(tokens, pair_heads, group_count, head_size)
    scores = (
        jnp.einsum(
            "qhgd,shd->hgqs",
            grouped,
            keys_band.reshape(band_length, pair_heads, head_size),
            preferred_element_type=jnp.float32,
        )
        * scale_factor
    )
    scores = jnp.where(visible, scores, -1e30)
    row_max = jnp.max(scores, axis=-1, keepdims=True)
    exponent = jnp.exp(scores - row_max)
    weights = (exponent / jnp.sum(exponent, axis=-1, keepdims=True)).astype(jnp.bfloat16)
    attended = jnp.einsum(
        "hgqs,shd->qhgd",
        weights,
        values_band.reshape(band_length, pair_heads, head_size),
        preferred_element_type=jnp.float32,
    )
    heads_out = attended.reshape(tokens, query_heads * head_size).astype(jnp.bfloat16)
    head_rows = lax.all_gather(heads_out, ("col", "sub"), axis=1, tiled=True)
    branch = jnp.dot(
        head_rows,
        lax.all_gather(output_weight, "row", axis=0, tiled=True),
        preferred_element_type=jnp.float32,
    )
    squares = lax.psum(jnp.sum(branch * branch, axis=-1), ("col", "sub"))
    scaled = branch * lax.rsqrt(squares[:, None] / MODEL_WIDTH + EPSILON) * post_gain
    return (stream_in.astype(jnp.float32) + scaled).astype(jnp.bfloat16)


def swapped(x, axis, rows=None):
    if rows is None or axis == "sub":
        return lax.ppermute(x, axis, [(0, 1), (1, 0)])
    count = lax.axis_size("row")
    names = ("groups", "row", "sub") if axis == "groups" else ("row", "col", "sub")
    row_stride = 2 if axis == "groups" else 4
    stride = 2 * count if axis == "groups" else 2
    pairs = []
    for device in range(4 * count):
        step = stride if (device // row_stride) % count in rows else 1
        pairs.append((device, device + step if (device // step) % 2 == 0 else device - step))
    return lax.ppermute(x, names, pairs)


def exchanged(x, planes):
    other = dict(zip(planes, planes[::-1]))
    pairs = [
        (2 * r + s, 2 * other[r] + s if r in other else 2 * r + 1 - s)
        for r in range(lax.axis_size("row"))
        for s in range(2)
    ]
    return lax.ppermute(x, ("row", "sub"), pairs)


def after(x, *earlier):
    return lax.optimization_barrier((x, *earlier))[0]


def settle(*values):
    return lax.optimization_barrier(values)


def whole(shape):
    return pl.BlockSpec(shape, lambda *_: (0,) * len(shape))


ANYWHERE = pl.BlockSpec(memory_space=pl.ANY)
LITTLE = pl.CostEstimate(flops=0, bytes_accessed=0, transcendentals=0)


def norm_kernel(table, *refs):
    *pieces, gain, out = refs[-6:]
    depth = pieces[0].shape[1]
    squares = sum(
        jnp.sum(jnp.square(p[0].astype(jnp.float32)), axis=0, keepdims=True) for p in pieces
    )
    scale = lax.rsqrt(squares / MODEL_WIDTH + EPSILON)
    for index, piece in enumerate(pieces):
        rows = pl.ds(pl.multiple_of(table[index] * depth, depth), depth)
        out[0, rows, :] = (piece[0].astype(jnp.float32) * scale * gain[index]).astype(jnp.bfloat16)


def norm_block(table, pieces, which, gain, index, held):
    _, depth, tokens = pieces[0].shape
    lanes = tokens // 2
    shape = (4, 4 * depth, tokens)
    before = () if held is None else (held,)
    return pl.pallas_call(
        norm_kernel,
        grid_spec=pltpu.PrefetchScalarGridSpec(
            num_scalar_prefetch=1,
            grid=(tokens // lanes,),
            in_specs=[ANYWHERE] * len(before)
            + [pl.BlockSpec((1, depth, lanes), lambda t, *_: (which, 0, t))] * 4
            + [whole((4, depth, 1))],
            out_specs=pl.BlockSpec((1, 4 * depth, lanes), lambda t, *_: (index, 0, t)),
        ),
        out_shape=jax.ShapeDtypeStruct(shape, jnp.bfloat16),
        input_output_aliases={1: 0} if before else {},
        compiler_params=pltpu.CompilerParams(vmem_limit_bytes=VMEM_BYTES),
        cost_estimate=pl.CostEstimate(
            flops=40 * depth * tokens, bytes_accessed=16 * depth * tokens, transcendentals=0
        ),
    )(table, *before, *pieces, gain)


def order_pieces(table, pieces, ordered):
    base = 0
    for index, piece in enumerate(pieces):
        depth, width = piece.shape
        rows = pl.ds(pl.multiple_of(table[2 * index], 16), depth)
        columns = pl.ds(pl.multiple_of(table[2 * index + 1], width), width)
        ordered[rows, columns] = piece[...]


def project_early_kernel(count, table, normed, *refs):
    pieces, out, ordered = refs[:count], refs[-2], refs[-1]

    @pl.when(pl.program_id(0) == 0)
    def _():
        order_pieces(table, pieces, ordered)

    out[0] = lax.dot_general(
        ordered[...], normed[0], (((0,), (0,)), ((), ())), preferred_element_type=jnp.float32
    )


def project_early(table, normed, pieces, first, blocks, held):
    _, features, tokens = normed.shape
    width = 2 * pieces[0].shape[1]
    before = () if held is None else (held,)
    return pl.pallas_call(
        functools.partial(project_early_kernel, len(pieces)),
        grid_spec=pltpu.PrefetchScalarGridSpec(
            num_scalar_prefetch=1,
            grid=(blocks,),
            in_specs=[pl.BlockSpec((1, features // 2, tokens), lambda i, t: (first + i, 0, 0))]
            + [whole(p.shape) for p in pieces]
            + [ANYWHERE] * len(before),
            out_specs=pl.BlockSpec((1, width, tokens), lambda i, t: (first + i, 0, 0)),
            scratch_shapes=[pltpu.VMEM((features // 2, width), jnp.bfloat16)],
        ),
        out_shape=jax.ShapeDtypeStruct((4, width, tokens), jnp.float32),
        input_output_aliases={2 + len(pieces): 0} if before else {},
        compiler_params=pltpu.CompilerParams(vmem_limit_bytes=VMEM_BYTES),
        cost_estimate=pl.CostEstimate(
            flops=2 * blocks * tokens * features // 2 * width,
            bytes_accessed=blocks * features * tokens + features * width + 4 * blocks * width * tokens,
            transcendentals=0,
        ),
    )(table, normed, *pieces, *before)


def project_late_kernel(count, table, normed, *refs):
    pieces, refs = refs[:count], refs[count:]
    early, q_gain, k_gain, cosine, sine, q_out, k_out, v_out, total, ordered = refs

    @pl.when(pl.program_id(0) == 0)
    def _():
        order_pieces(table, pieces, ordered)

    total[...] = early[0] + lax.dot_general(
        ordered[...], normed[0], (((0,), (0,)), ((), ())), preferred_element_type=jnp.float32
    )
    head = q_gain.shape[0]
    half = head // 2
    width = q_out.shape[1]
    cos, sin = cosine[...], sine[...]

    def rotated(start, head_gain):
        values = total[start : start + head, :]
        values = (
            values
            * lax.rsqrt(jnp.mean(values * values, axis=0, keepdims=True) + EPSILON)
            * head_gain[:, :1]
        )
        first, second = values[:half], values[half:]
        return jnp.concatenate(
            [first * cos - second * sin, second * cos + first * sin], axis=0
        ).astype(jnp.bfloat16)

    for start in range(0, width, head):
        q_out[0, start : start + head, :] = rotated(start, q_gain)
    for start in range(0, width // 2, head):
        k_out[:, start : start + head] = rotated(width + start, k_gain).T
    v_out[...] = total[width + width // 2 :, :].astype(jnp.bfloat16)


def project_late(table, normed, pieces, early, extras):
    blocks, features, tokens = normed.shape
    width = early.shape[1] // 2
    head = extras[0].shape[0]
    half = head // 2
    count = len(pieces)
    turn = pl.BlockSpec((half, tokens), lambda i, t: (0, t[2 * count + i]))
    return pl.pallas_call(
        functools.partial(project_late_kernel, count),
        grid_spec=pltpu.PrefetchScalarGridSpec(
            num_scalar_prefetch=1,
            grid=(blocks,),
            in_specs=[pl.BlockSpec((1, features // 2, tokens), lambda i, t: (i, 1, 0))]
            + [whole(p.shape) for p in pieces]
            + [
                pl.BlockSpec((1, 2 * width, tokens), lambda i, t: (i, 0, 0)),
                whole((head, head)),
                whole((head, head)),
                turn,
                turn,
            ],
            out_specs=[
                pl.BlockSpec((1, width, tokens), lambda i, t: (i, 0, 0)),
                pl.BlockSpec((tokens, width // 2), lambda i, t: (t[2 * count + i], 0)),
                pl.BlockSpec((width // 2, tokens), lambda i, t: (0, t[2 * count + i])),
            ],
            scratch_shapes=[
                pltpu.VMEM((2 * width, tokens), jnp.float32),
                pltpu.VMEM((features // 2, 2 * width), jnp.bfloat16),
            ],
        ),
        out_shape=[
            jax.ShapeDtypeStruct((blocks, width, tokens), jnp.bfloat16),
            jax.ShapeDtypeStruct((blocks * tokens, width // 2), jnp.bfloat16),
            jax.ShapeDtypeStruct((width // 2, blocks * tokens), jnp.bfloat16),
        ],
        compiler_params=pltpu.CompilerParams(vmem_limit_bytes=VMEM_BYTES),
        cost_estimate=pl.CostEstimate(
            flops=2 * blocks * tokens * features * width,
            bytes_accessed=blocks * features * tokens + 2 * features * width + 8 * blocks * width * tokens,
            transcendentals=0,
        ),
    )(table, normed, *pieces, early, *extras)


def attend_kernel(scale, table, q_ref, keys, values, *refs):
    out, mask = refs[-2:]
    head = 128
    tile = out.shape[1]
    span = WINDOW_LENGTH // tile + 1
    place = table[0] * 2 + pl.program_id(0)
    later = lax.broadcasted_iota(jnp.int32, (tile, tile), 1) >= lax.broadcasted_iota(
        jnp.int32, (tile, tile), 0
    )
    for index, seen in enumerate((later, jnp.logical_not(later))):
        hidden = jnp.where(seen, 0.0, -1e30)
        mask[index, :, :tile] = hidden
        mask[index, :, tile:] = hidden
    pairs = keys.shape[1] // head
    factor = scale * 1.4426950408889634

    def pair_of(index):
        return [slice((2 * index + i) * head, (2 * index + i + 1) * head) for i in range(2)]

    def against(count):
        def within(chunk):
            return pl.ds(pl.multiple_of((place - (count - 1) + chunk) * tile, tile), tile)

        def query(index):
            return jnp.concatenate([q_ref[0, rows, :] for rows in pair_of(index)], axis=1)

        def score(index, chunk, queries):
            columns = slice(index * head, (index + 1) * head)
            result = jnp.dot(
                keys[within(chunk), columns], queries, preferred_element_type=jnp.float32
            )
            if chunk == count - 1:
                result = result + mask[0]
            elif chunk == 0 and count == span:
                result = result + mask[1]
            return result

        queries = query(0)
        scores = [score(0, chunk, queries) for chunk in range(count)]
        for index in range(pairs):
            top = functools.reduce(
                jnp.maximum, [jnp.max(part, axis=0, keepdims=True) for part in scores]
            )
            queries = query(index + 1) if index + 1 < pairs else None
            exponents, upcoming, total = [], [], 0.0
            for chunk, part in enumerate(scores):
                exponent = jnp.exp2((part - top) * factor)
                exponents.append(exponent)
                total = total + jnp.sum(exponent, axis=0, keepdims=True)
                if queries is not None:
                    upcoming.append(score(index + 1, chunk, queries))
            inverse = 1.0 / total
            result = 0.0
            rows = slice(index * head, (index + 1) * head)
            for chunk, exponent in enumerate(exponents):
                result = result + jnp.dot(
                    values[rows, within(chunk)],
                    (exponent * inverse).astype(jnp.bfloat16),
                    preferred_element_type=jnp.float32,
                )
            for i, here in enumerate(pair_of(index)):
                out[here, :] = result[:, i * tile : (i + 1) * tile].astype(jnp.bfloat16)
            scores = upcoming

    chunks = jnp.minimum(place + 1, span)
    for count in range(1, min(span, keys.shape[0] // tile) + 1):

        @pl.when(chunks == count)
        def _(count=count):
            against(count)


def attend(block, index, queries, keys, values, earlier):
    _, width, tokens = queries.shape
    tile = tokens // 2
    return pl.pallas_call(
        functools.partial(attend_kernel, float(MODEL_WIDTH // QUERY_HEAD_COUNT) ** (-0.5)),
        grid_spec=pltpu.PrefetchScalarGridSpec(
            num_scalar_prefetch=1,
            grid=(2,),
            in_specs=[
                pl.BlockSpec((1, width, tile), lambda t, *_: (index, 0, t)),
                whole(keys.shape),
                whole(values.shape),
            ]
            + [ANYWHERE] * len(earlier),
            out_specs=pl.BlockSpec((width, tile), lambda t, *_: (0, t)),
            scratch_shapes=[pltpu.VMEM((2, tile, 2 * tile), jnp.float32)],
        ),
        out_shape=jax.ShapeDtypeStruct((width, tokens), jnp.bfloat16),
        compiler_params=pltpu.CompilerParams(vmem_limit_bytes=VMEM_BYTES),
        cost_estimate=pl.CostEstimate(
            flops=12 * tokens * (WINDOW_LENGTH + tile) * width,
            bytes_accessed=4 * tokens * width + 4 * keys.shape[0] * keys.shape[1],
            transcendentals=0,
        ),
    )(block[None], queries, keys, values, *earlier)


def output_kernel(count, table, *refs):
    parts, pieces, (out, squares, held, row_held) = refs[:8], refs[8 : 8 + count], refs[8 + count :]
    depth = parts[0].shape[0]

    @pl.when(pl.program_id(0) == 0)
    def _():
        for index, part in enumerate(parts):
            held[index * depth : (index + 1) * depth, :] = part[...]
        squares[...] = jnp.zeros_like(squares)

    for index, piece in enumerate(pieces):
        there = pl.ds(pl.multiple_of(table[index], 128), piece.shape[1])
        row_held[:, there] = piece[...]
    product = jnp.dot(row_held[...], held[...], preferred_element_type=jnp.float32)
    out[...] = product
    squares[...] += jnp.sum(jnp.square(product), axis=0, keepdims=True)


def output_product(table, parts, pieces):
    depth, tokens = parts[0].shape
    width = pieces[0][0].shape[0]
    full = 8 * depth
    tile = width // 4

    def rows(column, columns):
        return pl.BlockSpec((tile, columns), lambda t, *_: (t, column))

    return pl.pallas_call(
        functools.partial(output_kernel, len(pieces)),
        grid_spec=pltpu.PrefetchScalarGridSpec(
            num_scalar_prefetch=1,
            grid=(width // tile,),
            in_specs=[whole((depth, tokens))] * 8
            + [rows(column, columns) for _, column, columns in pieces],
            out_specs=[pl.BlockSpec((tile, tokens), lambda t, *_: (t, 0)), whole((1, tokens))],
            scratch_shapes=[
                pltpu.VMEM((full, tokens), jnp.bfloat16),
                pltpu.VMEM((tile, full), jnp.bfloat16),
            ],
        ),
        out_shape=[
            jax.ShapeDtypeStruct((width, tokens), jnp.float32),
            jax.ShapeDtypeStruct((1, tokens), jnp.float32),
        ],
        compiler_params=pltpu.CompilerParams(vmem_limit_bytes=VMEM_BYTES),
        cost_estimate=pl.CostEstimate(
            flops=2 * tokens * full * width,
            bytes_accessed=2 * full * (tokens + width) + 4 * tokens * width,
            transcendentals=0,
        ),
    )(table, *parts, *(piece for piece, _, _ in pieces))


def middle_form(
    stream_in,
    in_gain,
    query_weight,
    key_matrix,
    value_matrix,
    query_gain,
    key_norm_gain,
    output_weight,
    post_gain,
):
    stream = stream_in.T
    features, tokens = stream.shape
    head = query_gain.shape[0]
    row = lax.axis_index("row")
    group = lax.axis_index("groups")
    place = lax.axis_index("col") * 2 + lax.axis_index("sub")
    upper = (row >= 2).astype(jnp.int32)
    in_middle = (row == 1) | (row == 2)
    near_block, cross_block, far_block = 3 * upper, 3 - row, 3 - 3 * upper
    blocks = (row, near_block, cross_block, far_block)
    slot = lambda block: jnp.bitwise_xor(place, block)
    ints = lambda *values: jnp.stack([jnp.asarray(v, jnp.int32) for v in values])
    beside = [(0, 1), (1, 0), (2, 3), (3, 2)]
    beyond = [(0, 2), (1, 0), (2, 3), (3, 1)]
    outside = [(0, 1), (1, 3), (2, 0), (3, 2)]
    middles, ends = (1, 2), (0, 3)

    half = query_weight.shape[1] // 2
    quarter = key_matrix.shape[1] // 2

    def side(which):
        queries = lax.dynamic_slice_in_dim(query_weight, which * half, half, axis=1)
        keys = lax.dynamic_slice_in_dim(key_matrix, which * quarter, quarter, axis=1)
        values = lax.dynamic_slice_in_dim(value_matrix, which * quarter, quarter, axis=1)
        return queries, jnp.concatenate([keys, values], axis=1)

    own_queries, own_pairs = side(upper)
    own_side = jnp.where(group == 0, own_queries, own_pairs)
    other_side = jnp.where(group == 0, *side(1 - upper))
    turned = output_weight.T
    depth = turned.shape[1] // 2
    mine = lax.dynamic_slice_in_dim(turned, group * depth, depth, axis=1)
    theirs = lax.dynamic_slice_in_dim(turned, (1 - group) * depth, depth, axis=1)

    gain_rows = in_gain.reshape(4, features)
    gain = jnp.concatenate(
        [lax.dynamic_slice_in_dim(gain_rows, slot(j), 1, axis=0) for j in range(4)], axis=0
    )[:, :, None]
    arrival = lambda block: jnp.where(
        block == row, 0, jnp.where(block == near_block, 1, jnp.where(block == far_block, 2, 3))
    )
    order = ints(*(arrival(slot(j)) for j in range(4)))

    positions = jnp.arange(4 * tokens, dtype=jnp.int32).astype(jnp.float32)
    cosine, sine = rotary_tables(positions, head)
    spread = lambda gains: jnp.broadcast_to(gains[:, None], (head, head))
    tables = (spread(query_gain), spread(key_norm_gain), cosine.T, sine.T)

    x_cross = exchanged(stream, middles)
    x_near = lax.ppermute(stream, "row", beside)
    own_col = swapped(stream, "col")
    own_sub = swapped(stream, "sub")
    x_cross, x_near, own_col, own_side, other_side, mine = settle(
        x_cross, x_near, own_col, own_side, other_side, mine
    )

    x_far = exchanged(x_near, middles)
    w_near = lax.ppermute(own_side, "row", beside)
    near_col = swapped(x_near, "col")
    own_both = swapped(own_col, "sub")
    near_sub = swapped(x_near, "sub")
    own_pieces = (stream[None], own_sub[None], own_col[None], own_both[None])
    pair_block = jnp.bitwise_xor(row, 1)
    place_table = ints(
        *(
            (2 * slot(block) + jnp.bitwise_xor(which, upper)) * depth
            for block, which in (
                (row, 0),
                (row, 1),
                (pair_block, group),
                (pair_block, 1 - group),
                (3 - pair_block, group),
                (3 - pair_block, 1 - group),
                (3 - row, group),
                (3 - row, 1 - group),
            )
        )
    )
    order, place_table, *tables = settle(order, place_table, *tables)
    normed = norm_block(order, own_pieces, 0, gain, 0, None)
    x_far, w_near, near_col, other_side, normed, x_cross, mine = settle(
        x_far, w_near, near_col, other_side, normed, x_cross, mine
    )
    w_cross = exchanged(other_side, middles)
    cross_col = swapped(x_cross, "col")
    o_in = lax.ppermute(mine, "row", beside)
    w_near_y = swapped(w_near, "groups")
    near_both = swapped(near_col, "sub")
    cross_sub = swapped(x_cross, "sub")
    far_sub = swapped(x_far, "sub")
    near_pieces = (x_near[None], near_sub[None], near_col[None], near_both[None])
    normed = norm_block(order, near_pieces, 0, gain, 1, normed)
    w_cross, w_near_y, cross_col, x_far, normed, other_side, theirs, cross_sub, o_in = settle(
        w_cross, w_near_y, cross_col, x_far, normed, other_side, theirs, cross_sub, o_in
    )

    w_far = lax.ppermute(other_side, "row", beyond)
    far_col = swapped(x_far, "col")
    cross_both = swapped(cross_col, "sub")
    w_cross_y = swapped(w_cross, "groups")
    cross_pieces = (x_cross[None], cross_sub[None], cross_col[None], cross_both[None])
    normed = norm_block(order, cross_pieces, 0, gain, 2, normed)
    early_table = ints(0, 0, 0, half, features, group * half, features, (1 - group) * half)
    early_pieces = (own_queries, own_pairs, w_near, w_near_y)
    total = project_early(early_table, normed, early_pieces, 0, 3, None)
    w_far, far_col, w_cross_y, total, theirs, o_in = settle(
        w_far, far_col, w_cross_y, total, theirs, o_in
    )

    w_far_y = swapped(w_far, "groups")
    far_both = swapped(far_col, "sub")
    o_far = exchanged(o_in, middles)
    o_in_rest = lax.ppermute(theirs, "row", beside)
    far_pieces = (x_far[None], far_sub[None], far_col[None], far_both[None])
    normed = norm_block(order, far_pieces, 0, gain, 3, normed)
    total = project_early(early_table, normed, early_pieces, 3, 1, total)
    w_far_y, o_far, total, o_in_rest = settle(w_far_y, o_far, total, o_in_rest)
    o_cross = exchanged(mine, middles)
    o_far_y = swapped(o_far, "groups")
    here, there = group * half, (1 - group) * half
    queries, keys, values = project_late(
        ints(0, here, 0, there, features, here, features, there, *blocks),
        normed,
        (w_far, w_far_y, w_cross, w_cross_y),
        total,
        tables,
    )

    def attended(index, *earlier):
        return attend(blocks[index].astype(jnp.int32), index, queries, keys, values, earlier)

    far_part = attended(3)
    got_far = exchanged(far_part, middles)
    near_part = attended(1, far_part, o_far_y)
    near_col, near_sub = swapped(near_part, "col"), swapped(near_part, "sub")
    o_cross_y = swapped(after(o_cross, far_part), "groups")
    cross_part = attended(2, near_part)
    got_cross = exchanged(cross_part, middles)
    own_part = attended(0, cross_part)
    got_far = after(got_far, cross_part, near_col)
    far_col, far_sub = swapped(got_far, "col"), swapped(got_far, "sub")
    far_both = swapped(after(far_col, got_cross, own_part, o_cross_y), "sub")
    cross_col, cross_sub = swapped(got_cross, "col"), swapped(got_cross, "sub")
    own_col, own_sub = swapped(own_part, "col"), swapped(own_part, "sub")

    pieces = (turned, turned, o_in, o_in_rest, o_far, o_far_y, o_cross, o_cross_y)
    out_pieces = [(piece, int(index == 1), depth) for index, piece in enumerate(pieces)]

    def projected(table, residual, this_side, that_side, *earlier):
        parts = [part for pair in zip(this_side, that_side) for part in pair]
        branch, squares = output_product(table, parts, out_pieces)
        diagonal = lax.ppermute(squares, ("col", "sub"), [(0, 3), (1, 2), (2, 1), (3, 0)])
        total = squares + swapped(squares, "sub") + swapped(squares, "col") + diagonal
        if earlier:
            total = after(total, *earlier)
        scaled = branch * lax.rsqrt(total / MODEL_WIDTH + EPSILON) * post_gain[:, None]
        return (residual.astype(jnp.float32) + scaled).astype(jnp.bfloat16), branch

    near_out, near_branch = projected(
        after(place_table, own_part),
        x_near,
        (near_part, near_sub, near_col, swapped(near_col, "sub")),
        (got_far, far_sub, far_col, far_both),
        cross_col,
    )
    outer = lax.ppermute(near_out, "row", beside)
    own_out, _ = projected(
        after(place_table, near_branch),
        stream,
        (own_part, own_sub, own_col, swapped(own_col, "sub")),
        (got_cross, cross_sub, cross_col, swapped(cross_col, "sub")),
    )
    return jnp.where(in_middle, own_out, outer).T


def on_device(*args):
    stream_in, _, query_weight, key_matrix, value_matrix, query_gain, *_ = args
    sizes = tuple(lax.axis_size(name) for name in ("groups", "row", "col", "sub"))
    tokens, head = stream_in.shape[0], query_gain.shape[0]
    fits = (
        sizes == (2, 4, 2, 2)
        and head == 128
        and tokens % 256 == 0
        and WINDOW_LENGTH % (tokens // 2) == 0
        and key_matrix.shape[1] % (2 * head) == 0
        and query_weight.shape[1] == 2 * key_matrix.shape[1]
        and value_matrix.shape[1] == key_matrix.shape[1]
    )
    return middle_form(*args) if fits else general_form(*args)


def solution(mesh):
    placed = (
        P(("groups", "row"), ("col", "sub")),
        P(),
        P("row", ("col", "sub")),
        P("row", ("col", "sub")),
        P("row", ("col", "sub")),
        P(),
        P(),
        P("row", ("col", "sub")),
        P(("col", "sub")),
    )
    return jax.shard_map(
        on_device,
        mesh=mesh,
        in_specs=placed,
        out_specs=P(("groups", "row"), ("col", "sub")),
        check_vma=False,
    )
```

```python
import functools

import jax
import jax.numpy as jnp
from jax import lax
from jax.experimental import pallas as pl
from jax.experimental.pallas import tpu as pltpu
from jax.sharding import PartitionSpec as P

MODEL_WIDTH = 5376
QUERY_HEAD_COUNT = 32
WINDOW_LENGTH = 1024


EPSILON = 1e-06
MIB = 1024 * 1024


def shifted(x, axis, by):
    count = lax.axis_size(axis)
    pairs = [(i, i + by) for i in range(count) if 0 <= i + by < count]
    return lax.ppermute(x, axis, pairs)


def root_mean_scale(values, gain):
    return values * lax.rsqrt(jnp.mean(values * values, axis=-1, keepdims=True) + EPSILON) * gain


def rotary_tables(token_positions, size):
    half_dim = size // 2
    inverse = 10000.0 ** (-(jnp.arange(half_dim, dtype=jnp.float32) * 2.0) / size)
    angles = token_positions[:, None] * inverse[None, :]
    return jnp.cos(angles), jnp.sin(angles)


def apply_rotary(tensor, token_positions):
    half_dim = tensor.shape[-1] // 2
    cosine, sine_part = rotary_tables(token_positions, tensor.shape[-1])
    cosine, sine_part = cosine[:, None, :], sine_part[:, None, :]
    first_half = tensor[..., :half_dim]
    second_half = tensor[..., half_dim:]
    return jnp.concatenate(
        [
            first_half * cosine - second_half * sine_part,
            second_half * cosine + first_half * sine_part,
        ],
        axis=-1,
    )


def general_form(
    stream_in,
    in_gain,
    query_weight,
    key_matrix,
    value_matrix,
    query_gain,
    key_norm_gain,
    output_weight,
    post_gain,
):
    token_rows = lax.all_gather(stream_in, ("col", "sub"), axis=1, tiled=True)
    tokens = token_rows.shape[0]
    normed = root_mean_scale(token_rows.astype(jnp.float32), in_gain).astype(jnp.bfloat16)

    def add_panel(panel_piece):
        return jnp.dot(normed, panel_piece, preferred_element_type=jnp.float32)

    query_proj = add_panel(lax.all_gather(query_weight, "row", axis=0, tiled=True))
    projected_keys = add_panel(lax.all_gather(key_matrix, "row", axis=0, tiled=True))
    projected_values = add_panel(lax.all_gather(value_matrix, "row", axis=0, tiled=True))
    head_size = query_gain.shape[0]
    query_heads = query_weight.shape[1] // head_size
    pair_heads = key_matrix.shape[1] // head_size
    group_count = query_heads // pair_heads
    scale_factor = float(MODEL_WIDTH // QUERY_HEAD_COUNT) ** (-0.5)
    row_index = lax.axis_index("row")
    query_places = row_index * tokens + jnp.arange(tokens, dtype=jnp.int32)
    query_rot = apply_rotary(
        root_mean_scale(query_proj.reshape(tokens, query_heads, head_size), query_gain),
        query_places.astype(jnp.float32),
    ).astype(jnp.bfloat16)
    rotary_keys = apply_rotary(
        root_mean_scale(projected_keys.reshape(tokens, pair_heads, head_size), key_norm_gain),
        query_places.astype(jnp.float32),
    ).astype(jnp.bfloat16)
    keys_flat = rotary_keys.reshape(tokens, pair_heads * head_size)
    values_flat = projected_values.astype(jnp.bfloat16)
    shards_back = min(WINDOW_LENGTH // tokens, lax.axis_size("row") - 1)
    band_length = (shards_back + 1) * tokens
    key_parts = [keys_flat]
    value_parts = [values_flat]
    for offset in range(1, shards_back + 1):
        keys_prior, values_prior = shifted((keys_flat, values_flat), "row", offset)
        key_parts = [keys_prior] + key_parts
        value_parts = [values_prior] + value_parts
    keys_band = jnp.concatenate(key_parts, axis=0)
    values_band = jnp.concatenate(value_parts, axis=0)
    key_places = (row_index - shards_back) * tokens + jnp.arange(band_length, dtype=jnp.int32)
    distance = query_places[:, None] - key_places[None, :]
    visible = (distance >= 0) & (distance < WINDOW_LENGTH) & (key_places[None, :] >= 0)
    grouped = query_rot.reshape(tokens, pair_heads, group_count, head_size)
    scores = (
        jnp.einsum(
            "qhgd,shd->hgqs",
            grouped,
            keys_band.reshape(band_length, pair_heads, head_size),
            preferred_element_type=jnp.float32,
        )
        * scale_factor
    )
    scores = jnp.where(visible, scores, -1e30)
    row_max = jnp.max(scores, axis=-1, keepdims=True)
    exponent = jnp.exp(scores - row_max)
    weights = (exponent / jnp.sum(exponent, axis=-1, keepdims=True)).astype(jnp.bfloat16)
    attended = jnp.einsum(
        "hgqs,shd->qhgd",
        weights,
        values_band.reshape(band_length, pair_heads, head_size),
        preferred_element_type=jnp.float32,
    )
    heads_out = attended.reshape(tokens, query_heads * head_size).astype(jnp.bfloat16)
    head_rows = lax.all_gather(heads_out, ("col", "sub"), axis=1, tiled=True)
    branch = jnp.dot(
        head_rows,
        lax.all_gather(output_weight, "row", axis=0, tiled=True),
        preferred_element_type=jnp.float32,
    )
    squares = lax.psum(jnp.sum(branch * branch, axis=-1), ("col", "sub"))
    scaled = branch * lax.rsqrt(squares[:, None] / MODEL_WIDTH + EPSILON) * post_gain
    return (stream_in.astype(jnp.float32) + scaled).astype(jnp.bfloat16)


def swapped(x, axis, rows=None):
    if rows is None or axis == "sub":
        return lax.ppermute(x, axis, [(0, 1), (1, 0)])
    count = lax.axis_size("row")
    names = ("groups", "row", "sub") if axis == "groups" else ("row", "col", "sub")
    row_stride = 2 if axis == "groups" else 4
    stride = 2 * count if axis == "groups" else 2
    pairs = []
    for device in range(4 * count):
        step = stride if (device // row_stride) % count in rows else 1
        pairs.append((device, device + step if (device // step) % 2 == 0 else device - step))
    return lax.ppermute(x, names, pairs)


def exchanged(x, planes):
    other = dict(zip(planes, planes[::-1]))
    pairs = [
        (2 * r + s, 2 * other[r] + s if r in other else 2 * r + 1 - s)
        for r in range(lax.axis_size("row"))
        for s in range(2)
    ]
    return lax.ppermute(x, ("row", "sub"), pairs)


def after(x, *earlier):
    return lax.optimization_barrier((x, *earlier))[0]


def settle(*values):
    return lax.optimization_barrier(values)


def whole(shape):
    return pl.BlockSpec(shape, lambda *_: (0,) * len(shape))


ANYWHERE = pl.BlockSpec(memory_space=pl.ANY)
LITTLE = pl.CostEstimate(flops=0, bytes_accessed=0, transcendentals=0)


def norm_kernel(table, *refs):
    *pieces, gain, out = refs[-6:]
    depth = pieces[0].shape[1]
    squares = sum(
        jnp.sum(jnp.square(p[0].astype(jnp.float32)), axis=0, keepdims=True) for p in pieces
    )
    scale = lax.rsqrt(squares / MODEL_WIDTH + EPSILON)
    for index, piece in enumerate(pieces):
        rows = pl.ds(pl.multiple_of(table[index] * depth, depth), depth)
        out[0, rows, :] = (piece[0].astype(jnp.float32) * scale * gain[index]).astype(jnp.bfloat16)


def norm_block(table, pieces, which, gain, index, held):
    _, depth, tokens = pieces[0].shape
    lanes = tokens // 2
    shape = (4, 4 * depth, tokens)
    before = () if held is None else (held,)
    return pl.pallas_call(
        norm_kernel,
        grid_spec=pltpu.PrefetchScalarGridSpec(
            num_scalar_prefetch=1,
            grid=(tokens // lanes,),
            in_specs=[ANYWHERE] * len(before)
            + [pl.BlockSpec((1, depth, lanes), lambda t, *_: (which, 0, t))] * 4
            + [whole((4, depth, 1))],
            out_specs=pl.BlockSpec((1, 4 * depth, lanes), lambda t, *_: (index, 0, t)),
        ),
        out_shape=jax.ShapeDtypeStruct(shape, jnp.bfloat16),
        input_output_aliases={1: 0} if before else {},
        compiler_params=pltpu.CompilerParams(vmem_limit_bytes=44 * MIB),
        cost_estimate=pl.CostEstimate(
            flops=40 * depth * tokens, bytes_accessed=16 * depth * tokens, transcendentals=0
        ),
    )(table, *before, *pieces, gain)


def order_pieces(table, pieces, ordered):
    base = 0
    for index, piece in enumerate(pieces):
        depth, width = piece.shape
        rows = pl.ds(pl.multiple_of(table[2 * index], 16), depth)
        columns = pl.ds(pl.multiple_of(table[2 * index + 1], width), width)
        ordered[rows, columns] = piece[...]


def project_early_kernel(count, table, normed, *refs):
    pieces, out, ordered = refs[:count], refs[-2], refs[-1]

    @pl.when(pl.program_id(0) == 0)
    def _():
        order_pieces(table, pieces, ordered)

    out[0] = lax.dot_general(
        ordered[...], normed[0], (((0,), (0,)), ((), ())), preferred_element_type=jnp.float32
    )


def project_early(table, normed, pieces, first, blocks, held):
    _, features, tokens = normed.shape
    width = 2 * pieces[0].shape[1]
    before = () if held is None else (held,)
    return pl.pallas_call(
        functools.partial(project_early_kernel, len(pieces)),
        grid_spec=pltpu.PrefetchScalarGridSpec(
            num_scalar_prefetch=1,
            grid=(blocks,),
            in_specs=[pl.BlockSpec((1, features // 2, tokens), lambda i, t: (first + i, 0, 0))]
            + [whole(p.shape) for p in pieces]
            + [ANYWHERE] * len(before),
            out_specs=pl.BlockSpec((1, width, tokens), lambda i, t: (first + i, 0, 0)),
            scratch_shapes=[pltpu.VMEM((features // 2, width), jnp.bfloat16)],
        ),
        out_shape=jax.ShapeDtypeStruct((4, width, tokens), jnp.float32),
        input_output_aliases={2 + len(pieces): 0} if before else {},
        compiler_params=pltpu.CompilerParams(vmem_limit_bytes=44 * MIB),
        cost_estimate=pl.CostEstimate(
            flops=2 * blocks * tokens * features // 2 * width,
            bytes_accessed=blocks * features * tokens + features * width + 4 * blocks * width * tokens,
            transcendentals=0,
        ),
    )(table, normed, *pieces, *before)


def project_late_kernel(count, table, normed, *refs):
    pieces, refs = refs[:count], refs[count:]
    early, q_gain, k_gain, cosine, sine, q_out, k_out, v_out, total, ordered = refs

    @pl.when(pl.program_id(0) == 0)
    def _():
        order_pieces(table, pieces, ordered)

    total[...] = early[0] + lax.dot_general(
        ordered[...], normed[0], (((0,), (0,)), ((), ())), preferred_element_type=jnp.float32
    )
    head = q_gain.shape[0]
    half = head // 2
    width = q_out.shape[1]
    cos, sin = cosine[...], sine[...]

    def rotated(start, head_gain):
        values = total[start : start + head, :]
        values = (
            values
            * lax.rsqrt(jnp.mean(values * values, axis=0, keepdims=True) + EPSILON)
            * head_gain[:, :1]
        )
        first, second = values[:half], values[half:]
        return jnp.concatenate(
            [first * cos - second * sin, second * cos + first * sin], axis=0
        ).astype(jnp.bfloat16)

    for start in range(0, width, head):
        q_out[0, start : start + head, :] = rotated(start, q_gain)
    for start in range(0, width // 2, head):
        k_out[:, start : start + head] = rotated(width + start, k_gain).T
    v_out[...] = total[width + width // 2 :, :].astype(jnp.bfloat16)


def project_late(table, normed, pieces, early, extras):
    blocks, features, tokens = normed.shape
    width = early.shape[1] // 2
    head = extras[0].shape[0]
    half = head // 2
    count = len(pieces)
    turn = pl.BlockSpec((half, tokens), lambda i, t: (0, t[2 * count + i]))
    return pl.pallas_call(
        functools.partial(project_late_kernel, count),
        grid_spec=pltpu.PrefetchScalarGridSpec(
            num_scalar_prefetch=1,
            grid=(blocks,),
            in_specs=[pl.BlockSpec((1, features // 2, tokens), lambda i, t: (i, 1, 0))]
            + [whole(p.shape) for p in pieces]
            + [
                pl.BlockSpec((1, 2 * width, tokens), lambda i, t: (i, 0, 0)),
                whole((head, head)),
                whole((head, head)),
                turn,
                turn,
            ],
            out_specs=[
                pl.BlockSpec((1, width, tokens), lambda i, t: (i, 0, 0)),
                pl.BlockSpec((tokens, width // 2), lambda i, t: (t[2 * count + i], 0)),
                pl.BlockSpec((width // 2, tokens), lambda i, t: (0, t[2 * count + i])),
            ],
            scratch_shapes=[
                pltpu.VMEM((2 * width, tokens), jnp.float32),
                pltpu.VMEM((features // 2, 2 * width), jnp.bfloat16),
            ],
        ),
        out_shape=[
            jax.ShapeDtypeStruct((blocks, width, tokens), jnp.bfloat16),
            jax.ShapeDtypeStruct((blocks * tokens, width // 2), jnp.bfloat16),
            jax.ShapeDtypeStruct((width // 2, blocks * tokens), jnp.bfloat16),
        ],
        compiler_params=pltpu.CompilerParams(vmem_limit_bytes=48 * MIB),
        cost_estimate=pl.CostEstimate(
            flops=2 * blocks * tokens * features * width,
            bytes_accessed=blocks * features * tokens + 2 * features * width + 8 * blocks * width * tokens,
            transcendentals=0,
        ),
    )(table, normed, *pieces, early, *extras)


def attend_kernel(scale, table, q_ref, keys, values, *refs):
    out, mask = refs[-2:]
    head = 128
    tile = out.shape[1]
    span = WINDOW_LENGTH // tile + 1
    place = table[0] * 2 + pl.program_id(0)
    later = lax.broadcasted_iota(jnp.int32, (tile, tile), 1) >= lax.broadcasted_iota(
        jnp.int32, (tile, tile), 0
    )
    for index, seen in enumerate((later, jnp.logical_not(later))):
        hidden = jnp.where(seen, 0.0, -1e30)
        mask[index, :, :tile] = hidden
        mask[index, :, tile:] = hidden
    pairs = keys.shape[1] // head
    factor = scale * 1.4426950408889634

    def pair_of(index):
        return [slice((2 * index + i) * head, (2 * index + i + 1) * head) for i in range(2)]

    def against(count):
        def within(chunk):
            return pl.ds(pl.multiple_of((place - (count - 1) + chunk) * tile, tile), tile)

        def query(index):
            return jnp.concatenate([q_ref[0, rows, :] for rows in pair_of(index)], axis=1)

        def score(index, chunk, queries):
            columns = slice(index * head, (index + 1) * head)
            result = jnp.dot(
                keys[within(chunk), columns], queries, preferred_element_type=jnp.float32
            )
            if chunk == count - 1:
                result = result + mask[0]
            elif chunk == 0 and count == span:
                result = result + mask[1]
            return result

        queries = query(0)
        scores = [score(0, chunk, queries) for chunk in range(count)]
        for index in range(pairs):
            top = functools.reduce(
                jnp.maximum, [jnp.max(part, axis=0, keepdims=True) for part in scores]
            )
            queries = query(index + 1) if index + 1 < pairs else None
            exponents, upcoming, total = [], [], 0.0
            for chunk, part in enumerate(scores):
                exponent = jnp.exp2((part - top) * factor)
                exponents.append(exponent)
                total = total + jnp.sum(exponent, axis=0, keepdims=True)
                if queries is not None:
                    upcoming.append(score(index + 1, chunk, queries))
            inverse = 1.0 / total
            result = 0.0
            rows = slice(index * head, (index + 1) * head)
            for chunk, exponent in enumerate(exponents):
                result = result + jnp.dot(
                    values[rows, within(chunk)],
                    (exponent * inverse).astype(jnp.bfloat16),
                    preferred_element_type=jnp.float32,
                )
            for i, here in enumerate(pair_of(index)):
                out[here, :] = result[:, i * tile : (i + 1) * tile].astype(jnp.bfloat16)
            scores = upcoming

    chunks = jnp.minimum(place + 1, span)
    for count in range(1, min(span, keys.shape[0] // tile) + 1):

        @pl.when(chunks == count)
        def _(count=count):
            against(count)


def attend(block, index, queries, keys, values, earlier):
    _, width, tokens = queries.shape
    tile = tokens // 2
    return pl.pallas_call(
        functools.partial(attend_kernel, float(MODEL_WIDTH // QUERY_HEAD_COUNT) ** (-0.5)),
        grid_spec=pltpu.PrefetchScalarGridSpec(
            num_scalar_prefetch=1,
            grid=(2,),
            in_specs=[
                pl.BlockSpec((1, width, tile), lambda t, *_: (index, 0, t)),
                whole(keys.shape),
                whole(values.shape),
            ]
            + [ANYWHERE] * len(earlier),
            out_specs=pl.BlockSpec((width, tile), lambda t, *_: (0, t)),
            scratch_shapes=[pltpu.VMEM((2, tile, 2 * tile), jnp.float32)],
        ),
        out_shape=jax.ShapeDtypeStruct((width, tokens), jnp.bfloat16),
        compiler_params=pltpu.CompilerParams(vmem_limit_bytes=28 * MIB),
        cost_estimate=pl.CostEstimate(
            flops=12 * tokens * (WINDOW_LENGTH + tile) * width,
            bytes_accessed=4 * tokens * width + 4 * keys.shape[0] * keys.shape[1],
            transcendentals=0,
        ),
    )(block[None], queries, keys, values, *earlier)


def output_kernel(count, table, *refs):
    parts, pieces, (out, squares, held, row_held) = refs[:8], refs[8 : 8 + count], refs[8 + count :]
    depth = parts[0].shape[0]

    @pl.when(pl.program_id(0) == 0)
    def _():
        for index, part in enumerate(parts):
            held[index * depth : (index + 1) * depth, :] = part[...]
        squares[...] = jnp.zeros_like(squares)

    for index, piece in enumerate(pieces):
        there = pl.ds(pl.multiple_of(table[index], 128), piece.shape[1])
        row_held[:, there] = piece[...]
    product = jnp.dot(row_held[...], held[...], preferred_element_type=jnp.float32)
    out[...] = product
    squares[...] += jnp.sum(jnp.square(product), axis=0, keepdims=True)


def output_product(table, parts, pieces):
    depth, tokens = parts[0].shape
    width = pieces[0][0].shape[0]
    full = 8 * depth
    tile = width // 4

    def rows(column, columns):
        return pl.BlockSpec((tile, columns), lambda t, *_: (t, column))

    return pl.pallas_call(
        functools.partial(output_kernel, len(pieces)),
        grid_spec=pltpu.PrefetchScalarGridSpec(
            num_scalar_prefetch=1,
            grid=(width // tile,),
            in_specs=[whole((depth, tokens))] * 8
            + [rows(column, columns) for _, column, columns in pieces],
            out_specs=[pl.BlockSpec((tile, tokens), lambda t, *_: (t, 0)), whole((1, tokens))],
            scratch_shapes=[
                pltpu.VMEM((full, tokens), jnp.bfloat16),
                pltpu.VMEM((tile, full), jnp.bfloat16),
            ],
        ),
        out_shape=[
            jax.ShapeDtypeStruct((width, tokens), jnp.float32),
            jax.ShapeDtypeStruct((1, tokens), jnp.float32),
        ],
        compiler_params=pltpu.CompilerParams(vmem_limit_bytes=32 * MIB),
        cost_estimate=pl.CostEstimate(
            flops=2 * tokens * full * width,
            bytes_accessed=2 * full * (tokens + width) + 4 * tokens * width,
            transcendentals=0,
        ),
    )(table, *parts, *(piece for piece, _, _ in pieces))


def middle_form(
    stream_in,
    in_gain,
    query_weight,
    key_matrix,
    value_matrix,
    query_gain,
    key_norm_gain,
    output_weight,
    post_gain,
):
    stream = stream_in.T
    features, tokens = stream.shape
    head = query_gain.shape[0]
    row = lax.axis_index("row")
    group = lax.axis_index("groups")
    place = lax.axis_index("col") * 2 + lax.axis_index("sub")
    upper = (row >= 2).astype(jnp.int32)
    in_middle = (row == 1) | (row == 2)
    near_block, cross_block, far_block = 3 * upper, 3 - row, 3 - 3 * upper
    blocks = (row, near_block, cross_block, far_block)
    slot = lambda block: jnp.bitwise_xor(place, block)
    ints = lambda *values: jnp.stack([jnp.asarray(v, jnp.int32) for v in values])
    beside = [(0, 1), (1, 0), (2, 3), (3, 2)]
    beyond = [(0, 2), (1, 0), (2, 3), (3, 1)]
    outside = [(0, 1), (1, 3), (2, 0), (3, 2)]
    middles, ends = (1, 2), (0, 3)

    half = query_weight.shape[1] // 2
    quarter = key_matrix.shape[1] // 2

    def side(which):
        queries = lax.dynamic_slice_in_dim(query_weight, which * half, half, axis=1)
        keys = lax.dynamic_slice_in_dim(key_matrix, which * quarter, quarter, axis=1)
        values = lax.dynamic_slice_in_dim(value_matrix, which * quarter, quarter, axis=1)
        return queries, jnp.concatenate([keys, values], axis=1)

    own_queries, own_pairs = side(upper)
    own_side = jnp.where(group == 0, own_queries, own_pairs)
    other_side = jnp.where(group == 0, *side(1 - upper))
    turned = output_weight.T
    depth = turned.shape[1] // 2
    mine = lax.dynamic_slice_in_dim(turned, group * depth, depth, axis=1)
    theirs = lax.dynamic_slice_in_dim(turned, (1 - group) * depth, depth, axis=1)

    gain_rows = in_gain.reshape(4, features)
    gain = jnp.concatenate(
        [lax.dynamic_slice_in_dim(gain_rows, slot(j), 1, axis=0) for j in range(4)], axis=0
    )[:, :, None]
    arrival = lambda block: jnp.where(
        block == row, 0, jnp.where(block == near_block, 1, jnp.where(block == far_block, 2, 3))
    )
    order = ints(*(arrival(slot(j)) for j in range(4)))

    positions = jnp.arange(4 * tokens, dtype=jnp.int32).astype(jnp.float32)
    cosine, sine = rotary_tables(positions, head)
    spread = lambda gains: jnp.broadcast_to(gains[:, None], (head, head))
    tables = (spread(query_gain), spread(key_norm_gain), cosine.T, sine.T)

    x_cross = exchanged(stream, middles)
    x_near = lax.ppermute(stream, "row", beside)
    own_col = swapped(stream, "col")
    own_sub = swapped(stream, "sub")
    x_cross, x_near, own_col, own_side, other_side, mine = settle(
        x_cross, x_near, own_col, own_side, other_side, mine
    )

    x_far = exchanged(x_near, middles)
    w_near = lax.ppermute(own_side, "row", beside)
    near_col = swapped(x_near, "col")
    own_both = swapped(own_col, "sub")
    near_sub = swapped(x_near, "sub")
    own_pieces = (stream[None], own_sub[None], own_col[None], own_both[None])
    pair_block = jnp.bitwise_xor(row, 1)
    place_table = ints(
        *(
            (2 * slot(block) + jnp.bitwise_xor(which, upper)) * depth
            for block, which in (
                (row, 0),
                (row, 1),
                (pair_block, group),
                (pair_block, 1 - group),
                (3 - pair_block, group),
                (3 - pair_block, 1 - group),
                (3 - row, group),
                (3 - row, 1 - group),
            )
        )
    )
    order, place_table, *tables = settle(order, place_table, *tables)
    normed = norm_block(order, own_pieces, 0, gain, 0, None)
    x_far, w_near, near_col, other_side, normed, x_cross, mine = settle(
        x_far, w_near, near_col, other_side, normed, x_cross, mine
    )
    w_cross = exchanged(other_side, middles)
    cross_col = swapped(x_cross, "col")
    o_in = lax.ppermute(mine, "row", beside)
    w_near_y = swapped(w_near, "groups")
    near_both = swapped(near_col, "sub")
    cross_sub = swapped(x_cross, "sub")
    far_sub = swapped(x_far, "sub")
    near_pieces = (x_near[None], near_sub[None], near_col[None], near_both[None])
    normed = norm_block(order, near_pieces, 0, gain, 1, normed)
    w_cross, w_near_y, cross_col, x_far, normed, other_side, theirs, cross_sub, o_in = settle(
        w_cross, w_near_y, cross_col, x_far, normed, other_side, theirs, cross_sub, o_in
    )

    w_far = lax.ppermute(other_side, "row", beyond)
    far_col = swapped(x_far, "col")
    cross_both = swapped(cross_col, "sub")
    w_cross_y = swapped(w_cross, "groups")
    cross_pieces = (x_cross[None], cross_sub[None], cross_col[None], cross_both[None])
    normed = norm_block(order, cross_pieces, 0, gain, 2, normed)
    early_table = ints(0, 0, 0, half, features, group * half, features, (1 - group) * half)
    early_pieces = (own_queries, own_pairs, w_near, w_near_y)
    total = project_early(early_table, normed, early_pieces, 0, 3, None)
    w_far, far_col, w_cross_y, total, theirs, o_in = settle(
        w_far, far_col, w_cross_y, total, theirs, o_in
    )

    w_far_y = swapped(w_far, "groups")
    far_both = swapped(far_col, "sub")
    o_far = exchanged(o_in, middles)
    o_in_rest = lax.ppermute(theirs, "row", beside)
    far_pieces = (x_far[None], far_sub[None], far_col[None], far_both[None])
    normed = norm_block(order, far_pieces, 0, gain, 3, normed)
    total = project_early(early_table, normed, early_pieces, 3, 1, total)
    w_far_y, o_far, total, o_in_rest = settle(w_far_y, o_far, total, o_in_rest)
    o_cross = exchanged(mine, middles)
    o_far_y = swapped(o_far, "groups")
    here, there = group * half, (1 - group) * half
    queries, keys, values = project_late(
        ints(0, here, 0, there, features, here, features, there, *blocks),
        normed,
        (w_far, w_far_y, w_cross, w_cross_y),
        total,
        tables,
    )

    def attended(index, *earlier):
        return attend(blocks[index].astype(jnp.int32), index, queries, keys, values, earlier)

    far_part = attended(3)
    got_far = exchanged(far_part, middles)
    near_part = attended(1, far_part, o_far_y)
    near_col, near_sub = swapped(near_part, "col"), swapped(near_part, "sub")
    o_cross_y = swapped(after(o_cross, far_part), "groups")
    cross_part = attended(2, near_part)
    got_cross = exchanged(cross_part, middles)
    own_part = attended(0, cross_part)
    got_far = after(got_far, cross_part, near_col)
    far_col, far_sub = swapped(got_far, "col"), swapped(got_far, "sub")
    far_both = swapped(after(far_col, got_cross, own_part, o_cross_y), "sub")
    cross_col, cross_sub = swapped(got_cross, "col"), swapped(got_cross, "sub")
    own_col, own_sub = swapped(own_part, "col"), swapped(own_part, "sub")

    pieces = (turned, turned, o_in, o_in_rest, o_far, o_far_y, o_cross, o_cross_y)
    out_pieces = [(piece, int(index == 1), depth) for index, piece in enumerate(pieces)]

    def projected(table, residual, this_side, that_side, *earlier):
        parts = [part for pair in zip(this_side, that_side) for part in pair]
        branch, squares = output_product(table, parts, out_pieces)
        diagonal = lax.ppermute(squares, ("col", "sub"), [(0, 3), (1, 2), (2, 1), (3, 0)])
        total = squares + swapped(squares, "sub") + swapped(squares, "col") + diagonal
        if earlier:
            total = after(total, *earlier)
        scaled = branch * lax.rsqrt(total / MODEL_WIDTH + EPSILON) * post_gain[:, None]
        return (residual.astype(jnp.float32) + scaled).astype(jnp.bfloat16), branch

    near_out, near_branch = projected(
        after(place_table, own_part),
        x_near,
        (near_part, near_sub, near_col, swapped(near_col, "sub")),
        (got_far, far_sub, far_col, far_both),
        cross_col,
    )
    outer = lax.ppermute(near_out, "row", beside)
    own_out, _ = projected(
        after(place_table, near_branch),
        stream,
        (own_part, own_sub, own_col, swapped(own_col, "sub")),
        (got_cross, cross_sub, cross_col, swapped(cross_col, "sub")),
    )
    return jnp.where(in_middle, own_out, outer).T


def on_device(*args):
    stream_in, _, query_weight, key_matrix, value_matrix, query_gain, *_ = args
    sizes = tuple(lax.axis_size(name) for name in ("groups", "row", "col", "sub"))
    tokens, head = stream_in.shape[0], query_gain.shape[0]
    fits = (
        sizes == (2, 4, 2, 2)
        and head == 128
        and tokens % 256 == 0
        and WINDOW_LENGTH % (tokens // 2) == 0
        and key_matrix.shape[1] % (2 * head) == 0
        and query_weight.shape[1] == 2 * key_matrix.shape[1]
        and value_matrix.shape[1] == key_matrix.shape[1]
    )
    return middle_form(*args) if fits else general_form(*args)


def solution(mesh):
    placed = (
        P(("groups", "row"), ("col", "sub")),
        P(),
        P("row", ("col", "sub")),
        P("row", ("col", "sub")),
        P("row", ("col", "sub")),
        P(),
        P(),
        P("row", ("col", "sub")),
        P(("col", "sub")),
    )
    return jax.shard_map(
        on_device,
        mesh=mesh,
        in_specs=placed,
        out_specs=P(("groups", "row"), ("col", "sub")),
        check_vma=False,
    )
```

```python
import functools

import jax
import jax.numpy as jnp
from jax import lax
from jax.experimental import pallas as pl
from jax.experimental.pallas import tpu as pltpu
from jax.sharding import PartitionSpec as P

MODEL_WIDTH = 5376
QUERY_HEAD_COUNT = 32
WINDOW_LENGTH = 1024


EPSILON = 1e-06
MIB = 1024 * 1024


def shifted(x, axis, by):
    count = lax.axis_size(axis)
    pairs = [(i, i + by) for i in range(count) if 0 <= i + by < count]
    return lax.ppermute(x, axis, pairs)


def root_mean_scale(values, gain):
    return values * lax.rsqrt(jnp.mean(values * values, axis=-1, keepdims=True) + EPSILON) * gain


def rotary_tables(token_positions, size):
    half_dim = size // 2
    inverse = 10000.0 ** (-(jnp.arange(half_dim, dtype=jnp.float32) * 2.0) / size)
    angles = token_positions[:, None] * inverse[None, :]
    return jnp.cos(angles), jnp.sin(angles)


def apply_rotary(tensor, token_positions):
    half_dim = tensor.shape[-1] // 2
    cosine, sine_part = rotary_tables(token_positions, tensor.shape[-1])
    cosine, sine_part = cosine[:, None, :], sine_part[:, None, :]
    first_half = tensor[..., :half_dim]
    second_half = tensor[..., half_dim:]
    return jnp.concatenate(
        [
            first_half * cosine - second_half * sine_part,
            second_half * cosine + first_half * sine_part,
        ],
        axis=-1,
    )


def general_form(
    stream_in,
    in_gain,
    query_weight,
    key_matrix,
    value_matrix,
    query_gain,
    key_norm_gain,
    output_weight,
    post_gain,
):
    token_rows = lax.all_gather(stream_in, ("col", "sub"), axis=1, tiled=True)
    tokens = token_rows.shape[0]
    normed = root_mean_scale(token_rows.astype(jnp.float32), in_gain).astype(jnp.bfloat16)

    def add_panel(panel_piece):
        return jnp.dot(normed, panel_piece, preferred_element_type=jnp.float32)

    query_proj = add_panel(lax.all_gather(query_weight, "row", axis=0, tiled=True))
    projected_keys = add_panel(lax.all_gather(key_matrix, "row", axis=0, tiled=True))
    projected_values = add_panel(lax.all_gather(value_matrix, "row", axis=0, tiled=True))
    head_size = query_gain.shape[0]
    query_heads = query_weight.shape[1] // head_size
    pair_heads = key_matrix.shape[1] // head_size
    group_count = query_heads // pair_heads
    scale_factor = float(MODEL_WIDTH // QUERY_HEAD_COUNT) ** (-0.5)
    row_index = lax.axis_index("row")
    query_places = row_index * tokens + jnp.arange(tokens, dtype=jnp.int32)
    query_rot = apply_rotary(
        root_mean_scale(query_proj.reshape(tokens, query_heads, head_size), query_gain),
        query_places.astype(jnp.float32),
    ).astype(jnp.bfloat16)
    rotary_keys = apply_rotary(
        root_mean_scale(projected_keys.reshape(tokens, pair_heads, head_size), key_norm_gain),
        query_places.astype(jnp.float32),
    ).astype(jnp.bfloat16)
    keys_flat = rotary_keys.reshape(tokens, pair_heads * head_size)
    values_flat = projected_values.astype(jnp.bfloat16)
    shards_back = min(WINDOW_LENGTH // tokens, lax.axis_size("row") - 1)
    band_length = (shards_back + 1) * tokens
    key_parts = [keys_flat]
    value_parts = [values_flat]
    for offset in range(1, shards_back + 1):
        keys_prior, values_prior = shifted((keys_flat, values_flat), "row", offset)
        key_parts = [keys_prior] + key_parts
        value_parts = [values_prior] + value_parts
    keys_band = jnp.concatenate(key_parts, axis=0)
    values_band = jnp.concatenate(value_parts, axis=0)
    key_places = (row_index - shards_back) * tokens + jnp.arange(band_length, dtype=jnp.int32)
    distance = query_places[:, None] - key_places[None, :]
    visible = (distance >= 0) & (distance < WINDOW_LENGTH) & (key_places[None, :] >= 0)
    grouped = query_rot.reshape(tokens, pair_heads, group_count, head_size)
    scores = (
        jnp.einsum(
            "qhgd,shd->hgqs",
            grouped,
            keys_band.reshape(band_length, pair_heads, head_size),
            preferred_element_type=jnp.float32,
        )
        * scale_factor
    )
    scores = jnp.where(visible, scores, -1e30)
    row_max = jnp.max(scores, axis=-1, keepdims=True)
    exponent = jnp.exp(scores - row_max)
    weights = (exponent / jnp.sum(exponent, axis=-1, keepdims=True)).astype(jnp.bfloat16)
    attended = jnp.einsum(
        "hgqs,shd->qhgd",
        weights,
        values_band.reshape(band_length, pair_heads, head_size),
        preferred_element_type=jnp.float32,
    )
    heads_out = attended.reshape(tokens, query_heads * head_size).astype(jnp.bfloat16)
    head_rows = lax.all_gather(heads_out, ("col", "sub"), axis=1, tiled=True)
    branch = jnp.dot(
        head_rows,
        lax.all_gather(output_weight, "row", axis=0, tiled=True),
        preferred_element_type=jnp.float32,
    )
    squares = lax.psum(jnp.sum(branch * branch, axis=-1), ("col", "sub"))
    scaled = branch * lax.rsqrt(squares[:, None] / MODEL_WIDTH + EPSILON) * post_gain
    return (stream_in.astype(jnp.float32) + scaled).astype(jnp.bfloat16)


def swapped(x, axis, rows=None):
    if rows is None or axis == "sub":
        return lax.ppermute(x, axis, [(0, 1), (1, 0)])
    count = lax.axis_size("row")
    names = ("groups", "row", "sub") if axis == "groups" else ("row", "col", "sub")
    row_stride = 2 if axis == "groups" else 4
    stride = 2 * count if axis == "groups" else 2
    pairs = []
    for device in range(4 * count):
        step = stride if (device // row_stride) % count in rows else 1
        pairs.append((device, device + step if (device // step) % 2 == 0 else device - step))
    return lax.ppermute(x, names, pairs)


def exchanged(x, planes):
    other = dict(zip(planes, planes[::-1]))
    pairs = [
        (2 * r + s, 2 * other[r] + s if r in other else 2 * r + 1 - s)
        for r in range(lax.axis_size("row"))
        for s in range(2)
    ]
    return lax.ppermute(x, ("row", "sub"), pairs)


def after(x, *earlier):
    return lax.optimization_barrier((x, *earlier))[0]


def settle(*values):
    return lax.optimization_barrier(values)


def whole(shape):
    return pl.BlockSpec(shape, lambda *_: (0,) * len(shape))


ANYWHERE = pl.BlockSpec(memory_space=pl.ANY)
LITTLE = pl.CostEstimate(flops=0, bytes_accessed=0, transcendentals=0)


def norm_kernel(table, *refs):
    *pieces, gain, out = refs[-6:]
    depth = pieces[0].shape[1]
    squares = sum(
        jnp.sum(jnp.square(p[0].astype(jnp.float32)), axis=0, keepdims=True) for p in pieces
    )
    scale = lax.rsqrt(squares / MODEL_WIDTH + EPSILON)
    for index, piece in enumerate(pieces):
        rows = pl.ds(pl.multiple_of(table[index] * depth, depth), depth)
        out[0, rows, :] = (piece[0].astype(jnp.float32) * scale * gain[index]).astype(jnp.bfloat16)


def norm_block(table, pieces, which, gain, index, held):
    _, depth, tokens = pieces[0].shape
    lanes = tokens // 2
    shape = (4, 4 * depth, tokens)
    before = () if held is None else (held,)
    return pl.pallas_call(
        norm_kernel,
        grid_spec=pltpu.PrefetchScalarGridSpec(
            num_scalar_prefetch=1,
            grid=(tokens // lanes,),
            in_specs=[ANYWHERE] * len(before)
            + [pl.BlockSpec((1, depth, lanes), lambda t, *_: (which, 0, t))] * 4
            + [whole((4, depth, 1))],
            out_specs=pl.BlockSpec((1, 4 * depth, lanes), lambda t, *_: (index, 0, t)),
        ),
        out_shape=jax.ShapeDtypeStruct(shape, jnp.bfloat16),
        input_output_aliases={1: 0} if before else {},
        compiler_params=pltpu.CompilerParams(vmem_limit_bytes=63 * MIB),
        cost_estimate=pl.CostEstimate(
            flops=40 * depth * tokens, bytes_accessed=16 * depth * tokens, transcendentals=0
        ),
    )(table, *before, *pieces, gain)


def order_pieces(table, pieces, ordered):
    base = 0
    for index, piece in enumerate(pieces):
        depth, width = piece.shape
        rows = pl.ds(pl.multiple_of(table[2 * index], 16), depth)
        columns = pl.ds(pl.multiple_of(table[2 * index + 1], width), width)
        ordered[rows, columns] = piece[...]


def project_early_kernel(count, table, normed, *refs):
    pieces, out, ordered = refs[:count], refs[-2], refs[-1]

    @pl.when(pl.program_id(0) == 0)
    def _():
        order_pieces(table, pieces, ordered)

    out[0] = lax.dot_general(
        ordered[...], normed[0], (((0,), (0,)), ((), ())), preferred_element_type=jnp.float32
    )


def project_early(table, normed, pieces, first, blocks, held):
    _, features, tokens = normed.shape
    width = 2 * pieces[0].shape[1]
    before = () if held is None else (held,)
    return pl.pallas_call(
        functools.partial(project_early_kernel, len(pieces)),
        grid_spec=pltpu.PrefetchScalarGridSpec(
            num_scalar_prefetch=1,
            grid=(blocks,),
            in_specs=[pl.BlockSpec((1, features // 2, tokens), lambda i, t: (first + i, 0, 0))]
            + [whole(p.shape) for p in pieces]
            + [ANYWHERE] * len(before),
            out_specs=pl.BlockSpec((1, width, tokens), lambda i, t: (first + i, 0, 0)),
            scratch_shapes=[pltpu.VMEM((features // 2, width), jnp.bfloat16)],
        ),
        out_shape=jax.ShapeDtypeStruct((4, width, tokens), jnp.float32),
        input_output_aliases={2 + len(pieces): 0} if before else {},
        compiler_params=pltpu.CompilerParams(vmem_limit_bytes=63 * MIB),
        cost_estimate=pl.CostEstimate(
            flops=2 * blocks * tokens * features // 2 * width,
            bytes_accessed=blocks * features * tokens + features * width + 4 * blocks * width * tokens,
            transcendentals=0,
        ),
    )(table, normed, *pieces, *before)


def project_late_kernel(count, table, normed, *refs):
    pieces, refs = refs[:count], refs[count:]
    early, q_gain, k_gain, cosine, sine, q_out, k_out, v_out, total, ordered = refs

    @pl.when(pl.program_id(0) == 0)
    def _():
        order_pieces(table, pieces, ordered)

    total[...] = early[0] + lax.dot_general(
        ordered[...], normed[0], (((0,), (0,)), ((), ())), preferred_element_type=jnp.float32
    )
    head = q_gain.shape[0]
    half = head // 2
    width = q_out.shape[1]
    cos, sin = cosine[...], sine[...]

    def rotated(start, head_gain):
        values = total[start : start + head, :]
        values = (
            values
            * lax.rsqrt(jnp.mean(values * values, axis=0, keepdims=True) + EPSILON)
            * head_gain[:, :1]
        )
        first, second = values[:half], values[half:]
        return jnp.concatenate(
            [first * cos - second * sin, second * cos + first * sin], axis=0
        ).astype(jnp.bfloat16)

    for start in range(0, width, head):
        q_out[0, start : start + head, :] = rotated(start, q_gain)
    for start in range(0, width // 2, head):
        k_out[:, start : start + head] = rotated(width + start, k_gain).T
    v_out[...] = total[width + width // 2 :, :].astype(jnp.bfloat16)


def project_late(table, normed, pieces, early, extras):
    blocks, features, tokens = normed.shape
    width = early.shape[1] // 2
    head = extras[0].shape[0]
    half = head // 2
    count = len(pieces)
    turn = pl.BlockSpec((half, tokens), lambda i, t: (0, t[2 * count + i]))
    return pl.pallas_call(
        functools.partial(project_late_kernel, count),
        grid_spec=pltpu.PrefetchScalarGridSpec(
            num_scalar_prefetch=1,
            grid=(blocks,),
            in_specs=[pl.BlockSpec((1, features // 2, tokens), lambda i, t: (i, 1, 0))]
            + [whole(p.shape) for p in pieces]
            + [
                pl.BlockSpec((1, 2 * width, tokens), lambda i, t: (i, 0, 0)),
                whole((head, head)),
                whole((head, head)),
                turn,
                turn,
            ],
            out_specs=[
                pl.BlockSpec((1, width, tokens), lambda i, t: (i, 0, 0)),
                pl.BlockSpec((tokens, width // 2), lambda i, t: (t[2 * count + i], 0)),
                pl.BlockSpec((width // 2, tokens), lambda i, t: (0, t[2 * count + i])),
            ],
            scratch_shapes=[
                pltpu.VMEM((2 * width, tokens), jnp.float32),
                pltpu.VMEM((features // 2, 2 * width), jnp.bfloat16),
            ],
        ),
        out_shape=[
            jax.ShapeDtypeStruct((blocks, width, tokens), jnp.bfloat16),
            jax.ShapeDtypeStruct((blocks * tokens, width // 2), jnp.bfloat16),
            jax.ShapeDtypeStruct((width // 2, blocks * tokens), jnp.bfloat16),
        ],
        compiler_params=pltpu.CompilerParams(vmem_limit_bytes=48 * MIB),
        cost_estimate=pl.CostEstimate(
            flops=2 * blocks * tokens * features * width,
            bytes_accessed=blocks * features * tokens + 2 * features * width + 8 * blocks * width * tokens,
            transcendentals=0,
        ),
    )(table, normed, *pieces, early, *extras)


def attend_kernel(scale, table, q_ref, keys, values, *refs):
    out, mask = refs[-2:]
    head = 128
    tile = out.shape[1]
    span = WINDOW_LENGTH // tile + 1
    place = table[0] * 2 + pl.program_id(0)
    later = lax.broadcasted_iota(jnp.int32, (tile, tile), 1) >= lax.broadcasted_iota(
        jnp.int32, (tile, tile), 0
    )
    for index, seen in enumerate((later, jnp.logical_not(later))):
        hidden = jnp.where(seen, 0.0, -1e30)
        mask[index, :, :tile] = hidden
        mask[index, :, tile:] = hidden
    pairs = keys.shape[1] // head
    factor = scale * 1.4426950408889634

    def pair_of(index):
        return [slice((2 * index + i) * head, (2 * index + i + 1) * head) for i in range(2)]

    def against(count):
        def within(chunk):
            return pl.ds(pl.multiple_of((place - (count - 1) + chunk) * tile, tile), tile)

        def query(index):
            return jnp.concatenate([q_ref[0, rows, :] for rows in pair_of(index)], axis=1)

        def score(index, chunk, queries):
            columns = slice(index * head, (index + 1) * head)
            result = jnp.dot(
                keys[within(chunk), columns], queries, preferred_element_type=jnp.float32
            )
            if chunk == count - 1:
                result = result + mask[0]
            elif chunk == 0 and count == span:
                result = result + mask[1]
            return result

        queries = query(0)
        scores = [score(0, chunk, queries) for chunk in range(count)]
        for index in range(pairs):
            top = functools.reduce(
                jnp.maximum, [jnp.max(part, axis=0, keepdims=True) for part in scores]
            )
            queries = query(index + 1) if index + 1 < pairs else None
            exponents, upcoming, total = [], [], 0.0
            for chunk, part in enumerate(scores):
                exponent = jnp.exp2((part - top) * factor)
                exponents.append(exponent)
                total = total + jnp.sum(exponent, axis=0, keepdims=True)
                if queries is not None:
                    upcoming.append(score(index + 1, chunk, queries))
            inverse = 1.0 / total
            result = 0.0
            rows = slice(index * head, (index + 1) * head)
            for chunk, exponent in enumerate(exponents):
                result = result + jnp.dot(
                    values[rows, within(chunk)],
                    (exponent * inverse).astype(jnp.bfloat16),
                    preferred_element_type=jnp.float32,
                )
            for i, here in enumerate(pair_of(index)):
                out[here, :] = result[:, i * tile : (i + 1) * tile].astype(jnp.bfloat16)
            scores = upcoming

    chunks = jnp.minimum(place + 1, span)
    for count in range(1, min(span, keys.shape[0] // tile) + 1):

        @pl.when(chunks == count)
        def _(count=count):
            against(count)


def attend(block, index, queries, keys, values, earlier):
    _, width, tokens = queries.shape
    tile = tokens // 2
    return pl.pallas_call(
        functools.partial(attend_kernel, float(MODEL_WIDTH // QUERY_HEAD_COUNT) ** (-0.5)),
        grid_spec=pltpu.PrefetchScalarGridSpec(
            num_scalar_prefetch=1,
            grid=(2,),
            in_specs=[
                pl.BlockSpec((1, width, tile), lambda t, *_: (index, 0, t)),
                whole(keys.shape),
                whole(values.shape),
            ]
            + [ANYWHERE] * len(earlier),
            out_specs=pl.BlockSpec((width, tile), lambda t, *_: (0, t)),
            scratch_shapes=[pltpu.VMEM((2, tile, 2 * tile), jnp.float32)],
        ),
        out_shape=jax.ShapeDtypeStruct((width, tokens), jnp.bfloat16),
        compiler_params=pltpu.CompilerParams(vmem_limit_bytes=28 * MIB),
        cost_estimate=pl.CostEstimate(
            flops=12 * tokens * (WINDOW_LENGTH + tile) * width,
            bytes_accessed=4 * tokens * width + 4 * keys.shape[0] * keys.shape[1],
            transcendentals=0,
        ),
    )(block[None], queries, keys, values, *earlier)


def output_kernel(count, table, *refs):
    parts, pieces, (out, squares, held, row_held) = refs[:8], refs[8 : 8 + count], refs[8 + count :]
    depth = parts[0].shape[0]

    @pl.when(pl.program_id(0) == 0)
    def _():
        for index, part in enumerate(parts):
            held[index * depth : (index + 1) * depth, :] = part[...]
        squares[...] = jnp.zeros_like(squares)

    for index, piece in enumerate(pieces):
        there = pl.ds(pl.multiple_of(table[index], 128), piece.shape[1])
        row_held[:, there] = piece[...]
    product = jnp.dot(row_held[...], held[...], preferred_element_type=jnp.float32)
    out[...] = product
    squares[...] += jnp.sum(jnp.square(product), axis=0, keepdims=True)


def output_product(table, parts, pieces):
    depth, tokens = parts[0].shape
    width = pieces[0][0].shape[0]
    full = 8 * depth
    tile = width // 4

    def rows(column, columns):
        return pl.BlockSpec((tile, columns), lambda t, *_: (t, column))

    return pl.pallas_call(
        functools.partial(output_kernel, len(pieces)),
        grid_spec=pltpu.PrefetchScalarGridSpec(
            num_scalar_prefetch=1,
            grid=(width // tile,),
            in_specs=[whole((depth, tokens))] * 8
            + [rows(column, columns) for _, column, columns in pieces],
            out_specs=[pl.BlockSpec((tile, tokens), lambda t, *_: (t, 0)), whole((1, tokens))],
            scratch_shapes=[
                pltpu.VMEM((full, tokens), jnp.bfloat16),
                pltpu.VMEM((tile, full), jnp.bfloat16),
            ],
        ),
        out_shape=[
            jax.ShapeDtypeStruct((width, tokens), jnp.float32),
            jax.ShapeDtypeStruct((1, tokens), jnp.float32),
        ],
        compiler_params=pltpu.CompilerParams(vmem_limit_bytes=32 * MIB),
        cost_estimate=pl.CostEstimate(
            flops=2 * tokens * full * width,
            bytes_accessed=2 * full * (tokens + width) + 4 * tokens * width,
            transcendentals=0,
        ),
    )(table, *parts, *(piece for piece, _, _ in pieces))


def middle_form(
    stream_in,
    in_gain,
    query_weight,
    key_matrix,
    value_matrix,
    query_gain,
    key_norm_gain,
    output_weight,
    post_gain,
):
    stream = stream_in.T
    features, tokens = stream.shape
    head = query_gain.shape[0]
    row = lax.axis_index("row")
    group = lax.axis_index("groups")
    place = lax.axis_index("col") * 2 + lax.axis_index("sub")
    upper = (row >= 2).astype(jnp.int32)
    in_middle = (row == 1) | (row == 2)
    near_block, cross_block, far_block = 3 * upper, 3 - row, 3 - 3 * upper
    blocks = (row, near_block, cross_block, far_block)
    slot = lambda block: jnp.bitwise_xor(place, block)
    ints = lambda *values: jnp.stack([jnp.asarray(v, jnp.int32) for v in values])
    beside = [(0, 1), (1, 0), (2, 3), (3, 2)]
    beyond = [(0, 2), (1, 0), (2, 3), (3, 1)]
    outside = [(0, 1), (1, 3), (2, 0), (3, 2)]
    middles, ends = (1, 2), (0, 3)

    half = query_weight.shape[1] // 2
    quarter = key_matrix.shape[1] // 2

    def side(which):
        queries = lax.dynamic_slice_in_dim(query_weight, which * half, half, axis=1)
        keys = lax.dynamic_slice_in_dim(key_matrix, which * quarter, quarter, axis=1)
        values = lax.dynamic_slice_in_dim(value_matrix, which * quarter, quarter, axis=1)
        return queries, jnp.concatenate([keys, values], axis=1)

    own_queries, own_pairs = side(upper)
    own_side = jnp.where(group == 0, own_queries, own_pairs)
    other_side = jnp.where(group == 0, *side(1 - upper))
    turned = output_weight.T
    depth = turned.shape[1] // 2
    mine = lax.dynamic_slice_in_dim(turned, group * depth, depth, axis=1)
    theirs = lax.dynamic_slice_in_dim(turned, (1 - group) * depth, depth, axis=1)

    gain_rows = in_gain.reshape(4, features)
    gain = jnp.concatenate(
        [lax.dynamic_slice_in_dim(gain_rows, slot(j), 1, axis=0) for j in range(4)], axis=0
    )[:, :, None]
    arrival = lambda block: jnp.where(
        block == row, 0, jnp.where(block == near_block, 1, jnp.where(block == far_block, 2, 3))
    )
    order = ints(*(arrival(slot(j)) for j in range(4)))

    positions = jnp.arange(4 * tokens, dtype=jnp.int32).astype(jnp.float32)
    cosine, sine = rotary_tables(positions, head)
    spread = lambda gains: jnp.broadcast_to(gains[:, None], (head, head))
    tables = (spread(query_gain), spread(key_norm_gain), cosine.T, sine.T)

    x_cross = exchanged(stream, middles)
    x_near = lax.ppermute(stream, "row", beside)
    own_col = swapped(stream, "col")
    own_sub = swapped(stream, "sub")
    x_cross, x_near, own_col, own_side, other_side, mine = settle(
        x_cross, x_near, own_col, own_side, other_side, mine
    )

    x_far = exchanged(x_near, middles)
    w_near = lax.ppermute(own_side, "row", beside)
    near_col = swapped(x_near, "col")
    own_both = swapped(own_col, "sub")
    near_sub = swapped(x_near, "sub")
    own_pieces = (stream[None], own_sub[None], own_col[None], own_both[None])
    pair_block = jnp.bitwise_xor(row, 1)
    place_table = ints(
        *(
            (2 * slot(block) + jnp.bitwise_xor(which, upper)) * depth
            for block, which in (
                (row, 0),
                (row, 1),
                (pair_block, group),
                (pair_block, 1 - group),
                (3 - pair_block, group),
                (3 - pair_block, 1 - group),
                (3 - row, group),
                (3 - row, 1 - group),
            )
        )
    )
    order, place_table, *tables = settle(order, place_table, *tables)
    normed = norm_block(order, own_pieces, 0, gain, 0, None)
    x_far, w_near, near_col, other_side, normed, x_cross, mine = settle(
        x_far, w_near, near_col, other_side, normed, x_cross, mine
    )
    w_cross = exchanged(other_side, middles)
    cross_col = swapped(x_cross, "col")
    o_in = lax.ppermute(mine, "row", beside)
    w_near_y = swapped(w_near, "groups")
    near_both = swapped(near_col, "sub")
    cross_sub = swapped(x_cross, "sub")
    far_sub = swapped(x_far, "sub")
    near_pieces = (x_near[None], near_sub[None], near_col[None], near_both[None])
    normed = norm_block(order, near_pieces, 0, gain, 1, normed)
    w_cross_y = swapped(after(w_cross, w_near_y), "groups")
    w_cross, w_near_y, cross_col, x_far, normed, other_side, theirs, cross_sub, o_in = settle(
        w_cross, w_near_y, cross_col, x_far, normed, other_side, theirs, cross_sub, o_in
    )

    w_far = lax.ppermute(other_side, "row", beyond)
    far_col = swapped(x_far, "col")
    cross_both = swapped(cross_col, "sub")
    cross_pieces = (x_cross[None], cross_sub[None], cross_col[None], cross_both[None])
    normed = norm_block(order, cross_pieces, 0, gain, 2, normed)
    early_table = ints(0, 0, 0, half, features, group * half, features, (1 - group) * half)
    early_pieces = (own_queries, own_pairs, w_near, w_near_y)
    total = project_early(early_table, normed, early_pieces, 0, 3, None)
    w_far, far_col, w_cross_y, total, theirs, o_in = settle(
        w_far, far_col, w_cross_y, total, theirs, o_in
    )

    w_far_y = swapped(w_far, "groups")
    far_both = swapped(far_col, "sub")
    o_far = exchanged(o_in, middles)
    o_in_rest = lax.ppermute(theirs, "row", beside)
    far_pieces = (x_far[None], far_sub[None], far_col[None], far_both[None])
    normed = norm_block(order, far_pieces, 0, gain, 3, normed)
    total = project_early(early_table, normed, early_pieces, 3, 1, total)
    w_far_y, o_far, total, o_in_rest = settle(w_far_y, o_far, total, o_in_rest)
    o_cross = exchanged(mine, middles)
    o_far_y = swapped(o_far, "groups")
    here, there = group * half, (1 - group) * half
    queries, keys, values = project_late(
        ints(0, here, 0, there, features, here, features, there, *blocks),
        normed,
        (w_far, w_far_y, w_cross, w_cross_y),
        total,
        tables,
    )

    def attended(index, *earlier):
        return attend(blocks[index].astype(jnp.int32), index, queries, keys, values, earlier)

    far_part = attended(3)
    got_far = exchanged(far_part, middles)
    near_part = attended(1, far_part, o_far_y)
    near_col, near_sub = swapped(near_part, "col"), swapped(near_part, "sub")
    o_cross_y = swapped(after(o_cross, far_part), "groups")
    cross_part = attended(2, near_part)
    got_cross = exchanged(cross_part, middles)
    own_part = attended(0, cross_part)
    got_far = after(got_far, cross_part, near_col)
    far_col, far_sub = swapped(got_far, "col"), swapped(got_far, "sub")
    far_both = swapped(after(far_col, got_cross, own_part, o_cross_y), "sub")
    cross_col, cross_sub = swapped(got_cross, "col"), swapped(got_cross, "sub")
    own_col, own_sub = swapped(own_part, "col"), swapped(own_part, "sub")

    pieces = (turned, turned, o_in, o_in_rest, o_far, o_far_y, o_cross, o_cross_y)
    out_pieces = [(piece, int(index == 1), depth) for index, piece in enumerate(pieces)]

    def projected(table, residual, this_side, that_side, *earlier):
        parts = [part for pair in zip(this_side, that_side) for part in pair]
        branch, squares = output_product(table, parts, out_pieces)
        diagonal = lax.ppermute(squares, ("col", "sub"), [(0, 3), (1, 2), (2, 1), (3, 0)])
        total = squares + swapped(squares, "sub") + swapped(squares, "col") + diagonal
        if earlier:
            total = after(total, *earlier)
        scaled = branch * lax.rsqrt(total / MODEL_WIDTH + EPSILON) * post_gain[:, None]
        return (residual.astype(jnp.float32) + scaled).astype(jnp.bfloat16), branch

    near_out, near_branch = projected(
        after(place_table, own_part),
        x_near,
        (near_part, near_sub, near_col, swapped(near_col, "sub")),
        (got_far, far_sub, far_col, far_both),
        cross_col,
    )
    outer = lax.ppermute(near_out, "row", beside)
    own_out, _ = projected(
        after(place_table, near_branch),
        stream,
        (own_part, own_sub, own_col, swapped(own_col, "sub")),
        (got_cross, cross_sub, cross_col, swapped(cross_col, "sub")),
    )
    return jnp.where(in_middle, own_out, outer).T


def on_device(*args):
    stream_in, _, query_weight, key_matrix, value_matrix, query_gain, *_ = args
    sizes = tuple(lax.axis_size(name) for name in ("groups", "row", "col", "sub"))
    tokens, head = stream_in.shape[0], query_gain.shape[0]
    fits = (
        sizes == (2, 4, 2, 2)
        and head == 128
        and tokens % 256 == 0
        and WINDOW_LENGTH % (tokens // 2) == 0
        and key_matrix.shape[1] % (2 * head) == 0
        and query_weight.shape[1] == 2 * key_matrix.shape[1]
        and value_matrix.shape[1] == key_matrix.shape[1]
    )
    return middle_form(*args) if fits else general_form(*args)


def solution(mesh):
    placed = (
        P(("groups", "row"), ("col", "sub")),
        P(),
        P("row", ("col", "sub")),
        P("row", ("col", "sub")),
        P("row", ("col", "sub")),
        P(),
        P(),
        P("row", ("col", "sub")),
        P(("col", "sub")),
    )
    return jax.shard_map(
        on_device,
        mesh=mesh,
        in_specs=placed,
        out_specs=P(("groups", "row"), ("col", "sub")),
        check_vma=False,
    )
```

```python
import functools

import jax
import jax.numpy as jnp
from jax import lax
from jax.experimental import pallas as pl
from jax.experimental.pallas import tpu as pltpu
from jax.sharding import PartitionSpec as P

MODEL_WIDTH = 5376
QUERY_HEAD_COUNT = 32
WINDOW_LENGTH = 1024


EPSILON = 1e-06
MIB = 1024 * 1024


def shifted(x, axis, by):
    count = lax.axis_size(axis)
    pairs = [(i, i + by) for i in range(count) if 0 <= i + by < count]
    return lax.ppermute(x, axis, pairs)


def root_mean_scale(values, gain):
    return values * lax.rsqrt(jnp.mean(values * values, axis=-1, keepdims=True) + EPSILON) * gain


def rotary_tables(token_positions, size):
    half_dim = size // 2
    inverse = 10000.0 ** (-(jnp.arange(half_dim, dtype=jnp.float32) * 2.0) / size)
    angles = token_positions[:, None] * inverse[None, :]
    return jnp.cos(angles), jnp.sin(angles)


def apply_rotary(tensor, token_positions):
    half_dim = tensor.shape[-1] // 2
    cosine, sine_part = rotary_tables(token_positions, tensor.shape[-1])
    cosine, sine_part = cosine[:, None, :], sine_part[:, None, :]
    first_half = tensor[..., :half_dim]
    second_half = tensor[..., half_dim:]
    return jnp.concatenate(
        [
            first_half * cosine - second_half * sine_part,
            second_half * cosine + first_half * sine_part,
        ],
        axis=-1,
    )


def general_form(
    stream_in,
    in_gain,
    query_weight,
    key_matrix,
    value_matrix,
    query_gain,
    key_norm_gain,
    output_weight,
    post_gain,
):
    token_rows = lax.all_gather(stream_in, ("col", "sub"), axis=1, tiled=True)
    tokens = token_rows.shape[0]
    normed = root_mean_scale(token_rows.astype(jnp.float32), in_gain).astype(jnp.bfloat16)

    def add_panel(panel_piece):
        return jnp.dot(normed, panel_piece, preferred_element_type=jnp.float32)

    query_proj = add_panel(lax.all_gather(query_weight, "row", axis=0, tiled=True))
    projected_keys = add_panel(lax.all_gather(key_matrix, "row", axis=0, tiled=True))
    projected_values = add_panel(lax.all_gather(value_matrix, "row", axis=0, tiled=True))
    head_size = query_gain.shape[0]
    query_heads = query_weight.shape[1] // head_size
    pair_heads = key_matrix.shape[1] // head_size
    group_count = query_heads // pair_heads
    scale_factor = float(MODEL_WIDTH // QUERY_HEAD_COUNT) ** (-0.5)
    row_index = lax.axis_index("row")
    query_places = row_index * tokens + jnp.arange(tokens, dtype=jnp.int32)
    query_rot = apply_rotary(
        root_mean_scale(query_proj.reshape(tokens, query_heads, head_size), query_gain),
        query_places.astype(jnp.float32),
    ).astype(jnp.bfloat16)
    rotary_keys = apply_rotary(
        root_mean_scale(projected_keys.reshape(tokens, pair_heads, head_size), key_norm_gain),
        query_places.astype(jnp.float32),
    ).astype(jnp.bfloat16)
    keys_flat = rotary_keys.reshape(tokens, pair_heads * head_size)
    values_flat = projected_values.astype(jnp.bfloat16)
    shards_back = min(WINDOW_LENGTH // tokens, lax.axis_size("row") - 1)
    band_length = (shards_back + 1) * tokens
    key_parts = [keys_flat]
    value_parts = [values_flat]
    for offset in range(1, shards_back + 1):
        keys_prior, values_prior = shifted((keys_flat, values_flat), "row", offset)
        key_parts = [keys_prior] + key_parts
        value_parts = [values_prior] + value_parts
    keys_band = jnp.concatenate(key_parts, axis=0)
    values_band = jnp.concatenate(value_parts, axis=0)
    key_places = (row_index - shards_back) * tokens + jnp.arange(band_length, dtype=jnp.int32)
    distance = query_places[:, None] - key_places[None, :]
    visible = (distance >= 0) & (distance < WINDOW_LENGTH) & (key_places[None, :] >= 0)
    grouped = query_rot.reshape(tokens, pair_heads, group_count, head_size)
    scores = (
        jnp.einsum(
            "qhgd,shd->hgqs",
            grouped,
            keys_band.reshape(band_length, pair_heads, head_size),
            preferred_element_type=jnp.float32,
        )
        * scale_factor
    )
    scores = jnp.where(visible, scores, -1e30)
    row_max = jnp.max(scores, axis=-1, keepdims=True)
    exponent = jnp.exp(scores - row_max)
    weights = (exponent / jnp.sum(exponent, axis=-1, keepdims=True)).astype(jnp.bfloat16)
    attended = jnp.einsum(
        "hgqs,shd->qhgd",
        weights,
        values_band.reshape(band_length, pair_heads, head_size),
        preferred_element_type=jnp.float32,
    )
    heads_out = attended.reshape(tokens, query_heads * head_size).astype(jnp.bfloat16)
    head_rows = lax.all_gather(heads_out, ("col", "sub"), axis=1, tiled=True)
    branch = jnp.dot(
        head_rows,
        lax.all_gather(output_weight, "row", axis=0, tiled=True),
        preferred_element_type=jnp.float32,
    )
    squares = lax.psum(jnp.sum(branch * branch, axis=-1), ("col", "sub"))
    scaled = branch * lax.rsqrt(squares[:, None] / MODEL_WIDTH + EPSILON) * post_gain
    return (stream_in.astype(jnp.float32) + scaled).astype(jnp.bfloat16)


def swapped(x, axis, rows=None):
    if rows is None or axis == "sub":
        return lax.ppermute(x, axis, [(0, 1), (1, 0)])
    count = lax.axis_size("row")
    names = ("groups", "row", "sub") if axis == "groups" else ("row", "col", "sub")
    row_stride = 2 if axis == "groups" else 4
    stride = 2 * count if axis == "groups" else 2
    pairs = []
    for device in range(4 * count):
        step = stride if (device // row_stride) % count in rows else 1
        pairs.append((device, device + step if (device // step) % 2 == 0 else device - step))
    return lax.ppermute(x, names, pairs)


def exchanged(x, planes):
    other = dict(zip(planes, planes[::-1]))
    pairs = [
        (2 * r + s, 2 * other[r] + s if r in other else 2 * r + 1 - s)
        for r in range(lax.axis_size("row"))
        for s in range(2)
    ]
    return lax.ppermute(x, ("row", "sub"), pairs)


def after(x, *earlier):
    return lax.optimization_barrier((x, *earlier))[0]


def settle(*values):
    return lax.optimization_barrier(values)


def whole(shape):
    return pl.BlockSpec(shape, lambda *_: (0,) * len(shape))


ANYWHERE = pl.BlockSpec(memory_space=pl.ANY)
LITTLE = pl.CostEstimate(flops=0, bytes_accessed=0, transcendentals=0)


def norm_kernel(table, *refs):
    *pieces, gain, out = refs[-6:]
    depth = pieces[0].shape[1]
    squares = sum(
        jnp.sum(jnp.square(p[0].astype(jnp.float32)), axis=0, keepdims=True) for p in pieces
    )
    scale = lax.rsqrt(squares / MODEL_WIDTH + EPSILON)
    for index, piece in enumerate(pieces):
        rows = pl.ds(pl.multiple_of(table[index] * depth, depth), depth)
        out[0, rows, :] = (piece[0].astype(jnp.float32) * scale * gain[index]).astype(jnp.bfloat16)


def norm_block(table, pieces, which, gain, index, held):
    _, depth, tokens = pieces[0].shape
    lanes = tokens // 2
    shape = (4, 4 * depth, tokens)
    before = () if held is None else (held,)
    return pl.pallas_call(
        norm_kernel,
        grid_spec=pltpu.PrefetchScalarGridSpec(
            num_scalar_prefetch=1,
            grid=(tokens // lanes,),
            in_specs=[ANYWHERE] * len(before)
            + [pl.BlockSpec((1, depth, lanes), lambda t, *_: (which, 0, t))] * 4
            + [whole((4, depth, 1))],
            out_specs=pl.BlockSpec((1, 4 * depth, lanes), lambda t, *_: (index, 0, t)),
        ),
        out_shape=jax.ShapeDtypeStruct(shape, jnp.bfloat16),
        input_output_aliases={1: 0} if before else {},
        compiler_params=pltpu.CompilerParams(vmem_limit_bytes=63 * MIB),
        cost_estimate=pl.CostEstimate(
            flops=40 * depth * tokens, bytes_accessed=16 * depth * tokens, transcendentals=0
        ),
    )(table, *before, *pieces, gain)


def order_pieces(table, pieces, ordered):
    base = 0
    for index, piece in enumerate(pieces):
        depth, width = piece.shape
        rows = pl.ds(pl.multiple_of(table[2 * index], 16), depth)
        columns = pl.ds(pl.multiple_of(table[2 * index + 1], width), width)
        ordered[rows, columns] = piece[...]


def project_early_kernel(count, table, normed, *refs):
    pieces, out, ordered = refs[:count], refs[-2], refs[-1]

    @pl.when(pl.program_id(0) == 0)
    def _():
        order_pieces(table, pieces, ordered)

    out[0] = lax.dot_general(
        ordered[...], normed[0], (((0,), (0,)), ((), ())), preferred_element_type=jnp.float32
    )


def project_early(table, normed, pieces, first, blocks, held):
    _, features, tokens = normed.shape
    width = 2 * pieces[0].shape[1]
    before = () if held is None else (held,)
    return pl.pallas_call(
        functools.partial(project_early_kernel, len(pieces)),
        grid_spec=pltpu.PrefetchScalarGridSpec(
            num_scalar_prefetch=1,
            grid=(blocks,),
            in_specs=[pl.BlockSpec((1, features // 2, tokens), lambda i, t: (first + i, 0, 0))]
            + [whole(p.shape) for p in pieces]
            + [ANYWHERE] * len(before),
            out_specs=pl.BlockSpec((1, width, tokens), lambda i, t: (first + i, 0, 0)),
            scratch_shapes=[pltpu.VMEM((features // 2, width), jnp.bfloat16)],
        ),
        out_shape=jax.ShapeDtypeStruct((4, width, tokens), jnp.float32),
        input_output_aliases={2 + len(pieces): 0} if before else {},
        compiler_params=pltpu.CompilerParams(vmem_limit_bytes=63 * MIB),
        cost_estimate=pl.CostEstimate(
            flops=2 * blocks * tokens * features // 2 * width,
            bytes_accessed=blocks * features * tokens + features * width + 4 * blocks * width * tokens,
            transcendentals=0,
        ),
    )(table, normed, *pieces, *before)


def project_late_kernel(count, table, normed, *refs):
    pieces, refs = refs[:count], refs[count:]
    early, q_gain, k_gain, cosine, sine, q_out, k_out, v_out, total, ordered = refs

    @pl.when(pl.program_id(0) == 0)
    def _():
        order_pieces(table, pieces, ordered)

    total[...] = early[0] + lax.dot_general(
        ordered[...], normed[0], (((0,), (0,)), ((), ())), preferred_element_type=jnp.float32
    )
    head = q_gain.shape[0]
    half = head // 2
    width = q_out.shape[1]
    cos, sin = cosine[...], sine[...]

    def rotated(start, head_gain):
        values = total[start : start + head, :]
        values = (
            values
            * lax.rsqrt(jnp.mean(values * values, axis=0, keepdims=True) + EPSILON)
            * head_gain[:, :1]
        )
        first, second = values[:half], values[half:]
        return jnp.concatenate(
            [first * cos - second * sin, second * cos + first * sin], axis=0
        ).astype(jnp.bfloat16)

    for start in range(0, width, head):
        q_out[0, start : start + head, :] = rotated(start, q_gain)
    for start in range(0, width // 2, head):
        k_out[:, start : start + head] = rotated(width + start, k_gain).T
    v_out[...] = total[width + width // 2 :, :].astype(jnp.bfloat16)


def project_late(table, normed, pieces, early, extras):
    blocks, features, tokens = normed.shape
    width = early.shape[1] // 2
    head = extras[0].shape[0]
    half = head // 2
    count = len(pieces)
    turn = pl.BlockSpec((half, tokens), lambda i, t: (0, t[2 * count + i]))
    return pl.pallas_call(
        functools.partial(project_late_kernel, count),
        grid_spec=pltpu.PrefetchScalarGridSpec(
            num_scalar_prefetch=1,
            grid=(blocks,),
            in_specs=[pl.BlockSpec((1, features // 2, tokens), lambda i, t: (i, 1, 0))]
            + [whole(p.shape) for p in pieces]
            + [
                pl.BlockSpec((1, 2 * width, tokens), lambda i, t: (i, 0, 0)),
                whole((head, head)),
                whole((head, head)),
                turn,
                turn,
            ],
            out_specs=[
                pl.BlockSpec((1, width, tokens), lambda i, t: (i, 0, 0)),
                pl.BlockSpec((tokens, width // 2), lambda i, t: (t[2 * count + i], 0)),
                pl.BlockSpec((width // 2, tokens), lambda i, t: (0, t[2 * count + i])),
            ],
            scratch_shapes=[
                pltpu.VMEM((2 * width, tokens), jnp.float32),
                pltpu.VMEM((features // 2, 2 * width), jnp.bfloat16),
            ],
        ),
        out_shape=[
            jax.ShapeDtypeStruct((blocks, width, tokens), jnp.bfloat16),
            jax.ShapeDtypeStruct((blocks * tokens, width // 2), jnp.bfloat16),
            jax.ShapeDtypeStruct((width // 2, blocks * tokens), jnp.bfloat16),
        ],
        compiler_params=pltpu.CompilerParams(vmem_limit_bytes=48 * MIB),
        cost_estimate=pl.CostEstimate(
            flops=2 * blocks * tokens * features * width,
            bytes_accessed=blocks * features * tokens + 2 * features * width + 8 * blocks * width * tokens,
            transcendentals=0,
        ),
    )(table, normed, *pieces, early, *extras)


def attend_kernel(scale, table, q_ref, keys, values, *refs):
    out, mask = refs[-2:]
    head = 128
    tile = out.shape[1]
    span = WINDOW_LENGTH // tile + 1
    place = table[0] * 2 + pl.program_id(0)
    later = lax.broadcasted_iota(jnp.int32, (tile, tile), 1) >= lax.broadcasted_iota(
        jnp.int32, (tile, tile), 0
    )
    for index, seen in enumerate((later, jnp.logical_not(later))):
        hidden = jnp.where(seen, 0.0, -1e30)
        mask[index, :, :tile] = hidden
        mask[index, :, tile:] = hidden
    pairs = keys.shape[1] // head
    factor = scale * 1.4426950408889634

    def pair_of(index):
        return [slice((2 * index + i) * head, (2 * index + i + 1) * head) for i in range(2)]

    def against(count):
        def within(chunk):
            return pl.ds(pl.multiple_of((place - (count - 1) + chunk) * tile, tile), tile)

        def query(index):
            return jnp.concatenate([q_ref[0, rows, :] for rows in pair_of(index)], axis=1)

        def score(index, chunk, queries):
            columns = slice(index * head, (index + 1) * head)
            result = jnp.dot(
                keys[within(chunk), columns], queries, preferred_element_type=jnp.float32
            )
            if chunk == count - 1:
                result = result + mask[0]
            elif chunk == 0 and count == span:
                result = result + mask[1]
            return result

        queries = query(0)
        scores = [score(0, chunk, queries) for chunk in range(count)]
        for index in range(pairs):
            top = functools.reduce(
                jnp.maximum, [jnp.max(part, axis=0, keepdims=True) for part in scores]
            )
            queries = query(index + 1) if index + 1 < pairs else None
            exponents, upcoming, total = [], [], 0.0
            for chunk, part in enumerate(scores):
                exponent = jnp.exp2((part - top) * factor)
                exponents.append(exponent)
                total = total + jnp.sum(exponent, axis=0, keepdims=True)
                if queries is not None:
                    upcoming.append(score(index + 1, chunk, queries))
            inverse = 1.0 / total
            result = 0.0
            rows = slice(index * head, (index + 1) * head)
            for chunk, exponent in enumerate(exponents):
                result = result + jnp.dot(
                    values[rows, within(chunk)],
                    (exponent * inverse).astype(jnp.bfloat16),
                    preferred_element_type=jnp.float32,
                )
            for i, here in enumerate(pair_of(index)):
                out[here, :] = result[:, i * tile : (i + 1) * tile].astype(jnp.bfloat16)
            scores = upcoming

    chunks = jnp.minimum(place + 1, span)
    for count in range(1, min(span, keys.shape[0] // tile) + 1):

        @pl.when(chunks == count)
        def _(count=count):
            against(count)


def attend(block, index, queries, keys, values, earlier):
    _, width, tokens = queries.shape
    tile = tokens // 2
    return pl.pallas_call(
        functools.partial(attend_kernel, float(MODEL_WIDTH // QUERY_HEAD_COUNT) ** (-0.5)),
        grid_spec=pltpu.PrefetchScalarGridSpec(
            num_scalar_prefetch=1,
            grid=(2,),
            in_specs=[
                pl.BlockSpec((1, width, tile), lambda t, *_: (index, 0, t)),
                whole(keys.shape),
                whole(values.shape),
            ]
            + [ANYWHERE] * len(earlier),
            out_specs=pl.BlockSpec((width, tile), lambda t, *_: (0, t)),
            scratch_shapes=[pltpu.VMEM((2, tile, 2 * tile), jnp.float32)],
        ),
        out_shape=jax.ShapeDtypeStruct((width, tokens), jnp.bfloat16),
        compiler_params=pltpu.CompilerParams(vmem_limit_bytes=28 * MIB),
        cost_estimate=pl.CostEstimate(
            flops=12 * tokens * (WINDOW_LENGTH + tile) * width,
            bytes_accessed=4 * tokens * width + 4 * keys.shape[0] * keys.shape[1],
            transcendentals=0,
        ),
    )(block[None], queries, keys, values, *earlier)


def output_kernel(count, table, *refs):
    parts, pieces, (out, squares, held, row_held) = refs[:8], refs[8 : 8 + count], refs[8 + count :]
    depth = parts[0].shape[0]

    @pl.when(pl.program_id(0) == 0)
    def _():
        for index, part in enumerate(parts):
            held[index * depth : (index + 1) * depth, :] = part[...]
        squares[...] = jnp.zeros_like(squares)

    for index, piece in enumerate(pieces):
        there = pl.ds(pl.multiple_of(table[index], 128), piece.shape[1])
        row_held[:, there] = piece[...]
    product = jnp.dot(row_held[...], held[...], preferred_element_type=jnp.float32)
    out[...] = product
    squares[...] += jnp.sum(jnp.square(product), axis=0, keepdims=True)


def output_product(table, parts, pieces):
    depth, tokens = parts[0].shape
    width = pieces[0][0].shape[0]
    full = 8 * depth
    tile = width // 4

    def rows(column, columns):
        return pl.BlockSpec((tile, columns), lambda t, *_: (t, column))

    return pl.pallas_call(
        functools.partial(output_kernel, len(pieces)),
        grid_spec=pltpu.PrefetchScalarGridSpec(
            num_scalar_prefetch=1,
            grid=(width // tile,),
            in_specs=[whole((depth, tokens))] * 8
            + [rows(column, columns) for _, column, columns in pieces],
            out_specs=[pl.BlockSpec((tile, tokens), lambda t, *_: (t, 0)), whole((1, tokens))],
            scratch_shapes=[
                pltpu.VMEM((full, tokens), jnp.bfloat16),
                pltpu.VMEM((tile, full), jnp.bfloat16),
            ],
        ),
        out_shape=[
            jax.ShapeDtypeStruct((width, tokens), jnp.float32),
            jax.ShapeDtypeStruct((1, tokens), jnp.float32),
        ],
        compiler_params=pltpu.CompilerParams(vmem_limit_bytes=32 * MIB),
        cost_estimate=pl.CostEstimate(
            flops=2 * tokens * full * width,
            bytes_accessed=2 * full * (tokens + width) + 4 * tokens * width,
            transcendentals=0,
        ),
    )(table, *parts, *(piece for piece, _, _ in pieces))


def middle_form(
    stream_in,
    in_gain,
    query_weight,
    key_matrix,
    value_matrix,
    query_gain,
    key_norm_gain,
    output_weight,
    post_gain,
):
    stream = stream_in.T
    features, tokens = stream.shape
    head = query_gain.shape[0]
    row = lax.axis_index("row")
    group = lax.axis_index("groups")
    place = lax.axis_index("col") * 2 + lax.axis_index("sub")
    upper = (row >= 2).astype(jnp.int32)
    in_middle = (row == 1) | (row == 2)
    near_block, cross_block, far_block = 3 * upper, 3 - row, 3 - 3 * upper
    blocks = (row, near_block, cross_block, far_block)
    slot = lambda block: jnp.bitwise_xor(place, block)
    ints = lambda *values: jnp.stack([jnp.asarray(v, jnp.int32) for v in values])
    beside = [(0, 1), (1, 0), (2, 3), (3, 2)]
    beyond = [(0, 2), (1, 0), (2, 3), (3, 1)]
    outside = [(0, 1), (1, 3), (2, 0), (3, 2)]
    middles, ends = (1, 2), (0, 3)

    half = query_weight.shape[1] // 2
    quarter = key_matrix.shape[1] // 2

    def side(which):
        queries = lax.dynamic_slice_in_dim(query_weight, which * half, half, axis=1)
        keys = lax.dynamic_slice_in_dim(key_matrix, which * quarter, quarter, axis=1)
        values = lax.dynamic_slice_in_dim(value_matrix, which * quarter, quarter, axis=1)
        return queries, jnp.concatenate([keys, values], axis=1)

    own_queries, own_pairs = side(upper)
    own_side = jnp.where(group == 0, own_queries, own_pairs)
    other_side = jnp.where(group == 0, *side(1 - upper))
    turned = output_weight.T
    depth = turned.shape[1] // 2
    mine = lax.dynamic_slice_in_dim(turned, group * depth, depth, axis=1)
    theirs = lax.dynamic_slice_in_dim(turned, (1 - group) * depth, depth, axis=1)

    gain_rows = in_gain.reshape(4, features)
    gain = jnp.concatenate(
        [lax.dynamic_slice_in_dim(gain_rows, slot(j), 1, axis=0) for j in range(4)], axis=0
    )[:, :, None]
    arrival = lambda block: jnp.where(
        block == row, 0, jnp.where(block == near_block, 1, jnp.where(block == far_block, 2, 3))
    )
    order = ints(*(arrival(slot(j)) for j in range(4)))

    positions = jnp.arange(4 * tokens, dtype=jnp.int32).astype(jnp.float32)
    cosine, sine = rotary_tables(positions, head)
    spread = lambda gains: jnp.broadcast_to(gains[:, None], (head, head))
    tables = (spread(query_gain), spread(key_norm_gain), cosine.T, sine.T)

    x_cross = exchanged(stream, middles)
    x_near = lax.ppermute(stream, "row", beside)
    own_col = swapped(stream, "col")
    own_sub = swapped(stream, "sub")
    x_cross, x_near, own_col, own_side, other_side, mine = settle(
        x_cross, x_near, own_col, own_side, other_side, mine
    )

    x_far = exchanged(x_near, middles)
    w_near = lax.ppermute(own_side, "row", beside)
    near_col = swapped(x_near, "col")
    own_both = swapped(own_col, "sub")
    near_sub = swapped(x_near, "sub")
    own_pieces = (stream[None], own_sub[None], own_col[None], own_both[None])
    pair_block = jnp.bitwise_xor(row, 1)
    place_table = ints(
        *(
            (2 * slot(block) + jnp.bitwise_xor(which, upper)) * depth
            for block, which in (
                (row, 0),
                (row, 1),
                (pair_block, group),
                (pair_block, 1 - group),
                (3 - pair_block, group),
                (3 - pair_block, 1 - group),
                (3 - row, group),
                (3 - row, 1 - group),
            )
        )
    )
    order, place_table, *tables = settle(order, place_table, *tables)
    normed = norm_block(order, own_pieces, 0, gain, 0, None)
    x_far, w_near, near_col, other_side, normed, x_cross, mine = settle(
        x_far, w_near, near_col, other_side, normed, x_cross, mine
    )
    w_cross = exchanged(other_side, middles)
    cross_col = swapped(x_cross, "col")
    o_in = lax.ppermute(mine, "row", beside)
    w_near_y = swapped(w_near, "groups")
    near_both = swapped(near_col, "sub")
    cross_sub = swapped(x_cross, "sub")
    far_sub = swapped(x_far, "sub")
    near_pieces = (x_near[None], near_sub[None], near_col[None], near_both[None])
    normed = norm_block(order, near_pieces, 0, gain, 1, normed)
    w_cross_y = swapped(after(w_cross, w_near_y), "groups")
    w_cross, w_near_y, cross_col, x_far, normed, other_side, theirs, cross_sub, o_in = settle(
        w_cross, w_near_y, cross_col, x_far, normed, other_side, theirs, cross_sub, o_in
    )

    w_far = lax.ppermute(other_side, "row", beyond)
    far_col = swapped(x_far, "col")
    cross_both = swapped(cross_col, "sub")
    cross_pieces = (x_cross[None], cross_sub[None], cross_col[None], cross_both[None])
    normed = norm_block(order, cross_pieces, 0, gain, 2, normed)
    early_table = ints(0, 0, 0, half, features, group * half, features, (1 - group) * half)
    early_pieces = (own_queries, own_pairs, w_near, w_near_y)
    total = project_early(early_table, normed, early_pieces, 0, 3, None)
    w_far, far_col, w_cross_y, total, theirs, o_in = settle(
        w_far, far_col, w_cross_y, total, theirs, o_in
    )

    w_far_y = swapped(w_far, "groups")
    far_both = swapped(far_col, "sub")
    o_far = exchanged(o_in, middles)
    o_in_rest = lax.ppermute(theirs, "row", beside)
    far_pieces = (x_far[None], far_sub[None], far_col[None], far_both[None])
    normed = norm_block(order, far_pieces, 0, gain, 3, normed)
    total = project_early(early_table, normed, early_pieces, 3, 1, total)
    w_far_y, o_far, total, o_in_rest = settle(w_far_y, o_far, total, o_in_rest)
    o_cross = exchanged(mine, middles)
    o_far_y = swapped(o_far, "groups")
    here, there = group * half, (1 - group) * half
    queries, keys, values = project_late(
        ints(0, here, 0, there, features, here, features, there, *blocks),
        normed,
        (w_far, w_far_y, w_cross, w_cross_y),
        total,
        tables,
    )

    def attended(index, *earlier):
        return attend(blocks[index].astype(jnp.int32), index, queries, keys, values, earlier)

    far_part = attended(3)
    got_far = exchanged(far_part, middles)
    near_part = attended(1, far_part, o_far_y)
    near_col, near_sub = swapped(near_part, "col"), swapped(near_part, "sub")
    o_cross_y = swapped(after(o_cross, far_part), "groups")
    cross_part = attended(2, near_part)
    got_cross = exchanged(cross_part, middles)
    own_part = attended(0, cross_part)
    got_far = after(got_far, cross_part, near_col)
    far_col, far_sub = swapped(got_far, "col"), swapped(got_far, "sub")
    far_both = swapped(after(far_col, got_cross, own_part, o_cross_y), "sub")
    cross_col, cross_sub = swapped(got_cross, "col"), swapped(got_cross, "sub")
    own_col, own_sub = swapped(after(own_part, far_both), "col"), swapped(own_part, "sub")

    pieces = (turned, turned, o_in, o_in_rest, o_far, o_far_y, o_cross, o_cross_y)
    out_pieces = [(piece, int(index == 1), depth) for index, piece in enumerate(pieces)]

    def projected(table, residual, this_side, that_side, *earlier):
        parts = [part for pair in zip(this_side, that_side) for part in pair]
        branch, squares = output_product(table, parts, out_pieces)
        diagonal = lax.ppermute(squares, ("col", "sub"), [(0, 3), (1, 2), (2, 1), (3, 0)])
        total = squares + swapped(squares, "sub") + swapped(squares, "col") + diagonal
        if earlier:
            total = after(total, *earlier)
        scaled = branch * lax.rsqrt(total / MODEL_WIDTH + EPSILON) * post_gain[:, None]
        return (residual.astype(jnp.float32) + scaled).astype(jnp.bfloat16), branch

    near_out, near_branch = projected(
        after(place_table, own_part),
        x_near,
        (near_part, near_sub, near_col, swapped(near_col, "sub")),
        (got_far, far_sub, far_col, far_both),
        cross_col,
    )
    outer = lax.ppermute(near_out, "row", beside)
    own_out, _ = projected(
        after(place_table, near_branch),
        stream,
        (own_part, own_sub, own_col, swapped(own_col, "sub")),
        (got_cross, cross_sub, cross_col, swapped(cross_col, "sub")),
        near_out,
    )
    return jnp.where(in_middle, lax.optimization_barrier(own_out), outer).T


def on_device(*args):
    stream_in, _, query_weight, key_matrix, value_matrix, query_gain, *_ = args
    sizes = tuple(lax.axis_size(name) for name in ("groups", "row", "col", "sub"))
    tokens, head = stream_in.shape[0], query_gain.shape[0]
    fits = (
        sizes == (2, 4, 2, 2)
        and head == 128
        and tokens % 256 == 0
        and WINDOW_LENGTH % (tokens // 2) == 0
        and key_matrix.shape[1] % (2 * head) == 0
        and query_weight.shape[1] == 2 * key_matrix.shape[1]
        and value_matrix.shape[1] == key_matrix.shape[1]
    )
    return middle_form(*args) if fits else general_form(*args)


def solution(mesh):
    placed = (
        P(("groups", "row"), ("col", "sub")),
        P(),
        P("row", ("col", "sub")),
        P("row", ("col", "sub")),
        P("row", ("col", "sub")),
        P(),
        P(),
        P("row", ("col", "sub")),
        P(("col", "sub")),
    )
    return jax.shard_map(
        on_device,
        mesh=mesh,
        in_specs=placed,
        out_specs=P(("groups", "row"), ("col", "sub")),
        check_vma=False,
    )
```
